32 devices in a mesh: row: 16 (over z, y, x), blk: 2 (over core).
Axes of the slice: x: 2, y: 2, z: 4, core: 2. Of those that a mesh axis runs over, the one named last changes fastest.
Arguments:
- layer_input: bfloat16 [16, 768, 768], P('row', 'blk'), may hold values from -6 to 6
- doc_lengths: int32 [16, 8], P('row'), may hold values from 1 to 384, 768 in all within a row
- buckets: int32 [1535], replicated, may hold values from 0 to 31
- attn_gain: bfloat16 [768], P(('row', 'blk')), may hold values from 0.5 to 1.5
- qkv_weight: bfloat16 [768, 2304], P(('row', 'blk')), may hold values from -0.21875 to 0.21875
- out_weight: bfloat16 [768, 768], P(('row', 'blk')), may hold values from -1.75 to 1.75
- ffn_gain: bfloat16 [768], P(('row', 'blk')), may hold values from 0.5 to 1.5
- up_weight: bfloat16 [768, 3072], P(('row', 'blk')), may hold values from -0.21875 to 0.21875
- down_weight: bfloat16 [3072, 768], P(('row', 'blk')), may hold values from -0.15625 to 0.15625
- rel_bias: float32 [12, 32], replicated, may hold values from -4 to 4
- cotangent: bfloat16 [16, 768, 768], P('row', 'blk'), may hold values from -6 to 6
Outputs:
- output: bfloat16 [16, 768, 768], P('row', 'blk')
- grad_input: float32 [16, 768, 768], P('row', 'blk')
- grad_attn_gain: float32 [768], P(('row', 'blk'))
- grad_qkv: float32 [768, 2304], P(('row', 'blk'))
- grad_out: float32 [768, 768], P(('row', 'blk'))
- grad_ffn_gain: float32 [768], P(('row', 'blk'))
- grad_up: float32 [768, 3072], P(('row', 'blk'))
- grad_down: float32 [3072, 768], P(('row', 'blk'))
- grad_rel_bias: float32 [12, 32], replicated
The draws below stay inside these ranges and needn't reach their ends.
Inputs may be any that keep to these rules, and one draw needn't show every extreme that they name: `doc_lengths`: the 8 lengths of a row sum to 768, and the longest is exactly 384.
All inputs are finite; a program needn't handle non-finite values.
Results may differ from the reference program's by a relative error of at most 0.015.
Values may be sent and summed in bfloat16 or wider, within the bound.
A program may use at most 192 MiB of HBM per device.

```python
import math
import jax
import jax.numpy as jnp
import numpy as np
from jax import lax

D = 768
HEADS = 12
HEAD_DIM = 64
FF = 3072
BUCKETS = 32
DOCS = 8
SEQ = 768
ROWS = 16
MOST = 384


def set_ends(array, stream_key, smallest, top_value):
    longest = array.shape.index(max(array.shape))
    spots = []
    for shift in (0, 1):
        where = [jax.random.randint(jax.random.fold_in(stream_key, axis), (), 0, length) for axis, length in enumerate(array.shape)]
        where[longest] = (where[longest] + shift) % array.shape[longest]
        spots.append(tuple(where))
    return array.at[spots[0]].set(smallest).at[spots[1]].set(top_value)


def levels(rng, shape, shards, least, high):
    def one(position, parts):
        steps = jax.random.uniform(jax.random.fold_in(jax.random.fold_in(rng, 6), position), (parts,), jnp.float32, least / len(shards), high / len(shards))
        return jnp.repeat(jnp.exp(steps), shape[position] // parts).reshape((-1,) + (1,) * (len(shape) - position - 1))

    loudness = one(*shards[0])
    for cut in shards[1:]:
        loudness = loudness * one(*cut)
    return loudness


def length_profile(count, total, limit, skew):
    loads = [(1 << 20) // math.isqrt(grade ** skew) + 1 for grade in range(2, count + 1)]
    spare, counts = total - limit - (count - 1), [1] * (count - 1)
    while spare > 0:
        movable = [i for i in range(count - 1) if counts[i] < limit]
        whole, left = sum([loads[i] for i in movable]), spare
        for i in movable:
            extra = min(limit - counts[i], max(1, left * loads[i] // whole), spare)
            counts[i] = counts[i] + extra
            spare = spare - extra
    return np.array([limit] + counts)


def ragged(key, count, total, reach, lean):
    if count == 2:
        one = jax.random.randint(key, (), max(1, total - reach), min(reach, total - 1) + 1)
        return jnp.stack([one, total - one])
    lengths = jnp.asarray(length_profile(count, total, reach, lean), jnp.int32)
    twos = (count - 1) // 2
    donor, taker = lengths[1:1 + 2 * twos:2], lengths[2:2 + 2 * twos:2]
    slack = jnp.minimum(donor - 1, reach - taker)
    moved = jax.random.randint(jax.random.fold_in(key, 1), (twos,), 0, 1 << 20) % (slack + 1)
    lengths = lengths.at[1:1 + 2 * twos:2].set(donor - moved).at[2:2 + 2 * twos:2].set(taker + moved)
    return lengths[jax.random.permutation(jax.random.fold_in(key, 2), count)]


def noise(stream_key, dims, width, bound, pieces=(), kind=jnp.bfloat16):
    loudness = levels(stream_key, dims, pieces, -0.22, 0.18) if pieces else 1.0
    values = jax.random.normal(stream_key, dims, jnp.float32) * width * loudness
    return jnp.minimum(jnp.maximum(values, -bound), bound).astype(kind)


def setup_inputs(seed: int = 0) -> dict:
    splits = jax.random.split(jax.random.key(seed), 12)
    layer_input = noise(splits[0], (ROWS, SEQ, D), 1.0, 6.0, ((0, 16), (1, 2)))
    doc_lengths = jax.vmap(lambda own: ragged(own, DOCS, SEQ, MOST, 2))(jax.random.split(splits[1], ROWS)).reshape((ROWS, DOCS)).astype(jnp.int32)
    buckets = set_ends(jax.random.randint(splits[2], (2 * SEQ - 1,), 0, BUCKETS), jax.random.fold_in(splits[2], 1), 0, BUCKETS - 1).astype(jnp.int32)
    attn_gain = jnp.clip(1.0 + 0.1 * jax.random.normal(splits[3], (D,), jnp.float32), 0.5, 1.5).astype(jnp.bfloat16)
    qkv_weight = noise(splits[4], (D, 3 * D), D ** -0.5, 0.21875, ((0, 32),))
    out_weight = noise(splits[5], (D, D), (D // 64) ** -0.5, 1.75, ((0, 32),))
    ffn_gain = jnp.clip(1.0 + 0.1 * jax.random.normal(splits[6], (D,), jnp.float32), 0.5, 1.5).astype(jnp.bfloat16)
    up_weight = noise(splits[7], (D, FF), D ** -0.5, 0.21875, ((0, 32),))
    down_weight = noise(splits[8], (FF, D), (FF // 2) ** -0.5, 0.15625, ((0, 32),))
    rel_bias = noise(splits[9], (HEADS, BUCKETS), 1.0, 4.0, (), jnp.float32)
    cotangent = noise(splits[10], (ROWS, SEQ, D), 1.0, 6.0, ((0, 16), (1, 2)))
    return {"layer_input": layer_input, "doc_lengths": doc_lengths, "buckets": buckets, "attn_gain": attn_gain, "qkv_weight": qkv_weight, "out_weight": out_weight, "ffn_gain": ffn_gain, "up_weight": up_weight, "down_weight": down_weight, "rel_bias": rel_bias, "cotangent": cotangent}


EPSILON = 1e-06
SCORE_SCALE = 0.125
NEG_LARGE = -1e+30
PRECISE = lax.Precision.HIGHEST

@jax.custom_vjp
def low(v):
    return lax.optimization_barrier(v.astype(jnp.bfloat16)).astype(jnp.float32)

@jax.custom_vjp
def low_back(v):
    return v

def low_keep(v):
    return (low(v), None)

def low_pass(kept, grad):
    return (grad,)

def back_keep(v):
    return (v, None)

def back_low(kept, grad):
    return (low(grad),)
low.defvjp(low_keep, low_pass)
low_back.defvjp(back_keep, back_low)

def doc_index(positions, doc_ends):
    return lax.optimization_barrier(jnp.sum((positions[:, None] >= doc_ends[None, :]).astype(jnp.int32), axis=1))

def rms_norm(values, scale_gain):
    inverse = lax.rsqrt(lax.optimization_barrier(jnp.mean(values * values, axis=-1, keepdims=True)) + EPSILON)
    return values * inverse * scale_gain

def forward(layer_input, attn_gain, qkv_weight, out_weight, ffn_gain, up_weight, down_weight, rel_bias, doc_ends, buckets):
    normed = low(rms_norm(layer_input, attn_gain))
    projected = low_back(low(jnp.einsum('rsd,de->rse', normed, qkv_weight, precision=PRECISE)))
    query_proj = projected[:, :, :D].reshape(ROWS, SEQ, HEADS, HEAD_DIM)
    key_proj = projected[:, :, D:2 * D].reshape(ROWS, SEQ, HEADS, HEAD_DIM)
    value_proj = projected[:, :, 2 * D:].reshape(ROWS, SEQ, HEADS, HEAD_DIM)
    positions = jnp.arange(SEQ, dtype=jnp.int32)
    doc_ids = jax.vmap(lambda ends_row: doc_index(positions, ends_row))(doc_ends)
    block_rows = 512 if SEQ % 512 == 0 else SEQ
    block_count = SEQ // block_rows

    def one_row(row_items):
        query_row, key_row, value_row, doc_row = row_items

        def one_block(block_items):
            query_block, query_pos, query_doc = block_items
            raw_scores = jnp.einsum('qhd,khd->hqk', query_block, key_row, precision=PRECISE) * SCORE_SCALE
            bucket_ids = jnp.take(buckets, positions[None, :] - query_pos[:, None] + SEQ - 1)
            scores = low_back(raw_scores + jnp.take(rel_bias, bucket_ids, axis=1))
            same_doc = (query_doc[:, None] == doc_row[None, :])[None]
            probabilities = jax.nn.softmax(jnp.where(same_doc, scores, NEG_LARGE), axis=-1)
            return jnp.einsum('hqk,khd->qhd', low(probabilities), value_row, precision=PRECISE)
        block_out = lax.map(jax.checkpoint(one_block), (query_row.reshape(block_count, block_rows, HEADS, HEAD_DIM), positions.reshape(block_count, block_rows), doc_row.reshape(block_count, block_rows)))
        return block_out.reshape(SEQ, D)
    attended = low_back(low(lax.map(one_row, (query_proj, key_proj, value_proj, doc_ids))))
    residual = layer_input + low_back(jnp.einsum('rsd,de->rse', attended, out_weight, precision=PRECISE))
    normed_ffn = low(rms_norm(residual, ffn_gain))
    up_proj = low_back(jnp.einsum('rsd,df->rsf', normed_ffn, up_weight, precision=PRECISE))
    hidden = low(jax.nn.gelu(up_proj, approximate=True))
    return residual + low_back(jnp.einsum('rsf,fd->rsd', hidden, down_weight, precision=PRECISE))

def reference(layer_input, doc_lengths, buckets, attn_gain, qkv_weight, out_weight, ffn_gain, up_weight, down_weight, rel_bias, cotangent):
    doc_ends = jnp.cumsum(doc_lengths, axis=1).astype(jnp.int32)

    def forward_fn(input_value, attn_value, qkv_value, out_value, ffn_value, up_value, down_value, bias_value):
        return forward(input_value, attn_value, qkv_value, out_value, ffn_value, up_value, down_value, bias_value, doc_ends, buckets)
    result, pull_back = jax.vjp(forward_fn, layer_input.astype(jnp.float32), attn_gain.astype(jnp.float32), qkv_weight.astype(jnp.float32), out_weight.astype(jnp.float32), ffn_gain.astype(jnp.float32), up_weight.astype(jnp.float32), down_weight.astype(jnp.float32), rel_bias)
    gradients = pull_back(cotangent.astype(jnp.float32))
    return (result.astype(jnp.bfloat16), gradients[0], gradients[1], gradients[2], gradients[3], gradients[4], gradients[5], gradients[6], gradients[7])
```

```python
import jax
import jax.numpy as jnp
from jax import lax
from jax.experimental import pallas as pl
from jax.experimental.pallas import tpu as pltpu
from jax.sharding import PartitionSpec as P

D = 768
HEADS = 12
HEAD_DIM = 64


EPSILON = 1e-06
SCORE_SCALE = 0.125
NEG_LARGE = -1e30
PRECISE = lax.Precision.HIGHEST


def rms_forward(values, scale_gain):
    inverse = lax.rsqrt(jnp.mean(values * values, axis=-1, keepdims=True) + EPSILON)
    return (values * inverse * scale_gain, inverse)


def rms_backward(values, inverse, scale_gain, incoming):
    scaled = incoming * scale_gain
    gain_grad = jnp.sum(incoming * values * inverse, axis=0)
    value_grad = inverse * scaled - values * inverse**3 * jnp.mean(
        scaled * values, axis=-1, keepdims=True
    )
    return (value_grad, gain_grad)


def smooth_gate(values):
    return jax.nn.gelu(values, approximate=True)


def doc_index(positions, doc_ends):
    return jnp.sum((positions[:, None] >= doc_ends[None, :]).astype(jnp.int32), axis=1)


def block_width(row_count):
    return 512 if row_count % 512 == 0 else row_count


def bucket_hot(buckets, bucket_count, query_first, key_first, query_count, key_count):
    row_length = (buckets.shape[0] + 1) // 2
    span = query_count + key_count - 1
    start_at = key_first - query_first - (query_count - 1) + row_length - 1
    window_ids = lax.dynamic_slice_in_dim(buckets, start_at, span)
    return (window_ids[:, None] == jnp.arange(bucket_count, dtype=jnp.int32)[None, :]).astype(
        jnp.float32
    )


def spread_diagonals(window, query_count, key_count):
    head_count, span = window.shape
    tiled = jnp.broadcast_to(window[:, None, :], (head_count, query_count, span)).reshape(
        head_count, query_count * span
    )
    padded = jnp.pad(tiled, ((0, 0), (0, query_count)))
    grid = padded.reshape(head_count, query_count, span + 1)[:, :, :key_count]
    return grid[:, ::-1, :]


def sum_diagonals(grid):
    head_count, query_count, key_count = grid.shape
    span = query_count + key_count - 1
    flipped = grid[:, ::-1, :]
    padded = jnp.pad(flipped, ((0, 0), (0, 0), (0, span + 1 - key_count)))
    flat = padded.reshape(head_count, query_count * (span + 1))[:, : query_count * span]
    return jnp.sum(flat.reshape(head_count, query_count, span), axis=1)


def block_scores(query_heads, key_heads, query_pos, key_pos, query_doc, key_doc, buckets, rel_bias):
    query_count = query_heads.shape[0]
    key_count = key_heads.shape[0]
    raw_scores = (
        jnp.einsum("qhd,khd->hqk", query_heads, key_heads, preferred_element_type=jnp.float32)
        * SCORE_SCALE
    )
    hot_table = bucket_hot(
        buckets, rel_bias.shape[1], query_pos[0], key_pos[0], query_count, key_count
    )
    window = jnp.dot(rel_bias, hot_table.T, precision=PRECISE)
    scores = raw_scores + spread_diagonals(window, query_count, key_count)
    same_doc = (query_doc[:, None] == key_doc[None, :])[None]
    return (scores, same_doc, hot_table)


def grad_block(
    query_heads,
    dout_heads,
    log_total,
    delta,
    query_pos,
    query_doc,
    key_heads,
    value_heads,
    key_pos,
    key_doc,
    buckets,
    rel_bias,
):
    scores, same_doc, hot_table = block_scores(
        query_heads, key_heads, query_pos, key_pos, query_doc, key_doc, buckets, rel_bias
    )
    probabilities = jnp.where(same_doc, jnp.exp(scores - log_total[..., None]), 0.0)
    prob_grad = jnp.einsum(
        "qhd,khd->hqk", dout_heads, value_heads, preferred_element_type=jnp.float32
    )
    score_grad = (probabilities * (prob_grad - delta[..., None])).astype(jnp.bfloat16)
    query_part = (
        jnp.einsum("hqk,khd->qhd", score_grad, key_heads, preferred_element_type=jnp.float32)
        * SCORE_SCALE
    )
    key_part = (
        jnp.einsum("hqk,qhd->khd", score_grad, query_heads, preferred_element_type=jnp.float32)
        * SCORE_SCALE
    )
    value_part = jnp.einsum(
        "hqk,qhd->khd",
        probabilities.astype(jnp.bfloat16),
        dout_heads,
        preferred_element_type=jnp.float32,
    )
    diagonal_totals = sum_diagonals(score_grad.astype(jnp.float32))
    bias_part = jnp.dot(diagonal_totals, hot_table, precision=PRECISE)
    return (query_part, key_part, value_part, bias_part)


MESH = pl.DeviceIdType.MESH
CHIPS = 16
LINE = 4


def place():
    row = lax.axis_index("row")
    return (lax.rem(row, 2), lax.rem(lax.div(row, 2), 2), lax.div(row, 4), lax.axis_index("blk"))


def chip_of(x, y, z):
    return (z * 2 + y) * 2 + x


def greet(targets):
    barrier = pltpu.get_barrier_semaphore()
    for target in targets:
        pl.semaphore_signal(barrier, inc=1, device_id=target, device_id_type=MESH)
    pl.semaphore_wait(barrier, len(targets))


class Slice:
    def __init__(self):
        self.x, self.y, self.z, self.core = place()
        x, y, z, core = self.x, self.y, self.z, self.core
        self.chip = chip_of(x, y, z)
        self.sibling = (self.chip, 1 - core)
        self.to_x = (chip_of(1 - x, y, z), core)
        self.to_y = (chip_of(x, 1 - y, z), core)

    def line(self, step):
        return lax.rem(self.z + step, LINE)

    def to_z(self, step):
        return (chip_of(self.x, self.y, self.line(step)), self.core)

    def everyone(self):
        return [self.sibling, self.to_x, self.to_y] + [self.to_z(step) for step in (1, 2, 3)]


def remote(src, dst, send, recv, target):
    return pltpu.make_async_remote_copy(
        src_ref=src, dst_ref=dst, send_sem=send, recv_sem=recv, device_id=target, device_id_type=MESH
    )


def await_bytes(like, sem):
    pltpu.make_async_copy(like, like, sem).wait()


class Gather:
    def __init__(self, here, number, full, width, sems):
        self.here, self.number, self.full, self.width = here, number, full, width
        self.z_send, self.z_recv, self.x_send, self.x_recv, self.y_send, self.y_recv, self.c_send, self.c_recv = sems

    def block(self, chip, half=None):
        half = self.here.core if half is None else half
        if self.width is None:
            rows = self.full.shape[0] // CHIPS // 2
            return self.full.at[pl.ds(pl.multiple_of((2 * chip + half) * rows, rows), rows), :]
        rows = self.full.shape[0] // CHIPS
        return self.full.at[
            pl.ds(pl.multiple_of(chip * rows, rows), rows), pl.ds(pl.multiple_of(half * self.width, 128), self.width)
        ]

    def send_line(self):
        mine = self.block(self.here.chip)
        for step in (1, 2, 3):
            remote(mine, mine, self.z_send.at[self.number, step], self.z_recv.at[self.number, step], self.here.to_z(step)).start()

    def column(self, step, x, y):
        return self.block(chip_of(x, y, self.here.line(LINE - step)))

    def share(self, block):
        remote(block, block, self.c_send.at[self.number], self.c_recv.at[self.number], self.here.sibling).start()

    def spread(self, step):
        here, n = self.here, self.number
        block = self.column(step, here.x, here.y)
        if step:
            await_bytes(block, self.z_recv.at[n, step])
        remote(block, block, self.x_send.at[n, step], self.x_recv.at[n, step], here.to_x).start()
        remote(block, block, self.y_send.at[n, step], self.y_recv.at[n, step], here.to_y).start()
        self.share(block)

    def turn(self, step):
        here, n = self.here, self.number
        from_x = self.column(step, 1 - here.x, here.y)
        from_y = self.column(step, here.x, 1 - here.y)
        await_bytes(from_x, self.x_recv.at[n, step])
        if step % 2 == 0:
            remote(from_x, from_x, self.y_send.at[n, 4 + step], self.y_recv.at[n, 4 + step], here.to_y).start()
        self.share(from_x)
        await_bytes(from_y, self.y_recv.at[n, step])
        if step % 2 == 1:
            remote(from_y, from_y, self.x_send.at[n, 4 + step], self.x_recv.at[n, 4 + step], here.to_x).start()
        self.share(from_y)

    def close(self, step):
        here, n = self.here, self.number
        block = self.column(step, 1 - here.x, 1 - here.y)
        await_bytes(block, (self.y_recv if step % 2 == 0 else self.x_recv).at[n, 4 + step])
        self.share(block)

    def arrive(self):
        if self.width is None:
            half = self.full.at[pl.ds(0, self.full.shape[0] // 2), :]
        else:
            half = self.full.at[:, pl.ds(0, self.width)]
        await_bytes(half, self.c_recv.at[self.number])

    def drain(self):
        block = self.block(self.here.chip)
        for step in (1, 2, 3):
            await_bytes(block, self.z_send.at[self.number, step])
        for step in range(4):
            await_bytes(block, self.x_send.at[self.number, step])
            await_bytes(block, self.y_send.at[self.number, step])
            await_bytes(block, (self.y_send if step % 2 == 0 else self.x_send).at[self.number, 4 + step])
        if self.width is None:
            half = self.full.at[pl.ds(0, self.full.shape[0] // 2), :]
        else:
            half = self.full.at[:, pl.ds(0, self.width)]
        await_bytes(half, self.c_send.at[self.number])


def gather_scratch(pieces):
    dma = pltpu.SemaphoreType.DMA
    return [dma((pieces, 4)), dma((pieces, 4))] + [dma((pieces, 8))] * 4 + [dma((pieces,))] * 2


def gather_kernel(qkv_own, out_own, up_own, down_own, qkv, out, up, down, near_qkv, near_out, near_up, swap_send, swap_recv, *sems):
    here = Slice()
    greet(here.everyone())
    split = ((qkv_own, near_qkv, qkv), (out_own, near_out, out), (up_own, near_up, up))
    swaps = []
    for n, (own, near, full) in enumerate(split):
        width = near.shape[1]
        other = own.at[:, pl.ds(pl.multiple_of((1 - here.core) * width, 128), width)]
        swaps.append(remote(other, near, swap_send.at[n], swap_recv.at[n], here.sibling))
        swaps[-1].start()
    gathers = [Gather(here, n, full, near.shape[1], sems) for n, (own, near, full) in enumerate(split)]
    gathers.append(Gather(here, 3, down, None, sems))
    rows = down_own.shape[0]
    down[pl.ds(pl.multiple_of((2 * here.chip + here.core) * rows, rows), rows), :] = down_own[...]
    for n, (own, near, full) in enumerate(split):
        width, rows = near.shape[1], 2 * near.shape[0]
        swaps[n].wait_recv()
        mine = own[:, pl.ds(pl.multiple_of(here.core * width, 128), width)].astype(jnp.float32)
        theirs = near[...].astype(jnp.float32)
        first = jnp.where(here.core == 0, mine, theirs)
        second = jnp.where(here.core == 0, theirs, mine)
        full[pl.ds(pl.multiple_of(here.chip * rows, rows), rows), pl.ds(pl.multiple_of(here.core * width, 128), width)] = (
            jnp.concatenate([first, second], axis=0).astype(jnp.bfloat16)
        )
        gathers[n].send_line()
        gathers[n].spread(0)
    gathers[3].send_line()
    gathers[3].spread(0)
    for g in gathers:
        for step in (1, 2, 3):
            g.spread(step)
        for step in range(4):
            g.turn(step)
        for step in range(4):
            g.close(step)
    for g in gathers:
        g.arrive()
        g.drain()
    for swap in swaps:
        swap.wait_send()


def gather_weights(qkv_own, out_own, up_own, down_own):
    owns = (qkv_own, out_own, up_own, down_own)
    vmem = pl.BlockSpec(memory_space=pltpu.VMEM)
    bf16 = jnp.bfloat16
    total = lax.axis_size("row") * lax.axis_size("blk")
    near = [pltpu.VMEM((w.shape[0], w.shape[1] // 2), bf16) for w in owns[:3]]
    return pl.pallas_call(
        gather_kernel,
        out_shape=[jax.ShapeDtypeStruct((w.shape[0] * total, w.shape[1]), bf16) for w in owns],
        in_specs=[vmem] * 4,
        out_specs=[vmem] * 4,
        scratch_shapes=near + [pltpu.SemaphoreType.DMA((3,))] * 2 + gather_scratch(4),
        compiler_params=pltpu.CompilerParams(collective_id=0, has_side_effects=True, vmem_limit_bytes=56 * 2**20),
    )(*owns)


class Scatter:
    def __init__(self, here, number, part, bufs, sems):
        self.here, self.number, self.part = here, number, part
        self.held, self.near, self.x_turn, self.y_turn, self.x_in, self.y_in, self.z_in = bufs
        self.c_send, self.c_recv, self.x_send, self.x_recv, self.y_send, self.y_recv, self.z_send, self.z_recv = sems
        self.width = self.held.shape[2]

    def half(self, core):
        if len(self.part.shape) == 4:
            return self.part.at[:, core]
        return self.part.at[:, :, pl.ds(pl.multiple_of(core * self.width, 128), self.width)]

    def swap(self):
        n = self.number
        remote(self.half(1 - self.here.core), self.near, self.c_send.at[n], self.c_recv.at[n], self.here.sibling).start()

    def block(self, x, y, z):
        return self.held.at[chip_of(x, y, z)]

    def merge(self):
        here, n = self.here, self.number
        await_bytes(self.near, self.c_recv.at[n])
        mine = self.half(here.core)

        def one(chip, _):
            self.held[chip] = (mine[chip].astype(jnp.float32) + self.near[chip].astype(jnp.float32)).astype(jnp.bfloat16)
            return 0

        lax.fori_loop(0, CHIPS, one, 0)
        for z in range(LINE):
            block = self.block(1 - here.x, 1 - here.y, z)
            if z < 2:
                remote(block, self.x_turn.at[z], self.x_send.at[n, z], self.x_recv.at[n, z], here.to_x).start()
            else:
                remote(block, self.y_turn.at[z - 2], self.y_send.at[n, z], self.y_recv.at[n, z], here.to_y).start()
        for z in range(LINE):
            if z < 2:
                self.to_x(z)
            else:
                self.to_y(z)

    def to_x(self, z):
        here, n = self.here, self.number
        remote(self.block(1 - here.x, here.y, z), self.x_in.at[z], self.x_send.at[n, 4 + z], self.x_recv.at[n, 4 + z], here.to_x).start()

    def to_y(self, z):
        here, n = self.here, self.number
        remote(self.block(here.x, 1 - here.y, z), self.y_in.at[z], self.y_send.at[n, 4 + z], self.y_recv.at[n, 4 + z], here.to_y).start()

    def add(self, chip, *terms):
        total = self.held[chip].astype(jnp.float32)
        for term in terms:
            total = total + term[...].astype(jnp.float32)
        self.held[chip] = total.astype(jnp.bfloat16)

    def turn(self):
        here, n = self.here, self.number
        for z in range(LINE):
            if z < 2:
                await_bytes(self.x_turn.at[z], self.x_recv.at[n, z])
                self.add(chip_of(here.x, 1 - here.y, z), self.x_turn.at[z])
                self.to_y(z)
            else:
                await_bytes(self.y_turn.at[z - 2], self.y_recv.at[n, z])
                self.add(chip_of(1 - here.x, here.y, z), self.y_turn.at[z - 2])
                self.to_x(z)

    def column(self):
        here, n = self.here, self.number
        for step in (1, 2, 3, 0):
            z = here.line(step)
            await_bytes(self.x_in.at[z], self.x_recv.at[n, 4 + z])
            await_bytes(self.y_in.at[z], self.y_recv.at[n, 4 + z])
            self.add(chip_of(here.x, here.y, z), self.x_in.at[z], self.y_in.at[z])
            if step:
                remote(self.block(here.x, here.y, z), self.z_in.at[step - 1], self.z_send.at[n, step], self.z_recv.at[n, step], here.to_z(step)).start()

    def total(self):
        here, n = self.here, self.number
        total = self.held[here.chip].astype(jnp.float32)
        for step in (1, 2, 3):
            await_bytes(self.z_in.at[step - 1], self.z_recv.at[n, step])
            total = total + self.z_in[step - 1].astype(jnp.float32)
        return total

    def drain(self):
        n = self.number
        block = self.held.at[0]
        await_bytes(self.near, self.c_send.at[n])
        for z in range(LINE):
            await_bytes(block, (self.x_send if z < 2 else self.y_send).at[n, z])
            await_bytes(block, self.x_send.at[n, 4 + z])
            await_bytes(block, self.y_send.at[n, 4 + z])
        for step in (1, 2, 3):
            await_bytes(block, self.z_send.at[n, step])


def scatter_kernel(qkv_part, out_part, up_part, down_part, qkv, out, up, down, *scratch):
    parts = (down_part, up_part, out_part, qkv_part)
    bufs = [scratch[7 * n : 7 * n + 7] for n in range(4)]
    sends, gets, final_send, final_recv = scratch[28:31], scratch[31:34], scratch[34], scratch[35]
    sems = scratch[36:]
    here = Slice()
    greet(here.everyone())
    pieces = [Scatter(here, n, part, bufs[n], sems) for n, part in enumerate(parts)]
    for p in pieces:
        p.swap()
    outs = (up, out, qkv)

    def finish(n):
        total = pieces[n].total()
        if n == 0:
            down[...] = total
            return
        rows = total.shape[0] // 2
        sends[n - 1][0] = total[:rows]
        sends[n - 1][1] = total[rows:]
        remote(sends[n - 1].at[1 - here.core], gets[n - 1], final_send.at[n - 1], final_recv.at[n - 1], here.sibling).start()

    for step in range(len(pieces) + 3):
        for n, p in enumerate(pieces):
            stage = step - n
            if stage == 0:
                p.merge()
            if stage == 1:
                p.turn()
            if stage == 2:
                p.column()
            if stage == 3:
                finish(n)
    for n, full in enumerate(outs):
        width = gets[n].shape[1]
        await_bytes(gets[n], final_recv.at[n])
        mine, theirs = sends[n][here.core], gets[n][...]
        full[:, :width] = jnp.where(here.core == 0, mine, theirs)
        full[:, width:] = jnp.where(here.core == 0, theirs, mine)
        await_bytes(gets[n], final_send.at[n])
    for p in pieces:
        p.drain()


def scatter_grads(qkv_part, out_part, up_part, down_part):
    vmem = pl.BlockSpec(memory_space=pltpu.VMEM)
    bf16, f32 = jnp.bfloat16, jnp.float32
    views = [p.reshape(CHIPS, p.shape[0] // CHIPS, p.shape[1]) for p in (qkv_part, out_part, up_part)]
    views.append(down_part.reshape(CHIPS, 2, down_part.shape[0] // CHIPS // 2, down_part.shape[1]))
    blocks = [(views[3].shape[2], views[3].shape[3])]
    blocks += [(views[n].shape[1], views[n].shape[2] // 2) for n in (2, 1, 0)]
    scratch = []
    for rows, width in blocks:
        scratch += [pltpu.VMEM((count, rows, width), bf16) for count in (16, 16, 2, 2, 4, 4, 3)]
    scratch += [pltpu.VMEM((2, rows // 2, width), f32) for rows, width in blocks[1:]]
    scratch += [pltpu.VMEM((rows // 2, width), f32) for rows, width in blocks[1:]]
    dma = pltpu.SemaphoreType.DMA
    scratch += [dma((3,))] * 2 + [dma((4,))] * 2 + [dma((4, 8))] * 4 + [dma((4, 4))] * 2
    devices = 2 * CHIPS
    return pl.pallas_call(
        scatter_kernel,
        out_shape=[jax.ShapeDtypeStruct((p.shape[0] // devices, p.shape[1]), f32) for p in (qkv_part, out_part, up_part, down_part)],
        in_specs=[vmem] * 4,
        out_specs=[vmem] * 4,
        scratch_shapes=scratch,
        compiler_params=pltpu.CompilerParams(collective_id=1, has_side_effects=True, vmem_limit_bytes=60 * 2**20),
    )(*views)

def rms_scale(values):
    inverse = lax.rsqrt(jnp.mean(values * values, axis=-1, keepdims=True) + EPSILON)
    return (values * inverse, inverse)


def rms_pull(values, inverse, scaled):
    return inverse * scaled - values * inverse**3 * jnp.mean(scaled * values, axis=-1, keepdims=True)


def body(
    layer_input,
    doc_lengths,
    buckets,
    attn_gain,
    qkv_weight,
    out_weight,
    ffn_gain,
    up_weight,
    down_weight,
    rel_bias,
    cotangent,
):
    tokens = layer_input.shape[1]
    my_piece = lax.axis_index("blk")
    positions = my_piece * tokens + jnp.arange(tokens, dtype=jnp.int32)
    doc_ends = jnp.cumsum(doc_lengths[0])
    my_docs = doc_index(positions, doc_ends)
    gathered = (
        lax.all_gather(attn_gain, ("row", "blk"), axis=0, tiled=True),
        lax.all_gather(qkv_weight, ("row", "blk"), axis=0, tiled=True),
        lax.all_gather(out_weight, ("row", "blk"), axis=0, tiled=True),
        lax.all_gather(ffn_gain, ("row", "blk"), axis=0, tiled=True),
        lax.all_gather(up_weight, ("row", "blk"), axis=0, tiled=True),
        lax.all_gather(down_weight, ("row", "blk"), axis=0, tiled=True),
    )
    gain_first, qkv_full, out_full, gain_second, up_full, down_full = gathered
    gain_first = gain_first.astype(jnp.float32)
    gain_second = gain_second.astype(jnp.float32)
    inputs = layer_input[0].astype(jnp.float32)
    normed, inv_attn = rms_forward(inputs, gain_first)
    normed_b = normed.astype(jnp.bfloat16)
    projected = jnp.dot(normed_b, qkv_full, preferred_element_type=jnp.float32).astype(jnp.bfloat16)
    query_proj = projected[:, :D]
    key_proj = projected[:, D : 2 * D]
    value_proj = projected[:, 2 * D :]
    query_heads = query_proj.reshape(tokens, HEADS, HEAD_DIM)
    start_state = (
        jnp.zeros((HEADS, tokens, HEAD_DIM), jnp.float32),
        jnp.full((HEADS, tokens), NEG_LARGE, jnp.float32),
        jnp.zeros((HEADS, tokens), jnp.float32),
    )
    key_piece = lax.all_gather(key_proj, "blk", axis=0, tiled=True)
    value_piece = lax.all_gather(value_proj, "blk", axis=0, tiled=True)
    row_count = key_piece.shape[0]
    attend_block_rows = block_width(row_count)
    block_count = row_count // attend_block_rows
    key_blocks = key_piece.reshape(block_count, attend_block_rows, HEADS, HEAD_DIM)
    value_blocks = value_piece.reshape(block_count, attend_block_rows, HEADS, HEAD_DIM)
    offsets = attend_block_rows * jnp.arange(block_count, dtype=jnp.int32)

    def advance(state_in, block_item):
        weighted, running_max, denominator = state_in
        key_block, value_block, offset = block_item
        key_pos = offset + jnp.arange(attend_block_rows, dtype=jnp.int32)
        scores, same_doc, unused_hot = block_scores(
            query_heads,
            key_block,
            positions,
            key_pos,
            my_docs,
            doc_index(key_pos, doc_ends),
            buckets,
            rel_bias,
        )
        scores = jnp.where(same_doc, scores, NEG_LARGE)
        new_max = jnp.maximum(running_max, jnp.max(scores, axis=2))
        rescale = jnp.exp(running_max - new_max)
        probabilities = jnp.where(same_doc, jnp.exp(scores - new_max[..., None]), 0.0)
        denominator = denominator * rescale + jnp.sum(probabilities, axis=2)
        weighted = weighted * rescale[..., None] + jnp.einsum(
            "hqk,khd->hqd",
            probabilities.astype(jnp.bfloat16),
            value_block,
            preferred_element_type=jnp.float32,
        )
        return ((weighted, new_max, denominator), None)

    state_out, unused_out = lax.scan(advance, start_state, (key_blocks, value_blocks, offsets))
    weighted, running_max, denominator = state_out
    attended = jnp.transpose(weighted / denominator[..., None], (1, 0, 2)).reshape(tokens, D)
    log_total = running_max + jnp.log(denominator)
    attended_b = attended.astype(jnp.bfloat16)
    residual = inputs + jnp.dot(attended_b, out_full, preferred_element_type=jnp.float32)
    normed_ffn, inv_ffn = rms_forward(residual, gain_second)
    normed_ffn_b = normed_ffn.astype(jnp.bfloat16)
    up_proj = jnp.dot(normed_ffn_b, up_full, preferred_element_type=jnp.float32)
    activated, activate_back = jax.vjp(smooth_gate, up_proj)
    hidden = activated.astype(jnp.bfloat16)
    result = residual + jnp.dot(hidden, down_full, preferred_element_type=jnp.float32)
    output = result.astype(jnp.bfloat16)[None]
    qkv_full, out_full, up_full, down_full = (
        lax.all_gather(qkv_weight, ("row", "blk"), axis=0, tiled=True),
        lax.all_gather(out_weight, ("row", "blk"), axis=0, tiled=True),
        lax.all_gather(up_weight, ("row", "blk"), axis=0, tiled=True),
        lax.all_gather(down_weight, ("row", "blk"), axis=0, tiled=True),
    )
    out_grad_b = cotangent[0]
    out_grad = out_grad_b.astype(jnp.float32)
    grad_down = jnp.einsum("tf,td->fd", hidden, out_grad_b, preferred_element_type=jnp.float32)
    hidden_grad = jnp.einsum("td,fd->tf", out_grad_b, down_full, preferred_element_type=jnp.float32)
    up_grad = activate_back(hidden_grad)[0].astype(jnp.bfloat16)
    grad_up = jnp.einsum("td,tf->df", normed_ffn_b, up_grad, preferred_element_type=jnp.float32)
    ffn_norm_grad = jnp.einsum("tf,df->td", up_grad, up_full, preferred_element_type=jnp.float32)
    residual_part, grad_ffn_gain = rms_backward(residual, inv_ffn, gain_second, ffn_norm_grad)
    residual_grad = out_grad + residual_part
    residual_grad_b = residual_grad.astype(jnp.bfloat16)
    grad_out = jnp.einsum(
        "td,te->de", attended_b, residual_grad_b, preferred_element_type=jnp.float32
    )
    attended_grad = jnp.einsum(
        "te,de->td", residual_grad_b, out_full, preferred_element_type=jnp.float32
    ).astype(jnp.bfloat16)
    dout_heads = attended_grad.reshape(tokens, HEADS, HEAD_DIM)
    delta = jnp.einsum(
        "thd,thd->ht", dout_heads.astype(jnp.float32), attended.reshape(tokens, HEADS, HEAD_DIM)
    )
    bias_start = jnp.zeros(rel_bias.shape, jnp.float32)
    all_keys, all_values = (
        lax.all_gather(key_proj, "blk", axis=0, tiled=True),
        lax.all_gather(value_proj, "blk", axis=0, tiled=True),
    )
    row_count = all_keys.shape[0]
    block_rows = block_width(row_count)
    block_count = row_count // block_rows
    offsets = block_rows * jnp.arange(block_count, dtype=jnp.int32)

    def key_step(state_in, block_item):
        query_total, bias_total = state_in
        key_block, value_block, offset = block_item
        key_pos = offset + jnp.arange(block_rows, dtype=jnp.int32)
        query_part, key_part, value_part, bias_part = grad_block(
            query_heads,
            dout_heads,
            log_total,
            delta,
            positions,
            my_docs,
            key_block,
            value_block,
            key_pos,
            doc_index(key_pos, doc_ends),
            buckets,
            rel_bias,
        )
        return ((query_total + query_part, bias_total + bias_part), (key_part, value_part))

    key_start = (jnp.zeros((tokens, HEADS, HEAD_DIM), jnp.float32), bias_start)
    (query_total, bias_total), (key_parts, value_parts) = lax.scan(
        key_step,
        key_start,
        (
            all_keys.reshape(block_count, block_rows, HEADS, HEAD_DIM),
            all_values.reshape(block_count, block_rows, HEADS, HEAD_DIM),
            offsets,
        ),
    )
    key_grad, value_grad = (
        lax.psum_scatter(
            key_parts.reshape(row_count, D).astype(jnp.bfloat16),
            "blk",
            scatter_dimension=0,
            tiled=True,
        ).astype(jnp.float32),
        lax.psum_scatter(
            value_parts.reshape(row_count, D).astype(jnp.bfloat16),
            "blk",
            scatter_dimension=0,
            tiled=True,
        ).astype(jnp.float32),
    )
    query_grad = query_total.reshape(tokens, D)
    qkv_grad = jnp.concatenate([query_grad, key_grad, value_grad], axis=1).astype(jnp.bfloat16)
    grad_qkv = jnp.einsum("td,te->de", normed_b, qkv_grad, preferred_element_type=jnp.float32)
    normed_grad = jnp.einsum("te,de->td", qkv_grad, qkv_full, preferred_element_type=jnp.float32)
    input_part, grad_attn_gain = rms_backward(inputs, inv_attn, gain_first, normed_grad)
    grad_input = (residual_grad + input_part)[None]
    shares = (
        lax.psum_scatter(grad_attn_gain, ("row", "blk"), scatter_dimension=0, tiled=True),
        lax.psum_scatter(grad_qkv, ("row", "blk"), scatter_dimension=0, tiled=True),
        lax.psum_scatter(grad_out, ("row", "blk"), scatter_dimension=0, tiled=True),
        lax.psum_scatter(grad_ffn_gain, ("row", "blk"), scatter_dimension=0, tiled=True),
        lax.psum_scatter(grad_up, ("row", "blk"), scatter_dimension=0, tiled=True),
        lax.psum_scatter(grad_down, ("row", "blk"), scatter_dimension=0, tiled=True),
    )
    attn_share, qkv_share, out_share, ffn_share, up_share, down_share = shares
    bias_grad = lax.psum(bias_total, ("row", "blk"))
    return (
        output,
        grad_input,
        attn_share,
        qkv_share,
        out_share,
        ffn_share,
        up_share,
        down_share,
        bias_grad,
    )


def slice_body(
    layer_input,
    doc_lengths,
    buckets,
    attn_gain,
    qkv_weight,
    out_weight,
    ffn_gain,
    up_weight,
    down_weight,
    rel_bias,
    cotangent,
):
    tokens = layer_input.shape[1]
    my_piece = lax.axis_index("blk")
    positions = my_piece * tokens + jnp.arange(tokens, dtype=jnp.int32)
    doc_ends = jnp.cumsum(doc_lengths[0])
    my_docs = doc_index(positions, doc_ends)
    gain_rows_first = attn_gain.astype(jnp.float32)[:, None]
    gain_rows_second = ffn_gain.astype(jnp.float32)[:, None]
    qkv_full, out_full, up_full, down_full = gather_weights(
        (qkv_weight.astype(jnp.float32) * gain_rows_first).astype(jnp.bfloat16),
        out_weight,
        (up_weight.astype(jnp.float32) * gain_rows_second).astype(jnp.bfloat16),
        down_weight,
    )
    inputs = layer_input[0].astype(jnp.float32)
    normed, inv_attn = rms_scale(inputs)
    normed_b = normed.astype(jnp.bfloat16)
    projected = jnp.dot(normed_b, qkv_full, preferred_element_type=jnp.float32).astype(jnp.bfloat16)
    query_proj = projected[:, :D]
    key_proj = projected[:, D : 2 * D]
    value_proj = projected[:, 2 * D :]
    query_heads = query_proj.reshape(tokens, HEADS, HEAD_DIM)
    start_state = (
        jnp.zeros((HEADS, tokens, HEAD_DIM), jnp.float32),
        jnp.full((HEADS, tokens), NEG_LARGE, jnp.float32),
        jnp.zeros((HEADS, tokens), jnp.float32),
    )
    key_piece = lax.all_gather(key_proj, "blk", axis=0, tiled=True)
    value_piece = lax.all_gather(value_proj, "blk", axis=0, tiled=True)
    row_count = key_piece.shape[0]
    attend_block_rows = block_width(row_count)
    block_count = row_count // attend_block_rows
    key_blocks = key_piece.reshape(block_count, attend_block_rows, HEADS, HEAD_DIM)
    value_blocks = value_piece.reshape(block_count, attend_block_rows, HEADS, HEAD_DIM)
    offsets = attend_block_rows * jnp.arange(block_count, dtype=jnp.int32)

    def advance(state_in, block_item):
        weighted, running_max, denominator = state_in
        key_block, value_block, offset = block_item
        key_pos = offset + jnp.arange(attend_block_rows, dtype=jnp.int32)
        scores, same_doc, unused_hot = block_scores(
            query_heads,
            key_block,
            positions,
            key_pos,
            my_docs,
            doc_index(key_pos, doc_ends),
            buckets,
            rel_bias,
        )
        scores = jnp.where(same_doc, scores, NEG_LARGE)
        new_max = jnp.maximum(running_max, jnp.max(scores, axis=2))
        rescale = jnp.exp(running_max - new_max)
        probabilities = jnp.where(same_doc, jnp.exp(scores - new_max[..., None]), 0.0)
        denominator = denominator * rescale + jnp.sum(probabilities, axis=2)
        weighted = weighted * rescale[..., None] + jnp.einsum(
            "hqk,khd->hqd",
            probabilities.astype(jnp.bfloat16),
            value_block,
            preferred_element_type=jnp.float32,
        )
        return ((weighted, new_max, denominator), None)

    state_out, unused_out = lax.scan(advance, start_state, (key_blocks, value_blocks, offsets))
    weighted, running_max, denominator = state_out
    attended = jnp.transpose(weighted / denominator[..., None], (1, 0, 2)).reshape(tokens, D)
    log_total = running_max + jnp.log(denominator)
    attended_b = attended.astype(jnp.bfloat16)
    residual = inputs + jnp.dot(attended_b, out_full, preferred_element_type=jnp.float32)
    normed_ffn, inv_ffn = rms_scale(residual)
    normed_ffn_b = normed_ffn.astype(jnp.bfloat16)
    up_proj = jnp.dot(normed_ffn_b, up_full, preferred_element_type=jnp.float32)
    activated, activate_back = jax.vjp(smooth_gate, up_proj)
    hidden = activated.astype(jnp.bfloat16)
    result = residual + jnp.dot(hidden, down_full, preferred_element_type=jnp.float32)
    output = result.astype(jnp.bfloat16)[None]
    out_grad_b = cotangent[0]
    out_grad = out_grad_b.astype(jnp.float32)
    grad_down = jnp.einsum("tf,td->fd", hidden, out_grad_b, preferred_element_type=jnp.float32)
    hidden_grad = jnp.einsum("td,fd->tf", out_grad_b, down_full, preferred_element_type=jnp.float32)
    up_grad = activate_back(hidden_grad)[0].astype(jnp.bfloat16)
    grad_up = jnp.einsum("td,tf->df", normed_ffn_b, up_grad, preferred_element_type=jnp.float32)
    ffn_norm_grad = jnp.einsum("tf,df->td", up_grad, up_full, preferred_element_type=jnp.float32)
    residual_part = rms_pull(residual, inv_ffn, ffn_norm_grad)
    residual_grad = out_grad + residual_part
    residual_grad_b = residual_grad.astype(jnp.bfloat16)
    grad_out = jnp.einsum(
        "td,te->de", attended_b, residual_grad_b, preferred_element_type=jnp.float32
    )
    attended_grad = jnp.einsum(
        "te,de->td", residual_grad_b, out_full, preferred_element_type=jnp.float32
    ).astype(jnp.bfloat16)
    dout_heads = attended_grad.reshape(tokens, HEADS, HEAD_DIM)
    delta = jnp.einsum(
        "thd,thd->ht", dout_heads.astype(jnp.float32), attended.reshape(tokens, HEADS, HEAD_DIM)
    )
    bias_start = jnp.zeros(rel_bias.shape, jnp.float32)
    all_keys, all_values = (
        lax.all_gather(key_proj, "blk", axis=0, tiled=True),
        lax.all_gather(value_proj, "blk", axis=0, tiled=True),
    )
    row_count = all_keys.shape[0]
    block_rows = block_width(row_count)
    block_count = row_count // block_rows
    offsets = block_rows * jnp.arange(block_count, dtype=jnp.int32)

    def key_step(state_in, block_item):
        query_total, bias_total = state_in
        key_block, value_block, offset = block_item
        key_pos = offset + jnp.arange(block_rows, dtype=jnp.int32)
        query_part, key_part, value_part, bias_part = grad_block(
            query_heads,
            dout_heads,
            log_total,
            delta,
            positions,
            my_docs,
            key_block,
            value_block,
            key_pos,
            doc_index(key_pos, doc_ends),
            buckets,
            rel_bias,
        )
        return ((query_total + query_part, bias_total + bias_part), (key_part, value_part))

    key_start = (jnp.zeros((tokens, HEADS, HEAD_DIM), jnp.float32), bias_start)
    (query_total, bias_total), (key_parts, value_parts) = lax.scan(
        key_step,
        key_start,
        (
            all_keys.reshape(block_count, block_rows, HEADS, HEAD_DIM),
            all_values.reshape(block_count, block_rows, HEADS, HEAD_DIM),
            offsets,
        ),
    )
    key_grad, value_grad = (
        lax.psum_scatter(
            key_parts.reshape(row_count, D).astype(jnp.bfloat16),
            "blk",
            scatter_dimension=0,
            tiled=True,
        ).astype(jnp.float32),
        lax.psum_scatter(
            value_parts.reshape(row_count, D).astype(jnp.bfloat16),
            "blk",
            scatter_dimension=0,
            tiled=True,
        ).astype(jnp.float32),
    )
    query_grad = query_total.reshape(tokens, D)
    qkv_grad = jnp.concatenate([query_grad, key_grad, value_grad], axis=1).astype(jnp.bfloat16)
    grad_qkv = jnp.einsum("td,te->de", normed_b, qkv_grad, preferred_element_type=jnp.float32)
    normed_grad = jnp.einsum("te,de->td", qkv_grad, qkv_full, preferred_element_type=jnp.float32)
    input_part = rms_pull(inputs, inv_attn, normed_grad)
    grad_input = (residual_grad + input_part)[None]
    qkv_share, out_share, up_share, down_share = scatter_grads(
        *(g.astype(jnp.bfloat16) for g in (grad_qkv, grad_out, grad_up, grad_down))
    )
    attn_share = jnp.sum(qkv_share * qkv_weight.astype(jnp.float32), axis=1)
    ffn_share = jnp.sum(up_share * up_weight.astype(jnp.float32), axis=1)
    qkv_share = qkv_share * gain_rows_first
    up_share = up_share * gain_rows_second
    bias_grad = lax.psum(bias_total, ("row", "blk"))
    return (
        output,
        grad_input,
        attn_share,
        qkv_share,
        out_share,
        ffn_share,
        up_share,
        down_share,
        bias_grad,
    )


def solution(mesh):
    fits = dict(mesh.shape) == {"row": CHIPS, "blk": 2}
    return jax.shard_map(
        slice_body if fits else body,
        mesh=mesh,
        in_specs=(
            P("row", "blk", None),
            P("row", None),
            P(),
            P(("row", "blk")),
            P(("row", "blk"), None),
            P(("row", "blk"), None),
            P(("row", "blk")),
            P(("row", "blk"), None),
            P(("row", "blk"), None),
            P(),
            P("row", "blk", None),
        ),
        out_specs=(
            P("row", "blk", None),
            P("row", "blk", None),
            P(("row", "blk")),
            P(("row", "blk"), None),
            P(("row", "blk"), None),
            P(("row", "blk")),
            P(("row", "blk"), None),
            P(("row", "blk"), None),
            P(),
        ),
        check_vma=False,
    )
```

```python
import jax
import jax.numpy as jnp
from jax import lax
from jax.experimental import pallas as pl
from jax.experimental.pallas import tpu as pltpu
from jax.sharding import PartitionSpec as P

D = 768
HEADS = 12
HEAD_DIM = 64


EPSILON = 1e-06
SCORE_SCALE = 0.125
NEG_LARGE = -1e30
PRECISE = lax.Precision.HIGHEST


def rms_forward(values, scale_gain):
    inverse = lax.rsqrt(jnp.mean(values * values, axis=-1, keepdims=True) + EPSILON)
    return (values * inverse * scale_gain, inverse)


def rms_backward(values, inverse, scale_gain, incoming):
    scaled = incoming * scale_gain
    gain_grad = jnp.sum(incoming * values * inverse, axis=0)
    value_grad = inverse * scaled - values * inverse**3 * jnp.mean(
        scaled * values, axis=-1, keepdims=True
    )
    return (value_grad, gain_grad)


def smooth_gate(values):
    return jax.nn.gelu(values, approximate=True)


def doc_index(positions, doc_ends):
    return jnp.sum((positions[:, None] >= doc_ends[None, :]).astype(jnp.int32), axis=1)


def block_width(row_count):
    return 512 if row_count % 512 == 0 else row_count


def bucket_hot(buckets, bucket_count, query_first, key_first, query_count, key_count):
    row_length = (buckets.shape[0] + 1) // 2
    span = query_count + key_count - 1
    start_at = key_first - query_first - (query_count - 1) + row_length - 1
    window_ids = lax.dynamic_slice_in_dim(buckets, start_at, span)
    return (window_ids[:, None] == jnp.arange(bucket_count, dtype=jnp.int32)[None, :]).astype(
        jnp.float32
    )


def spread_diagonals(window, query_count, key_count):
    head_count, span = window.shape
    tiled = jnp.broadcast_to(window[:, None, :], (head_count, query_count, span)).reshape(
        head_count, query_count * span
    )
    padded = jnp.pad(tiled, ((0, 0), (0, query_count)))
    grid = padded.reshape(head_count, query_count, span + 1)[:, :, :key_count]
    return grid[:, ::-1, :]


def sum_diagonals(grid):
    head_count, query_count, key_count = grid.shape
    span = query_count + key_count - 1
    flipped = grid[:, ::-1, :]
    padded = jnp.pad(flipped, ((0, 0), (0, 0), (0, span + 1 - key_count)))
    flat = padded.reshape(head_count, query_count * (span + 1))[:, : query_count * span]
    return jnp.sum(flat.reshape(head_count, query_count, span), axis=1)


def block_scores(query_heads, key_heads, query_pos, key_pos, query_doc, key_doc, buckets, rel_bias):
    query_count = query_heads.shape[0]
    key_count = key_heads.shape[0]
    raw_scores = (
        jnp.einsum("qhd,khd->hqk", query_heads, key_heads, preferred_element_type=jnp.float32)
        * SCORE_SCALE
    )
    hot_table = bucket_hot(
        buckets, rel_bias.shape[1], query_pos[0], key_pos[0], query_count, key_count
    )
    window = jnp.dot(rel_bias, hot_table.T, precision=PRECISE)
    scores = raw_scores + spread_diagonals(window, query_count, key_count)
    same_doc = (query_doc[:, None] == key_doc[None, :])[None]
    return (scores, same_doc, hot_table)


def grad_block(
    query_heads,
    dout_heads,
    log_total,
    delta,
    query_pos,
    query_doc,
    key_heads,
    value_heads,
    key_pos,
    key_doc,
    buckets,
    rel_bias,
):
    scores, same_doc, hot_table = block_scores(
        query_heads, key_heads, query_pos, key_pos, query_doc, key_doc, buckets, rel_bias
    )
    probabilities = jnp.where(same_doc, jnp.exp(scores - log_total[..., None]), 0.0)
    prob_grad = jnp.einsum(
        "qhd,khd->hqk", dout_heads, value_heads, preferred_element_type=jnp.float32
    )
    score_grad = (probabilities * (prob_grad - delta[..., None])).astype(jnp.bfloat16)
    query_part = (
        jnp.einsum("hqk,khd->qhd", score_grad, key_heads, preferred_element_type=jnp.float32)
        * SCORE_SCALE
    )
    key_part = (
        jnp.einsum("hqk,qhd->khd", score_grad, query_heads, preferred_element_type=jnp.float32)
        * SCORE_SCALE
    )
    value_part = jnp.einsum(
        "hqk,qhd->khd",
        probabilities.astype(jnp.bfloat16),
        dout_heads,
        preferred_element_type=jnp.float32,
    )
    diagonal_totals = sum_diagonals(score_grad.astype(jnp.float32))
    bias_part = jnp.dot(diagonal_totals, hot_table, precision=PRECISE)
    return (query_part, key_part, value_part, bias_part)


def body(
    layer_input,
    doc_lengths,
    buckets,
    attn_gain,
    qkv_weight,
    out_weight,
    ffn_gain,
    up_weight,
    down_weight,
    rel_bias,
    cotangent,
):
    tokens = layer_input.shape[1]
    my_piece = lax.axis_index("blk")
    positions = my_piece * tokens + jnp.arange(tokens, dtype=jnp.int32)
    doc_ends = jnp.cumsum(doc_lengths[0])
    my_docs = doc_index(positions, doc_ends)
    gathered = (
        lax.all_gather(attn_gain, ("row", "blk"), axis=0, tiled=True),
        lax.all_gather(qkv_weight, ("row", "blk"), axis=0, tiled=True),
        lax.all_gather(out_weight, ("row", "blk"), axis=0, tiled=True),
        lax.all_gather(ffn_gain, ("row", "blk"), axis=0, tiled=True),
        lax.all_gather(up_weight, ("row", "blk"), axis=0, tiled=True),
        lax.all_gather(down_weight, ("row", "blk"), axis=0, tiled=True),
    )
    gain_first, qkv_full, out_full, gain_second, up_full, down_full = gathered
    gain_first = gain_first.astype(jnp.float32)
    gain_second = gain_second.astype(jnp.float32)
    inputs = layer_input[0].astype(jnp.float32)
    normed, inv_attn = rms_forward(inputs, gain_first)
    normed_b = normed.astype(jnp.bfloat16)
    projected = jnp.dot(normed_b, qkv_full, preferred_element_type=jnp.float32).astype(jnp.bfloat16)
    query_proj = projected[:, :D]
    key_proj = projected[:, D : 2 * D]
    value_proj = projected[:, 2 * D :]
    query_heads = query_proj.reshape(tokens, HEADS, HEAD_DIM)
    start_state = (
        jnp.zeros((HEADS, tokens, HEAD_DIM), jnp.float32),
        jnp.full((HEADS, tokens), NEG_LARGE, jnp.float32),
        jnp.zeros((HEADS, tokens), jnp.float32),
    )
    key_piece = lax.all_gather(key_proj, "blk", axis=0, tiled=True)
    value_piece = lax.all_gather(value_proj, "blk", axis=0, tiled=True)
    row_count = key_piece.shape[0]
    attend_block_rows = block_width(row_count)
    block_count = row_count // attend_block_rows
    key_blocks = key_piece.reshape(block_count, attend_block_rows, HEADS, HEAD_DIM)
    value_blocks = value_piece.reshape(block_count, attend_block_rows, HEADS, HEAD_DIM)
    offsets = attend_block_rows * jnp.arange(block_count, dtype=jnp.int32)

    def advance(state_in, block_item):
        weighted, running_max, denominator = state_in
        key_block, value_block, offset = block_item
        key_pos = offset + jnp.arange(attend_block_rows, dtype=jnp.int32)
        scores, same_doc, unused_hot = block_scores(
            query_heads,
            key_block,
            positions,
            key_pos,
            my_docs,
            doc_index(key_pos, doc_ends),
            buckets,
            rel_bias,
        )
        scores = jnp.where(same_doc, scores, NEG_LARGE)
        new_max = jnp.maximum(running_max, jnp.max(scores, axis=2))
        rescale = jnp.exp(running_max - new_max)
        probabilities = jnp.where(same_doc, jnp.exp(scores - new_max[..., None]), 0.0)
        denominator = denominator * rescale + jnp.sum(probabilities, axis=2)
        weighted = weighted * rescale[..., None] + jnp.einsum(
            "hqk,khd->hqd",
            probabilities.astype(jnp.bfloat16),
            value_block,
            preferred_element_type=jnp.float32,
        )
        return ((weighted, new_max, denominator), None)

    state_out, unused_out = lax.scan(advance, start_state, (key_blocks, value_blocks, offsets))
    weighted, running_max, denominator = state_out
    attended = jnp.transpose(weighted / denominator[..., None], (1, 0, 2)).reshape(tokens, D)
    log_total = running_max + jnp.log(denominator)
    attended_b = attended.astype(jnp.bfloat16)
    residual = inputs + jnp.dot(attended_b, out_full, preferred_element_type=jnp.float32)
    normed_ffn, inv_ffn = rms_forward(residual, gain_second)
    normed_ffn_b = normed_ffn.astype(jnp.bfloat16)
    up_proj = jnp.dot(normed_ffn_b, up_full, preferred_element_type=jnp.float32)
    activated, activate_back = jax.vjp(smooth_gate, up_proj)
    hidden = activated.astype(jnp.bfloat16)
    result = residual + jnp.dot(hidden, down_full, preferred_element_type=jnp.float32)
    output = result.astype(jnp.bfloat16)[None]
    qkv_full, out_full, up_full, down_full = (
        lax.all_gather(qkv_weight, ("row", "blk"), axis=0, tiled=True),
        lax.all_gather(out_weight, ("row", "blk"), axis=0, tiled=True),
        lax.all_gather(up_weight, ("row", "blk"), axis=0, tiled=True),
        lax.all_gather(down_weight, ("row", "blk"), axis=0, tiled=True),
    )
    out_grad_b = cotangent[0]
    out_grad = out_grad_b.astype(jnp.float32)
    grad_down = jnp.einsum("tf,td->fd", hidden, out_grad_b, preferred_element_type=jnp.float32)
    hidden_grad = jnp.einsum("td,fd->tf", out_grad_b, down_full, preferred_element_type=jnp.float32)
    up_grad = activate_back(hidden_grad)[0].astype(jnp.bfloat16)
    grad_up = jnp.einsum("td,tf->df", normed_ffn_b, up_grad, preferred_element_type=jnp.float32)
    ffn_norm_grad = jnp.einsum("tf,df->td", up_grad, up_full, preferred_element_type=jnp.float32)
    residual_part, grad_ffn_gain = rms_backward(residual, inv_ffn, gain_second, ffn_norm_grad)
    residual_grad = out_grad + residual_part
    residual_grad_b = residual_grad.astype(jnp.bfloat16)
    grad_out = jnp.einsum(
        "td,te->de", attended_b, residual_grad_b, preferred_element_type=jnp.float32
    )
    attended_grad = jnp.einsum(
        "te,de->td", residual_grad_b, out_full, preferred_element_type=jnp.float32
    ).astype(jnp.bfloat16)
    dout_heads = attended_grad.reshape(tokens, HEADS, HEAD_DIM)
    delta = jnp.einsum(
        "thd,thd->ht", dout_heads.astype(jnp.float32), attended.reshape(tokens, HEADS, HEAD_DIM)
    )
    bias_start = jnp.zeros(rel_bias.shape, jnp.float32)
    all_keys, all_values = (
        lax.all_gather(key_proj, "blk", axis=0, tiled=True),
        lax.all_gather(value_proj, "blk", axis=0, tiled=True),
    )
    row_count = all_keys.shape[0]
    block_rows = block_width(row_count)
    block_count = row_count // block_rows
    offsets = block_rows * jnp.arange(block_count, dtype=jnp.int32)

    def key_step(state_in, block_item):
        query_total, bias_total = state_in
        key_block, value_block, offset = block_item
        key_pos = offset + jnp.arange(block_rows, dtype=jnp.int32)
        query_part, key_part, value_part, bias_part = grad_block(
            query_heads,
            dout_heads,
            log_total,
            delta,
            positions,
            my_docs,
            key_block,
            value_block,
            key_pos,
            doc_index(key_pos, doc_ends),
            buckets,
            rel_bias,
        )
        return ((query_total + query_part, bias_total + bias_part), (key_part, value_part))

    key_start = (jnp.zeros((tokens, HEADS, HEAD_DIM), jnp.float32), bias_start)
    (query_total, bias_total), (key_parts, value_parts) = lax.scan(
        key_step,
        key_start,
        (
            all_keys.reshape(block_count, block_rows, HEADS, HEAD_DIM),
            all_values.reshape(block_count, block_rows, HEADS, HEAD_DIM),
            offsets,
        ),
    )
    key_grad, value_grad = (
        lax.psum_scatter(
            key_parts.reshape(row_count, D).astype(jnp.bfloat16),
            "blk",
            scatter_dimension=0,
            tiled=True,
        ).astype(jnp.float32),
        lax.psum_scatter(
            value_parts.reshape(row_count, D).astype(jnp.bfloat16),
            "blk",
            scatter_dimension=0,
            tiled=True,
        ).astype(jnp.float32),
    )
    query_grad = query_total.reshape(tokens, D)
    qkv_grad = jnp.concatenate([query_grad, key_grad, value_grad], axis=1).astype(jnp.bfloat16)
    grad_qkv = jnp.einsum("td,te->de", normed_b, qkv_grad, preferred_element_type=jnp.float32)
    normed_grad = jnp.einsum("te,de->td", qkv_grad, qkv_full, preferred_element_type=jnp.float32)
    input_part, grad_attn_gain = rms_backward(inputs, inv_attn, gain_first, normed_grad)
    grad_input = (residual_grad + input_part)[None]
    shares = (
        lax.psum_scatter(grad_attn_gain, ("row", "blk"), scatter_dimension=0, tiled=True),
        lax.psum_scatter(grad_qkv, ("row", "blk"), scatter_dimension=0, tiled=True),
        lax.psum_scatter(grad_out, ("row", "blk"), scatter_dimension=0, tiled=True),
        lax.psum_scatter(grad_ffn_gain, ("row", "blk"), scatter_dimension=0, tiled=True),
        lax.psum_scatter(grad_up, ("row", "blk"), scatter_dimension=0, tiled=True),
        lax.psum_scatter(grad_down, ("row", "blk"), scatter_dimension=0, tiled=True),
    )
    attn_share, qkv_share, out_share, ffn_share, up_share, down_share = shares
    bias_grad = lax.psum(bias_total, ("row", "blk"))
    return (
        output,
        grad_input,
        attn_share,
        qkv_share,
        out_share,
        ffn_share,
        up_share,
        down_share,
        bias_grad,
    )


MESH = pl.DeviceIdType.MESH
CHIPS = 16
LINE = 4
HALF = 64
PAIR = 128
TILE = 128
PAIRS = HEADS // 2
GELU_SLOPE = 0.7978845608028654
GELU_CUBE = 0.044715


def rms_scale(values):
    inverse = lax.rsqrt(jnp.mean(values * values, axis=-1, keepdims=True) + EPSILON)
    return (values * inverse, inverse)


def rms_pull(values, scaled):
    inverse = lax.rsqrt(jnp.mean(values * values, axis=-1, keepdims=True) + EPSILON)
    return inverse * scaled - values * inverse**3 * jnp.mean(scaled * values, axis=-1, keepdims=True)


def place():
    row = lax.axis_index("row")
    return (lax.rem(row, 2), lax.rem(lax.div(row, 2), 2), lax.div(row, 4), lax.axis_index("blk"))


def chip_of(x, y, z):
    return (z * 2 + y) * 2 + x


class Slice:
    def __init__(self):
        self.x, self.y, self.z, self.core = place()
        x, y, z, core = self.x, self.y, self.z, self.core
        self.chip = chip_of(x, y, z)
        self.sibling = (self.chip, 1 - core)
        self.to_x = (chip_of(1 - x, y, z), core)
        self.to_y = (chip_of(x, 1 - y, z), core)

    def line(self, step):
        return lax.rem(self.z + step, LINE)

    def to_z(self, step):
        return (chip_of(self.x, self.y, self.line(step)), self.core)

    def greet(self):
        barrier = pltpu.get_barrier_semaphore()
        everyone = [self.sibling, self.to_x, self.to_y] + [self.to_z(step) for step in (1, 2, 3)]
        for target in everyone:
            pl.semaphore_signal(barrier, inc=1, device_id=target, device_id_type=MESH)
        pl.semaphore_wait(barrier, len(everyone))


def remote(src, dst, send, recv, target):
    return pltpu.make_async_remote_copy(
        src_ref=src, dst_ref=dst, send_sem=send, recv_sem=recv, device_id=target, device_id_type=MESH
    )


def await_bytes(like, sem):
    pltpu.make_async_copy(like, like, sem).wait()


class Gather:
    def __init__(self, here, number, full, rows, pitch, width, start, core_step, sems):
        self.here, self.number, self.full = here, number, full
        self.rows, self.pitch, self.width, self.start, self.core_step = rows, pitch, width, start, core_step
        self.z_send, self.z_recv, self.x_send, self.x_recv, self.y_send, self.y_recv, self.c_send, self.c_recv = sems

    def block(self, chip):
        row = pl.multiple_of(chip * self.pitch + self.here.core * self.core_step[0] + self.start[0], 16)
        column = pl.multiple_of(self.here.core * self.core_step[1] + self.start[1], 128)
        return self.full.at[pl.ds(row, self.rows), pl.ds(column, self.width)]

    def line(self):
        mine, n = self.block(self.here.chip), self.number
        for step in (1, 2, 3):
            remote(mine, mine, self.z_send.at[n, step], self.z_recv.at[n, step], self.here.to_z(step)).start()

    def column(self, step, x, y):
        return self.block(chip_of(x, y, self.here.line(LINE - step)))

    def share(self, block):
        remote(block, block, self.c_send.at[self.number], self.c_recv.at[self.number], self.here.sibling).start()

    def spread(self, step):
        here, n = self.here, self.number
        block = self.column(step, here.x, here.y)
        if step:
            await_bytes(block, self.z_recv.at[n, step])
        remote(block, block, self.x_send.at[n, step], self.x_recv.at[n, step], here.to_x).start()
        remote(block, block, self.y_send.at[n, step], self.y_recv.at[n, step], here.to_y).start()
        self.share(block)

    def turn(self, step):
        here, n = self.here, self.number
        from_x = self.column(step, 1 - here.x, here.y)
        from_y = self.column(step, here.x, 1 - here.y)
        await_bytes(from_x, self.x_recv.at[n, step])
        if step % 2 == 0:
            remote(from_x, from_x, self.y_send.at[n, 4 + step], self.y_recv.at[n, 4 + step], here.to_y).start()
        self.share(from_x)
        await_bytes(from_y, self.y_recv.at[n, step])
        if step % 2 == 1:
            remote(from_y, from_y, self.x_send.at[n, 4 + step], self.x_recv.at[n, 4 + step], here.to_x).start()
        self.share(from_y)

    def close(self, step):
        here, n = self.here, self.number
        block = self.column(step, 1 - here.x, 1 - here.y)
        await_bytes(block, (self.y_recv if step % 2 == 0 else self.x_recv).at[n, 4 + step])
        self.share(block)

    def whole(self):
        return self.full.at[pl.ds(0, CHIPS * self.rows), pl.ds(0, self.width)]

    def arrive(self):
        await_bytes(self.whole(), self.c_recv.at[self.number])

    def drain(self):
        block, n = self.block(self.here.chip), self.number
        for step in (1, 2, 3):
            await_bytes(block, self.z_send.at[n, step])
        for step in range(4):
            await_bytes(block, self.x_send.at[n, step])
            await_bytes(block, self.y_send.at[n, step])
            await_bytes(block, (self.y_send if step % 2 == 0 else self.x_send).at[n, 4 + step])
        await_bytes(self.whole(), self.c_send.at[n])


def low_lanes(shape):
    return lax.broadcasted_iota(jnp.int32, shape, 1) < HALF


def one_head(block, second):
    low = low_lanes(block.shape)
    return jnp.where(low != bool(second), block, jnp.zeros_like(block))


def dot_nt(a, b):
    return lax.dot_general(a, b, (((1,), (1,)), ((), ())), preferred_element_type=jnp.float32)


def dot_tn(a, b):
    return lax.dot_general(a, b, (((0,), (0,)), ((), ())), preferred_element_type=jnp.float32)


def dot_nn(a, b):
    return jnp.dot(a, b, preferred_element_type=jnp.float32)


def bias_table(window_row, span):
    rows = jnp.broadcast_to(window_row, (TILE, span))
    return pltpu.roll(rows, span - (TILE - 1), 1, stride=1, stride_axis=0)


def diagonal_sums(table, span):
    wide = jnp.concatenate([table, jnp.zeros((TILE, span - table.shape[1]), jnp.float32)], axis=1)
    total = jnp.zeros((8, span), jnp.float32)
    for group in range(TILE // 8):
        total = total + pltpu.roll(wide[8 * group : 8 * group + 8, :], TILE - 1 - 8 * group, 1)
    sums = total[0:1, :]
    for row in range(1, 8):
        sums = sums + pltpu.roll(total[row : row + 1, :], span - row, 1)
    return sums


def attend_pair(pair, q, keys, values, window, q_doc, k_doc, table, attended, log_total):
    tokens, span = q.shape[0], window.shape[1]
    lanes = slice(pair * PAIR, (pair + 1) * PAIR)
    for second in (0, 1):
        table[second] = bias_table(window[2 * pair + second : 2 * pair + second + 1, :], span)[:, : table.shape[2]]

    def block(k, _):
        rows = pl.ds(pl.multiple_of(k * TILE, TILE), TILE)
        shift = pl.multiple_of(tokens - TILE - k * TILE, TILE)
        same = q_doc[rows, :] == k_doc[...]
        query = q[rows, lanes]
        parts = []
        logs = log_total[rows, :]
        lane = lax.broadcasted_iota(jnp.int32, logs.shape, 1)
        for second in (0, 1):
            scores = dot_nt(one_head(query, second), keys[:, lanes]) + table[second, :, pl.ds(shift, keys.shape[0])]
            scores = jnp.where(same, scores, NEG_LARGE)
            top = jnp.max(scores, axis=1, keepdims=True)
            weights = jnp.exp(scores - top)
            total = jnp.sum(weights, axis=1, keepdims=True)
            parts.append(dot_nn(weights.astype(jnp.bfloat16), values[:, lanes]) * (1.0 / total))
            logs = jnp.where(lane == 2 * pair + second, top + jnp.log(total), logs)
        log_total[rows, :] = logs
        attended[rows, lanes] = jnp.where(low_lanes(parts[0].shape), parts[0], parts[1])
        return 0

    lax.fori_loop(0, tokens // TILE, block, 0)


def pull_pair(pair, q, keys, values, window, q_doc, k_doc, attended, attended_grad, log_total, table, sums, probs, grads, diagonals, q_grad, k_grad, v_grad):
    tokens, span, count = q.shape[0], window.shape[1], keys.shape[0]
    lanes = slice(pair * PAIR, (pair + 1) * PAIR)
    for second in (0, 1):
        table[second] = bias_table(window[2 * pair + second : 2 * pair + second + 1, :], span)[:, : table.shape[2]]
    sums[...] = jnp.zeros_like(sums)

    def block(k, _):
        rows = pl.ds(pl.multiple_of(k * TILE, TILE), TILE)
        shift = pl.multiple_of(tokens - TILE - k * TILE, TILE)
        same = q_doc[rows, :] == k_doc[...]
        query, out_grad = q[rows, lanes], attended_grad[rows, lanes]
        product = out_grad.astype(jnp.float32) * attended[rows, lanes]
        logs = log_total[rows, :]
        lane = lax.broadcasted_iota(jnp.int32, logs.shape, 1)
        for second in (0, 1):
            log = jnp.sum(jnp.where(lane == 2 * pair + second, logs, 0.0), axis=1, keepdims=True)
            delta = jnp.sum(one_head(product, second), axis=1, keepdims=True)
            scores = dot_nt(one_head(query, second), keys[:, lanes]) + table[second, :, pl.ds(shift, count)]
            weights = jnp.exp(jnp.where(same, scores - log, NEG_LARGE))
            pulled = dot_nt(one_head(out_grad, second), values[:, lanes])
            score_grad = weights * (pulled - delta)
            sums[second, :, pl.ds(shift, count)] += score_grad
            here = pl.ds(pl.multiple_of(second * tokens + k * TILE, TILE), TILE)
            probs[here, :] = weights.astype(jnp.bfloat16)
            grads[here, :] = score_grad.astype(jnp.bfloat16)
        return 0

    lax.fori_loop(0, tokens // TILE, block, 0)
    for second in (0, 1):
        diagonals[2 * pair + second : 2 * pair + second + 1, :] = diagonal_sums(sums[second], span)
    both = lambda rows: jnp.concatenate([one_head(rows, 0), one_head(rows, 1)], axis=0)
    k_grad[:, lanes] = dot_tn(grads[...], both(q[:, lanes])).astype(jnp.bfloat16)
    v_grad[:, lanes] = dot_tn(probs[...], both(attended_grad[:, lanes])).astype(jnp.bfloat16)
    key = keys[:, lanes]
    pulled = dot_nn(grads[:tokens, :], one_head(key, 0)) + dot_nn(grads[tokens:, :], one_head(key, 1))
    q_grad[:, lanes] = (SCORE_SCALE * pulled).astype(jnp.bfloat16)


def documents(lengths, core, tokens, q_doc, k_doc):
    count = k_doc.shape[1]
    queries = core * tokens + lax.broadcasted_iota(jnp.int32, (tokens, 1), 0)
    keys = lax.broadcasted_iota(jnp.int32, (1, count), 1)
    end = jnp.int32(0)
    q_index, k_index = jnp.zeros((tokens, 1), jnp.int32), jnp.zeros((1, count), jnp.int32)
    for n in range(lengths.shape[1]):
        end = end + lengths[0, n]
        q_index = q_index + (queries >= end).astype(jnp.int32)
        k_index = k_index + (keys >= end).astype(jnp.int32)
    q_doc[...] = q_index
    k_doc[...] = k_index


def window_hot(buckets, core, tokens, span, count):
    ids = buckets[:, pl.ds(pl.multiple_of((1 - core) * tokens, 128), span)]
    return (jnp.broadcast_to(ids, (count, span)) == lax.broadcasted_iota(jnp.int32, (count, span), 0)).astype(jnp.float32)


def forward_kernel(
    layer_input, cotangent, lengths, buckets, rel_bias, attn_gain, ffn_gain, qkv_own, out_own, up_own, down_own,
    output_h, qkv_h, out_h, up_h, q_h, keys_h, values_h, attended_h, logs_h, residual_h, normed_h, up_grad_h, down_part_h,
    window,
    qkv, out, up, down, q, keys, values, attended, logs, residual, normed, up_grad, down_part, output,
    fold_qkv, fold_up, near_qkv, near_out, near_up, first, hidden, slope, table, q_doc, k_doc,
    swap_send, swap_recv, kv_send, kv_recv, stash, *sems,
):
    here = Slice()
    core = here.core
    tokens = layer_input.shape[0]
    bf16, f32 = jnp.bfloat16, jnp.float32
    here.greet()
    fold_qkv[...] = (qkv_own[...].astype(f32) * attn_gain[...]).astype(bf16)
    fold_up[...] = (up_own[...].astype(f32) * ffn_gain[...]).astype(bf16)
    split = ((fold_qkv, near_qkv, qkv), (out_own, near_out, out), (fold_up, near_up, up))
    swaps = []
    for n, (own, near, full) in enumerate(split):
        width = near.shape[1]
        other = own.at[:, pl.ds(pl.multiple_of((1 - core) * width, 128), width)]
        swaps.append(remote(other, near, swap_send.at[n], swap_recv.at[n], here.sibling))
        swaps[-1].start()
    rows = down_own.shape[0]
    down[pl.ds(pl.multiple_of((2 * here.chip + core) * rows, rows), rows), :] = down_own[...]
    shard = 2 * qkv_own.shape[0]
    width = near_up.shape[1] // 2
    pieces = [
        Gather(here, 0, qkv, shard, shard, near_qkv.shape[1], (0, 0), (0, near_qkv.shape[1]), sems),
        Gather(here, 1, out, shard, shard, near_out.shape[1], (0, 0), (0, near_out.shape[1]), sems),
        Gather(here, 2, up, shard, shard, width, (0, 0), (0, 2 * width), sems),
        Gather(here, 3, up, shard, shard, width, (0, width), (0, 2 * width), sems),
        Gather(here, 4, down, rows // 2, 2 * rows, down.shape[1], (0, 0), (rows, 0), sems),
        Gather(here, 5, down, rows // 2, 2 * rows, down.shape[1], (rows // 2, 0), (rows, 0), sems),
    ]

    def assemble(n):
        own, near, full = split[n]
        width = near.shape[1]
        swaps[n].wait_recv()
        mine = own[:, pl.ds(pl.multiple_of(core * width, 128), width)].astype(f32)
        theirs = near[...].astype(f32)
        both = [jnp.where(core == 0, mine, theirs), jnp.where(core == 0, theirs, mine)]
        full[pl.ds(pl.multiple_of(here.chip * shard, shard), shard), pl.ds(pl.multiple_of(core * width, 128), width)] = (
            jnp.concatenate(both, axis=0).astype(bf16)
        )

    assemble(0)
    pieces[0].line()
    pieces[0].spread(0)
    assemble(1)
    pieces[1].line()
    pieces[1].spread(0)
    assemble(2)
    for n in (2, 3, 4, 5):
        pieces[n].spread(0)

    stashed = []

    def keep(src, dst):
        stashed.append(pltpu.make_async_copy(src, dst, stash.at[len(stashed)]))
        stashed[-1].start()

    def spread(n):
        for step in (1, 2, 3):
            pieces[n].spread(step)
        if n + 2 < len(pieces):
            pieces[n + 2].line()

    def turn(n):
        for step in range(4):
            pieces[n].turn(step)

    def close(n):
        for step in range(4):
            pieces[n].close(step)

    documents(lengths, core, tokens, q_doc, k_doc)
    span = window.shape[1]
    window[...] = jnp.dot(
        rel_bias[...], window_hot(buckets, core, tokens, span, rel_bias.shape[1]), precision=lax.Precision.HIGHEST
    )
    first[...] = rms_scale(layer_input[...].astype(f32))[0].astype(bf16)
    spread(0)
    spread(1)
    turn(0)
    spread(2)
    turn(1)
    close(0)
    pieces[0].arrive()
    mine = pl.ds(pl.multiple_of(core * tokens, tokens), tokens)
    for n in (2, 3, 4, 5, 0, 1):
        value = dot_nn(first[...], qkv[:, 384 * n : 384 * n + 384]).astype(bf16)
        lanes = slice(384 * (n % 2), 384 * (n % 2) + 384)
        if n < 2:
            q[:, lanes] = (value.astype(f32) * SCORE_SCALE).astype(bf16)
        elif n < 4:
            keys[mine, lanes] = value
        else:
            values[mine, lanes] = value
        if n in (3, 5):
            ref = keys if n == 3 else values
            remote(ref.at[mine], ref.at[mine], kv_send.at[n // 4], kv_recv.at[n // 4], here.sibling).start()
    keep(qkv, qkv_h)
    keep(q, q_h)
    close(1)
    pieces[1].arrive()
    keep(out, out_h)
    theirs = pl.ds(pl.multiple_of((1 - core) * tokens, tokens), tokens)
    await_bytes(keys.at[theirs], kv_recv.at[0])
    await_bytes(values.at[theirs], kv_recv.at[1])
    keep(keys, keys_h)
    keep(values, values_h)

    def attend(pair):
        attend_pair(pair, q, keys, values, window, q_doc, k_doc, table, attended, logs)

    attend(0)
    spread(3)
    attend(1)
    turn(2)
    attend(2)
    spread(4)
    close(2)
    attend(3)
    turn(3)
    attend(4)
    spread(5)
    close(3)
    attend(5)
    turn(4)
    keep(attended, attended_h)
    keep(logs, logs_h)
    pieces[2].arrive()
    pieces[3].arrive()
    keep(up, up_h)
    for n in range(3):
        lanes = slice(256 * n, 256 * n + 256)
        residual[:, lanes] = layer_input[:, lanes].astype(f32) + dot_nn(attended[...].astype(bf16), out[:, lanes])
    normed[...] = rms_scale(residual[...])[0].astype(bf16)
    keep(residual, residual_h)
    keep(normed, normed_h)

    def ascend(n):
        lanes = slice(256 * n, 256 * n + 256)
        value = dot_nn(normed[...], up[:, lanes])
        square = value * value
        bent = jnp.tanh(GELU_SLOPE * value * (1.0 + GELU_CUBE * square))
        hidden[:, lanes] = (0.5 * value * (1.0 + bent)).astype(bf16)
        slope[:, lanes] = 0.5 * (1.0 + bent) + (0.5 * GELU_SLOPE) * value * (1.0 - bent * bent) * (
            1.0 + (3.0 * GELU_CUBE) * square
        )

    def pull_down(n):
        lanes = slice(256 * n, 256 * n + 256)
        down_part[lanes, :] = dot_tn(hidden[:, lanes], cotangent[...]).astype(bf16)

    for n in range(12):
        ascend(n)
        if n == 5:
            close(4)
            turn(5)
    close(5)
    for n in range(12):
        pull_down(n)
    keep(down_part, down_part_h)
    pieces[4].arrive()
    pieces[5].arrive()
    for n in range(12):
        lanes = slice(256 * n, 256 * n + 256)
        up_grad[:, lanes] = (slope[:, lanes] * dot_nt(cotangent[...], down[lanes, :])).astype(bf16)
    keep(up_grad, up_grad_h)
    for n in range(3):
        lanes = slice(256 * n, 256 * n + 256)
        output[:, lanes] = (residual[:, lanes] + dot_nn(hidden[...], down[:, lanes])).astype(bf16)
    keep(output, output_h)
    for copy in stashed:
        copy.wait()
    for piece in pieces:
        piece.drain()
    for swap in swaps:
        swap.wait_send()
    await_bytes(keys.at[mine], kv_send.at[0])
    await_bytes(values.at[mine], kv_send.at[1])


def forward(layer_input, cotangent, lengths, buckets, rel_bias, attn_gain, ffn_gain, qkv_own, out_own, up_own, down_own):
    tokens, width = layer_input.shape
    pieces = lax.axis_size("blk")
    devices = lax.axis_size("row") * pieces
    count = tokens * pieces
    ff = up_own.shape[1]
    span = count + tokens
    bf16, f32 = jnp.bfloat16, jnp.float32
    vmem, anywhere = pl.BlockSpec(memory_space=pltpu.VMEM), pl.BlockSpec(memory_space=pl.ANY)
    wholes = [(w.shape[0] * devices, w.shape[1]) for w in (qkv_own, out_own, up_own, down_own)]
    kept = [
        (wholes[0], bf16), (wholes[1], bf16), (wholes[2], bf16), ((tokens, width), bf16), ((count, width), bf16),
        ((count, width), bf16), ((tokens, width), f32), ((tokens, 128), f32), ((tokens, width), f32), ((tokens, width), bf16),
        ((tokens, ff), bf16), ((ff, width), bf16),
    ]
    shapes = [((tokens, width), bf16)] + kept
    scratch = [wholes[0], wholes[1], wholes[2], wholes[3]]
    scratch = [pltpu.VMEM(shape, bf16) for shape in scratch] + [pltpu.VMEM(*k) for k in kept[3:]]
    scratch += [pltpu.VMEM((tokens, width), bf16), pltpu.VMEM(qkv_own.shape, bf16), pltpu.VMEM(up_own.shape, bf16)]
    scratch += [pltpu.VMEM((w.shape[0], w.shape[1] // 2), bf16) for w in (qkv_own, out_own, up_own)]
    scratch += [
        pltpu.VMEM((tokens, width), bf16), pltpu.VMEM((tokens, ff), bf16), pltpu.VMEM((tokens, ff), f32),
        pltpu.VMEM((2, TILE, span - TILE), f32), pltpu.VMEM((tokens, 1), jnp.int32), pltpu.VMEM((1, count), jnp.int32),
    ]
    dma = pltpu.SemaphoreType.DMA
    scratch += [dma((3,))] * 2 + [dma((2,))] * 2 + [dma((16,))]
    scratch += [dma((6, 4))] * 2 + [dma((6, 8))] * 4 + [dma((6,))] * 2
    return pl.pallas_call(
        forward_kernel,
        out_shape=[jax.ShapeDtypeStruct(*s) for s in shapes] + [jax.ShapeDtypeStruct((HEADS, span), f32)],
        in_specs=[vmem, vmem, pl.BlockSpec(memory_space=pltpu.SMEM)] + [vmem] * 8,
        out_specs=[anywhere] * len(shapes) + [vmem],
        scratch_shapes=scratch,
        compiler_params=pltpu.CompilerParams(collective_id=0, has_side_effects=True, vmem_limit_bytes=60 * 2**20),
    )(layer_input, cotangent, lengths, buckets, rel_bias, attn_gain, ffn_gain, qkv_own, out_own, up_own, down_own)


class Scatter:
    def __init__(self, here, number, half, mine, bufs, sems):
        self.here, self.number, self.half, self.mine = here, number, half, mine
        self.held, self.x_turn, self.y_turn, self.x_in, self.y_in, self.z_in = bufs
        self.c_send, self.c_recv, self.x_send, self.x_recv, self.y_send, self.y_recv, self.z_send, self.z_recv = sems

    def swap(self):
        n = self.number
        remote(self.half(1 - self.here.core), self.held, self.c_send.at[n], self.c_recv.at[n], self.here.sibling).start()

    def block(self, x, y, z):
        return self.held.at[chip_of(x, y, z)]

    def merge(self):
        here, n = self.here, self.number
        await_bytes(self.held, self.c_recv.at[n])
        mine = self.mine()

        def one(chip, _):
            self.held[chip] = (mine[chip].astype(jnp.float32) + self.held[chip].astype(jnp.float32)).astype(jnp.bfloat16)
            return 0

        lax.fori_loop(0, CHIPS, one, 0)
        for z in range(LINE):
            block = self.block(1 - here.x, 1 - here.y, z)
            if z < 2:
                remote(block, self.x_turn.at[z], self.x_send.at[n, z], self.x_recv.at[n, z], here.to_x).start()
            else:
                remote(block, self.y_turn.at[z - 2], self.y_send.at[n, z], self.y_recv.at[n, z], here.to_y).start()
        for z in range(LINE):
            if z < 2:
                self.to_x(z)
            else:
                self.to_y(z)

    def to_x(self, z):
        here, n = self.here, self.number
        remote(self.block(1 - here.x, here.y, z), self.x_in.at[z], self.x_send.at[n, 4 + z], self.x_recv.at[n, 4 + z], here.to_x).start()

    def to_y(self, z):
        here, n = self.here, self.number
        remote(self.block(here.x, 1 - here.y, z), self.y_in.at[z], self.y_send.at[n, 4 + z], self.y_recv.at[n, 4 + z], here.to_y).start()

    def add(self, chip, *terms):
        total = self.held[chip].astype(jnp.float32)
        for term in terms:
            total = total + term[...].astype(jnp.float32)
        self.held[chip] = total.astype(jnp.bfloat16)

    def turn(self):
        here, n = self.here, self.number
        for z in range(LINE):
            if z < 2:
                await_bytes(self.x_turn.at[z], self.x_recv.at[n, z])
                self.add(chip_of(here.x, 1 - here.y, z), self.x_turn.at[z])
                self.to_y(z)
            else:
                await_bytes(self.y_turn.at[z - 2], self.y_recv.at[n, z])
                self.add(chip_of(1 - here.x, here.y, z), self.y_turn.at[z - 2])
                self.to_x(z)

    def column(self):
        here, n = self.here, self.number
        for step in (1, 2, 3, 0):
            z = here.line(step)
            await_bytes(self.x_in.at[z], self.x_recv.at[n, 4 + z])
            await_bytes(self.y_in.at[z], self.y_recv.at[n, 4 + z])
            self.add(chip_of(here.x, here.y, z), self.x_in.at[z], self.y_in.at[z])
            if step:
                remote(self.block(here.x, here.y, z), self.z_in.at[step - 1], self.z_send.at[n, step], self.z_recv.at[n, step], here.to_z(step)).start()

    def total(self):
        here, n = self.here, self.number
        total = self.held[here.chip].astype(jnp.float32)
        for step in (1, 2, 3):
            await_bytes(self.z_in.at[step - 1], self.z_recv.at[n, step])
            total = total + self.z_in[step - 1].astype(jnp.float32)
        return total

    def drain(self):
        n = self.number
        block = self.held.at[0]
        await_bytes(self.held, self.c_send.at[n])
        for z in range(LINE):
            await_bytes(block, (self.x_send if z < 2 else self.y_send).at[n, z])
            await_bytes(block, self.x_send.at[n, 4 + z])
            await_bytes(block, self.y_send.at[n, 4 + z])
        for step in (1, 2, 3):
            await_bytes(block, self.z_send.at[n, step])


def backward_kernel(
    layer_input, cotangent, lengths, buckets, rel_bias, attn_gain, ffn_gain, qkv_own, up_own, window,
    qkv_h, out_h, up_h, q_h, keys_h, values_h, attended_h, logs_h, residual_h, normed_h, up_grad_h, down_part_h,
    grad_input, attn_total, qkv_total, out_total, ffn_total, up_total, down_total, bias_total,
    qkv, out, up, q, keys, values, attended, logs, residual, normed, up_grad, down_mine,
    up_part, out_part, qkv_part, residual_grad, attended_grad, qkv_grad, k_parts, v_parts, k_near, v_near,
    table, sums, probs, grads, diagonals, q_doc, k_doc, bias_buf, *rest,
):
    scatter_bufs = [rest[6 * n : 6 * n + 6] for n in range(6)]
    ends = rest[36:40]
    gets = rest[40:44]
    loads, kv_send, kv_recv, end_send, end_recv, bias_send, bias_recv = rest[44:51]
    sems = rest[51:]
    here = Slice()
    core = here.core
    tokens = layer_input.shape[0]
    bf16, f32 = jnp.bfloat16, jnp.float32
    pending = {}

    def load(name, src, dst):
        pending[name] = pltpu.make_async_copy(src, dst, loads.at[len(pending)])
        pending[name].start()

    half_rows = down_part_h.shape[2] // 2
    down_half = lambda n: lambda c: down_part_h.at[:, c, pl.ds(n * half_rows, half_rows), :]
    load("down0", down_half(0)(core), down_mine.at[0])
    load("normed", normed_h, normed)
    load("up_grad", up_grad_h, up_grad)
    load("down1", down_half(1)(core), down_mine.at[1])
    load("up", up_h, up)
    load("residual", residual_h, residual)
    load("attended", attended_h, attended)
    load("out", out_h, out)
    load("q", q_h, q)
    load("keys", keys_h, keys)
    load("values", values_h, values)
    load("logs", logs_h, logs)
    load("qkv", qkv_h, qkv)

    def columns(part, width, start, step):
        return lambda c: part.at[:, :, pl.ds(pl.multiple_of(c * step + start, 128), width)]

    widths = [buf[0].shape[2] for buf in scatter_bufs]
    halves = [
        down_half(0), down_half(1),
        columns(up_part, widths[2], 0, 2 * widths[2]), columns(up_part, widths[3], widths[3], 2 * widths[3]),
        columns(out_part, widths[4], 0, widths[4]), columns(qkv_part, widths[5], 0, widths[5]),
    ]
    mines = [lambda: down_mine.at[0], lambda: down_mine.at[1]] + [lambda h=h: h(core) for h in halves[2:]]
    down0, down1, up0, up1, outs, qkvs = pieces = [
        Scatter(here, n, halves[n], mines[n], scatter_bufs[n], sems) for n in range(6)
    ]
    here.greet()
    down0.swap()
    down1.swap()
    documents(lengths, core, tokens, q_doc, k_doc)

    def finish(n):
        total = pieces[n].total()
        if n < 2:
            down_total[n * half_rows : (n + 1) * half_rows, :] = total
            return
        rows = total.shape[0] // 2
        ends[n - 2][0] = total[:rows]
        ends[n - 2][1] = total[rows:]
        remote(ends[n - 2].at[1 - core], gets[n - 2], end_send.at[n - 2], end_recv.at[n - 2], here.sibling).start()

    def owned(n):
        await_bytes(gets[n - 2], end_recv.at[n - 2])
        mine, theirs = ends[n - 2][core], gets[n - 2][...]
        return (jnp.where(core == 0, mine, theirs), jnp.where(core == 0, theirs, mine))

    def chips(value):
        return value.reshape(CHIPS, value.shape[0] // CHIPS, value.shape[1])

    def pull_up(n):
        lanes = slice(256 * n, 256 * n + 256)
        up_part[:, :, lanes] = chips(dot_tn(normed[...], up_grad[:, lanes]).astype(bf16))

    pending["normed"].wait()
    pending["up_grad"].wait()
    for n in (0, 1, 2, 6, 7, 8):
        pull_up(n)
    up0.swap()
    pending["down0"].wait()
    down0.merge()
    for n in (3, 4, 5, 9, 10, 11):
        pull_up(n)
    up1.swap()
    pending["down1"].wait()
    down1.merge()
    down0.turn()
    pending["up"].wait()
    for n in range(3):
        lanes = slice(256 * n, 256 * n + 256)
        residual_grad[:, lanes] = dot_nt(up_grad[...], up[lanes, :])
    up0.merge()
    down1.turn()
    pending["residual"].wait()
    residual_grad[...] = cotangent[...].astype(f32) + rms_pull(residual[...], residual_grad[...])
    rounded = residual_grad[...].astype(bf16)
    pending["attended"].wait()
    pending["out"].wait()
    out_part[...] = chips(dot_tn(attended[...].astype(bf16), rounded).astype(bf16))
    outs.swap()
    down0.column()
    attended_grad[...] = dot_nt(rounded, out[...]).astype(bf16)
    for name in ("q", "keys", "values", "logs"):
        pending[name].wait()

    def pull(pair):
        pull_pair(pair, q, keys, values, window, q_doc, k_doc, attended, attended_grad, logs, table, sums, probs, grads, diagonals, qkv_grad, k_parts, v_parts)

    pull(0)
    up1.merge()
    up0.turn()
    down1.column()
    finish(0)
    pull(1)
    outs.merge()
    up1.turn()
    pull(2)
    up0.column()
    finish(1)
    pull(3)
    outs.turn()
    up1.column()
    finish(2)
    pull(4)
    pull(5)
    mine = pl.ds(pl.multiple_of(core * tokens, tokens), tokens)
    theirs = pl.ds(pl.multiple_of((1 - core) * tokens, tokens), tokens)
    for n, (part, near) in enumerate(((k_parts, k_near), (v_parts, v_near))):
        remote(part.at[theirs], near, kv_send.at[n], kv_recv.at[n], here.sibling).start()
    outs.column()
    finish(3)
    hot = window_hot(buckets, core, tokens, window.shape[1], rel_bias.shape[1])
    bias_buf[0, :HEADS, : rel_bias.shape[1]] = lax.dot_general(
        diagonals[...], hot, (((1,), (1,)), ((), ())), precision=lax.Precision.HIGHEST, preferred_element_type=f32
    )
    width = layer_input.shape[1]
    for n, (part, near) in enumerate(((k_parts, k_near), (v_parts, v_near))):
        await_bytes(near, kv_recv.at[n])
        qkv_grad[:, (n + 1) * width : (n + 2) * width] = (part[mine, :].astype(f32) + near[...].astype(f32)).astype(bf16)
    pending["qkv"].wait()
    first = rms_scale(layer_input[...].astype(f32))[0].astype(bf16)
    for n in range(6):
        lanes = slice(384 * n, 384 * n + 384)
        qkv_part[:, :, lanes] = chips(dot_tn(first, qkv_grad[:, lanes]).astype(bf16))
    qkvs.swap()

    def pass_bias(n, slot, target):
        remote(bias_buf.at[slot], bias_buf.at[slot + 1], bias_send.at[n], bias_recv.at[n], target).start()

    def add_bias(n, slot):
        await_bytes(bias_buf.at[slot + 1], bias_recv.at[n])
        bias_buf[slot + 2] = bias_buf[slot] + bias_buf[slot + 1]

    pass_bias(0, 0, here.sibling)
    finish(4)
    add_bias(0, 0)
    pass_bias(1, 2, here.to_x)
    qkvs.merge()
    add_bias(1, 2)
    pass_bias(2, 4, here.to_y)
    for n in range(3):
        lanes = slice(256 * n, 256 * n + 256)
        grad_input[:, lanes] = dot_nt(qkv_grad[...], qkv[lanes, :])
    grad_input[...] = residual_grad[...] + rms_pull(layer_input[...].astype(f32), grad_input[...])
    add_bias(2, 4)
    bias_buf[7 + here.z] = bias_buf[6]
    for step in (1, 2, 3):
        remote(bias_buf.at[6], bias_buf.at[7 + here.z], bias_send.at[2 + step], bias_recv.at[2 + step], here.to_z(step)).start()
    qkvs.turn()
    first_half, second_half = owned(2), owned(3)
    up_sum = jnp.concatenate([first_half[0], second_half[0], first_half[1], second_half[1]], axis=1)
    up_total[...] = up_sum * ffn_gain[...]
    ffn_total[...] = jnp.sum(up_sum * up_own[...].astype(f32), axis=1, keepdims=True)
    out_total[...] = jnp.concatenate(owned(4), axis=1)
    qkvs.column()
    for step in (1, 2, 3):
        await_bytes(bias_buf.at[6], bias_recv.at[2 + step])
    bias_total[...] = ((bias_buf[7] + bias_buf[8]) + (bias_buf[9] + bias_buf[10]))[:HEADS, : rel_bias.shape[1]]
    finish(5)
    qkv_sum = jnp.concatenate(owned(5), axis=1)
    qkv_total[...] = qkv_sum * attn_gain[...]
    attn_total[...] = jnp.sum(qkv_sum * qkv_own[...].astype(f32), axis=1, keepdims=True)
    for piece in pieces:
        piece.drain()
    for n in range(4):
        await_bytes(gets[n], end_send.at[n])
    for n in range(2):
        await_bytes(k_near, kv_send.at[n])
    for n in range(6):
        await_bytes(bias_buf.at[0], bias_send.at[n])


def backward(layer_input, cotangent, lengths, buckets, rel_bias, attn_gain, ffn_gain, qkv_own, up_own, window, kept):
    tokens, width = layer_input.shape
    count = tokens * lax.axis_size("blk")
    ff = up_own.shape[1]
    shard = qkv_own.shape[0]
    span = window.shape[1]
    bf16, f32 = jnp.bfloat16, jnp.float32
    vmem, anywhere = pl.BlockSpec(memory_space=pltpu.VMEM), pl.BlockSpec(memory_space=pl.ANY)
    kept = list(kept)
    kept[-1] = kept[-1].reshape(CHIPS, 2, ff // CHIPS // 2, width)
    block = 2 * shard
    down_rows = ff // CHIPS // 4
    shapes = [(down_rows, width), (down_rows, width), (block, ff // 4), (block, ff // 4), (block, width // 2), (block, 3 * width // 2)]
    scratch = [pltpu.VMEM(k.shape, k.dtype) for k in kept[:-1]]
    scratch += [
        pltpu.VMEM((2, CHIPS, down_rows, width), bf16),
        pltpu.VMEM((CHIPS, block, ff), bf16), pltpu.VMEM((CHIPS, block, width), bf16), pltpu.VMEM((CHIPS, block, 3 * width), bf16),
        pltpu.VMEM((tokens, width), f32), pltpu.VMEM((tokens, width), bf16), pltpu.VMEM((tokens, 3 * width), bf16),
        pltpu.VMEM((count, width), bf16), pltpu.VMEM((count, width), bf16), pltpu.VMEM((tokens, width), bf16), pltpu.VMEM((tokens, width), bf16),
        pltpu.VMEM((2, TILE, span - TILE), f32), pltpu.VMEM((2, TILE, span - TILE), f32),
        pltpu.VMEM((2 * tokens, count), bf16), pltpu.VMEM((2 * tokens, count), bf16),
        pltpu.VMEM((HEADS, span), f32), pltpu.VMEM((tokens, 1), jnp.int32), pltpu.VMEM((1, count), jnp.int32),
        pltpu.VMEM((11, 16, 128), f32),
    ]
    for rows, columns in shapes:
        scratch += [pltpu.VMEM((n, rows, columns), bf16) for n in (CHIPS, 2, 2, 4, 4, 3)]
    scratch += [pltpu.VMEM((2, rows // 2, columns), f32) for rows, columns in shapes[2:]]
    scratch += [pltpu.VMEM((rows // 2, columns), f32) for rows, columns in shapes[2:]]
    dma = pltpu.SemaphoreType.DMA
    scratch += [dma((16,)), dma((2,)), dma((2,)), dma((4,)), dma((4,)), dma((6,)), dma((6,))]
    scratch += [dma((6,))] * 2 + [dma((6, 8))] * 4 + [dma((6, 4))] * 2
    outs = [(tokens, width), (shard, 1), (shard, 3 * width), (shard, width), (shard, 1), (shard, ff), (ff // CHIPS // 2, width), rel_bias.shape]
    return pl.pallas_call(
        backward_kernel,
        out_shape=[jax.ShapeDtypeStruct(s, f32) for s in outs],
        in_specs=[vmem, vmem, pl.BlockSpec(memory_space=pltpu.SMEM)] + [vmem] * 7 + [anywhere] * len(kept),
        out_specs=[vmem] * len(outs),
        scratch_shapes=scratch,
        compiler_params=pltpu.CompilerParams(collective_id=1, has_side_effects=True, vmem_limit_bytes=63 * 2**20),
    )(layer_input, cotangent, lengths, buckets, rel_bias, attn_gain, ffn_gain, qkv_own, up_own, window, *kept)


def slice_body(
    layer_input, doc_lengths, buckets, attn_gain, qkv_weight, out_weight, ffn_gain, up_weight, down_weight, rel_bias, cotangent
):
    f32 = jnp.float32
    row_buckets = jnp.pad(buckets, (0, 1))[None, :]
    gains = (attn_gain.astype(f32)[:, None], ffn_gain.astype(f32)[:, None])
    output, *kept, window = forward(
        layer_input[0], cotangent[0], doc_lengths, row_buckets, rel_bias, *gains, qkv_weight, out_weight, up_weight, down_weight
    )
    grad_input, attn_total, qkv_total, out_total, ffn_total, up_total, down_total, bias_total = backward(
        layer_input[0], cotangent[0], doc_lengths, row_buckets, rel_bias, *gains, qkv_weight, up_weight, window, kept
    )
    return (
        output[None], grad_input[None], attn_total[:, 0], qkv_total, out_total, ffn_total[:, 0], up_total, down_total, bias_total
    )


def solution(mesh):
    fits = dict(mesh.shape) == {"row": CHIPS, "blk": 2}
    return jax.shard_map(
        slice_body if fits else body,
        mesh=mesh,
        in_specs=(
            P("row", "blk", None),
            P("row", None),
            P(),
            P(("row", "blk")),
            P(("row", "blk"), None),
            P(("row", "blk"), None),
            P(("row", "blk")),
            P(("row", "blk"), None),
            P(("row", "blk"), None),
            P(),
            P("row", "blk", None),
        ),
        out_specs=(
            P("row", "blk", None),
            P("row", "blk", None),
            P(("row", "blk")),
            P(("row", "blk"), None),
            P(("row", "blk"), None),
            P(("row", "blk")),
            P(("row", "blk"), None),
            P(("row", "blk"), None),
            P(),
        ),
        check_vma=False,
    )
```

```python
import jax
import jax.numpy as jnp
from jax import lax
from jax.experimental import pallas as pl
from jax.experimental.pallas import tpu as pltpu
from jax.sharding import PartitionSpec as P

D = 768
HEADS = 12
HEAD_DIM = 64


EPSILON = 1e-06
SCORE_SCALE = 0.125
NEG_LARGE = -1e30
PRECISE = lax.Precision.HIGHEST


def rms_forward(values, scale_gain):
    inverse = lax.rsqrt(jnp.mean(values * values, axis=-1, keepdims=True) + EPSILON)
    return (values * inverse * scale_gain, inverse)


def rms_backward(values, inverse, scale_gain, incoming):
    scaled = incoming * scale_gain
    gain_grad = jnp.sum(incoming * values * inverse, axis=0)
    value_grad = inverse * scaled - values * inverse**3 * jnp.mean(
        scaled * values, axis=-1, keepdims=True
    )
    return (value_grad, gain_grad)


def smooth_gate(values):
    return jax.nn.gelu(values, approximate=True)


def doc_index(positions, doc_ends):
    return jnp.sum((positions[:, None] >= doc_ends[None, :]).astype(jnp.int32), axis=1)


def block_width(row_count):
    return 512 if row_count % 512 == 0 else row_count


def bucket_hot(buckets, bucket_count, query_first, key_first, query_count, key_count):
    row_length = (buckets.shape[0] + 1) // 2
    span = query_count + key_count - 1
    start_at = key_first - query_first - (query_count - 1) + row_length - 1
    window_ids = lax.dynamic_slice_in_dim(buckets, start_at, span)
    return (window_ids[:, None] == jnp.arange(bucket_count, dtype=jnp.int32)[None, :]).astype(
        jnp.float32
    )


def spread_diagonals(window, query_count, key_count):
    head_count, span = window.shape
    tiled = jnp.broadcast_to(window[:, None, :], (head_count, query_count, span)).reshape(
        head_count, query_count * span
    )
    padded = jnp.pad(tiled, ((0, 0), (0, query_count)))
    grid = padded.reshape(head_count, query_count, span + 1)[:, :, :key_count]
    return grid[:, ::-1, :]


def sum_diagonals(grid):
    head_count, query_count, key_count = grid.shape
    span = query_count + key_count - 1
    flipped = grid[:, ::-1, :]
    padded = jnp.pad(flipped, ((0, 0), (0, 0), (0, span + 1 - key_count)))
    flat = padded.reshape(head_count, query_count * (span + 1))[:, : query_count * span]
    return jnp.sum(flat.reshape(head_count, query_count, span), axis=1)


def block_scores(query_heads, key_heads, query_pos, key_pos, query_doc, key_doc, buckets, rel_bias):
    query_count = query_heads.shape[0]
    key_count = key_heads.shape[0]
    raw_scores = (
        jnp.einsum("qhd,khd->hqk", query_heads, key_heads, preferred_element_type=jnp.float32)
        * SCORE_SCALE
    )
    hot_table = bucket_hot(
        buckets, rel_bias.shape[1], query_pos[0], key_pos[0], query_count, key_count
    )
    window = jnp.dot(rel_bias, hot_table.T, precision=PRECISE)
    scores = raw_scores + spread_diagonals(window, query_count, key_count)
    same_doc = (query_doc[:, None] == key_doc[None, :])[None]
    return (scores, same_doc, hot_table)


def grad_block(
    query_heads,
    dout_heads,
    log_total,
    delta,
    query_pos,
    query_doc,
    key_heads,
    value_heads,
    key_pos,
    key_doc,
    buckets,
    rel_bias,
):
    scores, same_doc, hot_table = block_scores(
        query_heads, key_heads, query_pos, key_pos, query_doc, key_doc, buckets, rel_bias
    )
    probabilities = jnp.where(same_doc, jnp.exp(scores - log_total[..., None]), 0.0)
    prob_grad = jnp.einsum(
        "qhd,khd->hqk", dout_heads, value_heads, preferred_element_type=jnp.float32
    )
    score_grad = (probabilities * (prob_grad - delta[..., None])).astype(jnp.bfloat16)
    query_part = (
        jnp.einsum("hqk,khd->qhd", score_grad, key_heads, preferred_element_type=jnp.float32)
        * SCORE_SCALE
    )
    key_part = (
        jnp.einsum("hqk,qhd->khd", score_grad, query_heads, preferred_element_type=jnp.float32)
        * SCORE_SCALE
    )
    value_part = jnp.einsum(
        "hqk,qhd->khd",
        probabilities.astype(jnp.bfloat16),
        dout_heads,
        preferred_element_type=jnp.float32,
    )
    diagonal_totals = sum_diagonals(score_grad.astype(jnp.float32))
    bias_part = jnp.dot(diagonal_totals, hot_table, precision=PRECISE)
    return (query_part, key_part, value_part, bias_part)


def body(
    layer_input,
    doc_lengths,
    buckets,
    attn_gain,
    qkv_weight,
    out_weight,
    ffn_gain,
    up_weight,
    down_weight,
    rel_bias,
    cotangent,
):
    tokens = layer_input.shape[1]
    my_piece = lax.axis_index("blk")
    positions = my_piece * tokens + jnp.arange(tokens, dtype=jnp.int32)
    doc_ends = jnp.cumsum(doc_lengths[0])
    my_docs = doc_index(positions, doc_ends)
    gathered = (
        lax.all_gather(attn_gain, ("row", "blk"), axis=0, tiled=True),
        lax.all_gather(qkv_weight, ("row", "blk"), axis=0, tiled=True),
        lax.all_gather(out_weight, ("row", "blk"), axis=0, tiled=True),
        lax.all_gather(ffn_gain, ("row", "blk"), axis=0, tiled=True),
        lax.all_gather(up_weight, ("row", "blk"), axis=0, tiled=True),
        lax.all_gather(down_weight, ("row", "blk"), axis=0, tiled=True),
    )
    gain_first, qkv_full, out_full, gain_second, up_full, down_full = gathered
    gain_first = gain_first.astype(jnp.float32)
    gain_second = gain_second.astype(jnp.float32)
    inputs = layer_input[0].astype(jnp.float32)
    normed, inv_attn = rms_forward(inputs, gain_first)
    normed_b = normed.astype(jnp.bfloat16)
    projected = jnp.dot(normed_b, qkv_full, preferred_element_type=jnp.float32).astype(jnp.bfloat16)
    query_proj = projected[:, :D]
    key_proj = projected[:, D : 2 * D]
    value_proj = projected[:, 2 * D :]
    query_heads = query_proj.reshape(tokens, HEADS, HEAD_DIM)
    start_state = (
        jnp.zeros((HEADS, tokens, HEAD_DIM), jnp.float32),
        jnp.full((HEADS, tokens), NEG_LARGE, jnp.float32),
        jnp.zeros((HEADS, tokens), jnp.float32),
    )
    key_piece = lax.all_gather(key_proj, "blk", axis=0, tiled=True)
    value_piece = lax.all_gather(value_proj, "blk", axis=0, tiled=True)
    row_count = key_piece.shape[0]
    attend_block_rows = block_width(row_count)
    block_count = row_count // attend_block_rows
    key_blocks = key_piece.reshape(block_count, attend_block_rows, HEADS, HEAD_DIM)
    value_blocks = value_piece.reshape(block_count, attend_block_rows, HEADS, HEAD_DIM)
    offsets = attend_block_rows * jnp.arange(block_count, dtype=jnp.int32)

    def advance(state_in, block_item):
        weighted, running_max, denominator = state_in
        key_block, value_block, offset = block_item
        key_pos = offset + jnp.arange(attend_block_rows, dtype=jnp.int32)
        scores, same_doc, unused_hot = block_scores(
            query_heads,
            key_block,
            positions,
            key_pos,
            my_docs,
            doc_index(key_pos, doc_ends),
            buckets,
            rel_bias,
        )
        scores = jnp.where(same_doc, scores, NEG_LARGE)
        new_max = jnp.maximum(running_max, jnp.max(scores, axis=2))
        rescale = jnp.exp(running_max - new_max)
        probabilities = jnp.where(same_doc, jnp.exp(scores - new_max[..., None]), 0.0)
        denominator = denominator * rescale + jnp.sum(probabilities, axis=2)
        weighted = weighted * rescale[..., None] + jnp.einsum(
            "hqk,khd->hqd",
            probabilities.astype(jnp.bfloat16),
            value_block,
            preferred_element_type=jnp.float32,
        )
        return ((weighted, new_max, denominator), None)

    state_out, unused_out = lax.scan(advance, start_state, (key_blocks, value_blocks, offsets))
    weighted, running_max, denominator = state_out
    attended = jnp.transpose(weighted / denominator[..., None], (1, 0, 2)).reshape(tokens, D)
    log_total = running_max + jnp.log(denominator)
    attended_b = attended.astype(jnp.bfloat16)
    residual = inputs + jnp.dot(attended_b, out_full, preferred_element_type=jnp.float32)
    normed_ffn, inv_ffn = rms_forward(residual, gain_second)
    normed_ffn_b = normed_ffn.astype(jnp.bfloat16)
    up_proj = jnp.dot(normed_ffn_b, up_full, preferred_element_type=jnp.float32)
    activated, activate_back = jax.vjp(smooth_gate, up_proj)
    hidden = activated.astype(jnp.bfloat16)
    result = residual + jnp.dot(hidden, down_full, preferred_element_type=jnp.float32)
    output = result.astype(jnp.bfloat16)[None]
    qkv_full, out_full, up_full, down_full = (
        lax.all_gather(qkv_weight, ("row", "blk"), axis=0, tiled=True),
        lax.all_gather(out_weight, ("row", "blk"), axis=0, tiled=True),
        lax.all_gather(up_weight, ("row", "blk"), axis=0, tiled=True),
        lax.all_gather(down_weight, ("row", "blk"), axis=0, tiled=True),
    )
    out_grad_b = cotangent[0]
    out_grad = out_grad_b.astype(jnp.float32)
    grad_down = jnp.einsum("tf,td->fd", hidden, out_grad_b, preferred_element_type=jnp.float32)
    hidden_grad = jnp.einsum("td,fd->tf", out_grad_b, down_full, preferred_element_type=jnp.float32)
    up_grad = activate_back(hidden_grad)[0].astype(jnp.bfloat16)
    grad_up = jnp.einsum("td,tf->df", normed_ffn_b, up_grad, preferred_element_type=jnp.float32)
    ffn_norm_grad = jnp.einsum("tf,df->td", up_grad, up_full, preferred_element_type=jnp.float32)
    residual_part, grad_ffn_gain = rms_backward(residual, inv_ffn, gain_second, ffn_norm_grad)
    residual_grad = out_grad + residual_part
    residual_grad_b = residual_grad.astype(jnp.bfloat16)
    grad_out = jnp.einsum(
        "td,te->de", attended_b, residual_grad_b, preferred_element_type=jnp.float32
    )
    attended_grad = jnp.einsum(
        "te,de->td", residual_grad_b, out_full, preferred_element_type=jnp.float32
    ).astype(jnp.bfloat16)
    dout_heads = attended_grad.reshape(tokens, HEADS, HEAD_DIM)
    delta = jnp.einsum(
        "thd,thd->ht", dout_heads.astype(jnp.float32), attended.reshape(tokens, HEADS, HEAD_DIM)
    )
    bias_start = jnp.zeros(rel_bias.shape, jnp.float32)
    all_keys, all_values = (
        lax.all_gather(key_proj, "blk", axis=0, tiled=True),
        lax.all_gather(value_proj, "blk", axis=0, tiled=True),
    )
    row_count = all_keys.shape[0]
    block_rows = block_width(row_count)
    block_count = row_count // block_rows
    offsets = block_rows * jnp.arange(block_count, dtype=jnp.int32)

    def key_step(state_in, block_item):
        query_total, bias_total = state_in
        key_block, value_block, offset = block_item
        key_pos = offset + jnp.arange(block_rows, dtype=jnp.int32)
        query_part, key_part, value_part, bias_part = grad_block(
            query_heads,
            dout_heads,
            log_total,
            delta,
            positions,
            my_docs,
            key_block,
            value_block,
            key_pos,
            doc_index(key_pos, doc_ends),
            buckets,
            rel_bias,
        )
        return ((query_total + query_part, bias_total + bias_part), (key_part, value_part))

    key_start = (jnp.zeros((tokens, HEADS, HEAD_DIM), jnp.float32), bias_start)
    (query_total, bias_total), (key_parts, value_parts) = lax.scan(
        key_step,
        key_start,
        (
            all_keys.reshape(block_count, block_rows, HEADS, HEAD_DIM),
            all_values.reshape(block_count, block_rows, HEADS, HEAD_DIM),
            offsets,
        ),
    )
    key_grad, value_grad = (
        lax.psum_scatter(
            key_parts.reshape(row_count, D).astype(jnp.bfloat16),
            "blk",
            scatter_dimension=0,
            tiled=True,
        ).astype(jnp.float32),
        lax.psum_scatter(
            value_parts.reshape(row_count, D).astype(jnp.bfloat16),
            "blk",
            scatter_dimension=0,
            tiled=True,
        ).astype(jnp.float32),
    )
    query_grad = query_total.reshape(tokens, D)
    qkv_grad = jnp.concatenate([query_grad, key_grad, value_grad], axis=1).astype(jnp.bfloat16)
    grad_qkv = jnp.einsum("td,te->de", normed_b, qkv_grad, preferred_element_type=jnp.float32)
    normed_grad = jnp.einsum("te,de->td", qkv_grad, qkv_full, preferred_element_type=jnp.float32)
    input_part, grad_attn_gain = rms_backward(inputs, inv_attn, gain_first, normed_grad)
    grad_input = (residual_grad + input_part)[None]
    shares = (
        lax.psum_scatter(grad_attn_gain, ("row", "blk"), scatter_dimension=0, tiled=True),
        lax.psum_scatter(grad_qkv, ("row", "blk"), scatter_dimension=0, tiled=True),
        lax.psum_scatter(grad_out, ("row", "blk"), scatter_dimension=0, tiled=True),
        lax.psum_scatter(grad_ffn_gain, ("row", "blk"), scatter_dimension=0, tiled=True),
        lax.psum_scatter(grad_up, ("row", "blk"), scatter_dimension=0, tiled=True),
        lax.psum_scatter(grad_down, ("row", "blk"), scatter_dimension=0, tiled=True),
    )
    attn_share, qkv_share, out_share, ffn_share, up_share, down_share = shares
    bias_grad = lax.psum(bias_total, ("row", "blk"))
    return (
        output,
        grad_input,
        attn_share,
        qkv_share,
        out_share,
        ffn_share,
        up_share,
        down_share,
        bias_grad,
    )


MESH = pl.DeviceIdType.MESH
CHIPS = 16
LINE = 4
HALF = 64
PAIR = 128
TILE = 128
PAIRS = HEADS // 2
GELU_SLOPE = 0.7978845608028654
GELU_CUBE = 0.044715


def rms_scale(values):
    inverse = lax.rsqrt(jnp.mean(values * values, axis=-1, keepdims=True) + EPSILON)
    return (values * inverse, inverse)


def rms_pull(values, scaled):
    inverse = lax.rsqrt(jnp.mean(values * values, axis=-1, keepdims=True) + EPSILON)
    return inverse * scaled - values * inverse**3 * jnp.mean(scaled * values, axis=-1, keepdims=True)


def place():
    row = lax.axis_index("row")
    return (lax.rem(row, 2), lax.rem(lax.div(row, 2), 2), lax.div(row, 4), lax.axis_index("blk"))


def chip_of(x, y, z):
    return (z * 2 + y) * 2 + x


class Slice:
    def __init__(self):
        self.x, self.y, self.z, self.core = place()
        x, y, z, core = self.x, self.y, self.z, self.core
        self.chip = chip_of(x, y, z)
        self.sibling = (self.chip, 1 - core)
        self.to_x = (chip_of(1 - x, y, z), core)
        self.to_y = (chip_of(x, 1 - y, z), core)
        self.beside = z + 1 - 2 * lax.rem(z, 2)
        self.to_beside = (chip_of(x, y, self.beside), core)

    def line(self, step):
        return lax.rem(self.z + step, LINE)

    def to_z(self, step):
        return (chip_of(self.x, self.y, self.line(step)), self.core)

    def everyone(self):
        return [self.sibling, self.to_x, self.to_y] + [self.to_z(step) for step in (1, 2, 3)]


def run(*steps):
    for step, *given in steps:
        step(*given)


def remote(src, dst, send, recv, target):
    return pltpu.make_async_remote_copy(
        src_ref=src, dst_ref=dst, send_sem=send, recv_sem=recv, device_id=target, device_id_type=MESH
    )


def await_bytes(like, sem):
    pltpu.make_async_copy(like, like, sem).wait()


class Gather:
    def __init__(self, here, number, full, rows, pitch, width, start, core_step, beside, sems):
        self.here, self.number, self.full, self.beside = here, number, full, beside
        self.rows, self.pitch, self.width, self.start, self.core_step = rows, pitch, width, start, core_step
        self.z_send, self.z_recv, self.x_send, self.x_recv, self.y_send, self.y_recv, self.b_send, self.b_recv = sems[:8]
        self.c_send, self.c_recv = sems[8:]

    def block(self, chip):
        row = pl.multiple_of(chip * self.pitch + self.here.core * self.core_step[0] + self.start[0], 16)
        column = pl.multiple_of(self.here.core * self.core_step[1] + self.start[1], 128)
        return self.full.at[pl.ds(row, self.rows), pl.ds(column, self.width)]

    def line(self):
        mine, n = self.block(self.here.chip), self.number
        for step in (1, 2, 3):
            remote(mine, mine, self.z_send.at[n, step], self.z_recv.at[n, step], self.here.to_z(step)).start()

    def column(self, step, x, y):
        return self.block(chip_of(x, y, self.here.line(LINE - step)))

    def share(self, block):
        remote(block, block, self.c_send.at[self.number], self.c_recv.at[self.number], self.here.sibling).start()

    def spread(self, step):
        here, n = self.here, self.number
        block = self.column(step, here.x, here.y)
        if step:
            await_bytes(block, self.z_recv.at[n, step])
        remote(block, block, self.x_send.at[n, step], self.x_recv.at[n, step], here.to_x).start()
        remote(block, block, self.y_send.at[n, step], self.y_recv.at[n, step], here.to_y).start()
        self.share(block)

    def steps(self):
        return (0, 2) if self.beside else (0, 1, 2, 3)

    def relay_x(self, step):
        here, n = self.here, self.number
        block = self.column(step, 1 - here.x, here.y)
        await_bytes(block, self.x_recv.at[n, step])
        if step < 2 and step in self.steps():
            remote(block, block, self.y_send.at[n, 4 + step], self.y_recv.at[n, 4 + step], here.to_y).start()
        self.share(block)

    def relay_y(self, step):
        here, n = self.here, self.number
        block = self.column(step, here.x, 1 - here.y)
        await_bytes(block, self.y_recv.at[n, step])
        if step >= 2 and step in self.steps():
            remote(block, block, self.x_send.at[n, 2 + step], self.x_recv.at[n, 2 + step], here.to_x).start()
        self.share(block)

    def close(self, step):
        here, n = self.here, self.number
        block = self.column(step, 1 - here.x, 1 - here.y)
        await_bytes(block, self.y_recv.at[n, 4 + step] if step < 2 else self.x_recv.at[n, 2 + step])
        if self.beside:
            remote(block, block, self.b_send.at[n, step // 2], self.b_recv.at[n, step // 2], here.to_beside).start()
        self.share(block)

    def last(self, m):
        here, n = self.here, self.number
        block = self.block(chip_of(1 - here.x, 1 - here.y, lax.rem(here.beside + 2 * m, LINE)))
        await_bytes(block, self.b_recv.at[n, m])
        self.share(block)

    def whole(self):
        return self.full.at[pl.ds(0, CHIPS * self.rows), pl.ds(0, self.width)]

    def arrive(self):
        await_bytes(self.whole(), self.c_recv.at[self.number])

    def drain(self):
        block, n = self.block(self.here.chip), self.number
        for step in (1, 2, 3):
            await_bytes(block, self.z_send.at[n, step])
        for step in range(5 if self.beside else 6):
            await_bytes(block, self.x_send.at[n, step])
            await_bytes(block, self.y_send.at[n, step])
        if self.beside:
            for m in (0, 1):
                await_bytes(block, self.b_send.at[n, m])
        await_bytes(self.whole(), self.c_send.at[n])


class Scatter:
    def __init__(self, here, number, half, beside, bufs, sems):
        self.here, self.number, self.half, self.beside = here, number, half, beside
        self.held, self.b_in, self.x_turn, self.y_turn, self.x_in, self.y_in, self.z_in = bufs
        self.z_send, self.z_recv, self.x_send, self.x_recv, self.y_send, self.y_recv, self.b_send, self.b_recv = sems[:8]
        self.c_send, self.c_recv = sems[8:]

    def swap(self):
        n = self.number
        remote(self.half(1 - self.here.core), self.held, self.c_send.at[n], self.c_recv.at[n], self.here.sibling).start()

    def swapped(self):
        await_bytes(self.held, self.c_send.at[self.number])

    def block(self, x, y, z):
        return self.held.at[chip_of(x, y, z)]

    def merge(self):
        here, n = self.here, self.number
        await_bytes(self.held, self.c_recv.at[n])
        mine = self.half(here.core)

        def one(chip, _):
            self.held[chip] = (mine[chip].astype(jnp.float32) + self.held[chip].astype(jnp.float32)).astype(jnp.bfloat16)
            return 0

        lax.fori_loop(0, CHIPS, one, 0)
        if self.beside:
            for m in (0, 1):
                block = self.block(1 - here.x, 1 - here.y, lax.rem(here.beside + 2 * m, LINE))
                remote(block, self.b_in.at[m], self.b_send.at[n, m], self.b_recv.at[n, m], here.to_beside).start()
        else:
            for step in (0, 2, 1, 3):
                self.across(step)
        for step in range(LINE):
            if step >= 2 or step not in self.steps():
                self.to_x(here.line(step))
            if step < 2 or step not in self.steps():
                self.to_y(here.line(step))

    def steps(self):
        return (0, 2) if self.beside else (0, 1, 2, 3)

    def across(self, step):
        here, n = self.here, self.number
        block = self.block(1 - here.x, 1 - here.y, here.line(step))
        if step < 2:
            remote(block, self.y_turn.at[step], self.y_send.at[n, 4 + step], self.y_recv.at[n, 4 + step], here.to_y).start()
        else:
            remote(block, self.x_turn.at[step - 2], self.x_send.at[n, 2 + step], self.x_recv.at[n, 2 + step], here.to_x).start()

    def to_x(self, z):
        here, n = self.here, self.number
        remote(self.block(1 - here.x, here.y, z), self.x_in.at[z], self.x_send.at[n, z], self.x_recv.at[n, z], here.to_x).start()

    def to_y(self, z):
        here, n = self.here, self.number
        remote(self.block(here.x, 1 - here.y, z), self.y_in.at[z], self.y_send.at[n, z], self.y_recv.at[n, z], here.to_y).start()

    def add(self, x, y, z, *terms):
        chip = chip_of(x, y, z)
        total = self.held[chip].astype(jnp.float32)
        for term in terms:
            total = total + term[...].astype(jnp.float32)
        self.held[chip] = total.astype(jnp.bfloat16)

    def cross(self, m):
        here, n = self.here, self.number
        await_bytes(self.b_in.at[m], self.b_recv.at[n, m])
        self.add(1 - here.x, 1 - here.y, here.line(2 * m), self.b_in.at[m])
        self.across(2 * m)

    def turn(self, step):
        here, n = self.here, self.number
        z = here.line(step)
        if step < 2:
            await_bytes(self.y_turn.at[step], self.y_recv.at[n, 4 + step])
            self.add(1 - here.x, here.y, z, self.y_turn.at[step])
            self.to_x(z)
        else:
            await_bytes(self.x_turn.at[step - 2], self.x_recv.at[n, 2 + step])
            self.add(here.x, 1 - here.y, z, self.x_turn.at[step - 2])
            self.to_y(z)

    def column(self):
        here, n = self.here, self.number
        for step in (1, 3, 2, 0):
            z = here.line(step)
            await_bytes(self.x_in.at[z], self.x_recv.at[n, z])
            await_bytes(self.y_in.at[z], self.y_recv.at[n, z])
            self.add(here.x, here.y, z, self.x_in.at[z], self.y_in.at[z])
            if step:
                remote(self.block(here.x, here.y, z), self.z_in.at[step - 1], self.z_send.at[n, step], self.z_recv.at[n, step], here.to_z(step)).start()

    def total(self):
        here, n = self.here, self.number
        total = self.held[here.chip].astype(jnp.float32)
        for step in (1, 2, 3):
            await_bytes(self.z_in.at[step - 1], self.z_recv.at[n, step])
            total = total + self.z_in[step - 1].astype(jnp.float32)
        return total

    def drain(self):
        n = self.number
        block = self.held.at[0]
        for step in range(5 if self.beside else 6):
            await_bytes(block, self.x_send.at[n, step])
            await_bytes(block, self.y_send.at[n, step])
        if self.beside:
            for m in (0, 1):
                await_bytes(block, self.b_send.at[n, m])
        for step in (1, 2, 3):
            await_bytes(block, self.z_send.at[n, step])


def low_lanes(shape):
    return lax.broadcasted_iota(jnp.int32, shape, 1) < HALF


def one_head(block, second):
    low = low_lanes(block.shape)
    return jnp.where(low != bool(second), block, jnp.zeros_like(block))


def dot_nt(a, b):
    return lax.dot_general(a, b, (((1,), (1,)), ((), ())), preferred_element_type=jnp.float32)


def dot_tn(a, b):
    return lax.dot_general(a, b, (((0,), (0,)), ((), ())), preferred_element_type=jnp.float32)


def dot_nn(a, b):
    return jnp.dot(a, b, preferred_element_type=jnp.float32)


def bias_table(window_row, span):
    rows = jnp.broadcast_to(window_row, (TILE, span))
    return pltpu.roll(rows, span - (TILE - 1), 1, stride=1, stride_axis=0)


def diagonal_sums(table, span):
    wide = jnp.concatenate([table, jnp.zeros((TILE, span - table.shape[1]), jnp.float32)], axis=1)
    total = jnp.zeros((8, span), jnp.float32)
    for group in range(TILE // 8):
        total = total + pltpu.roll(wide[8 * group : 8 * group + 8, :], TILE - 1 - 8 * group, 1)
    sums = total[0:1, :]
    for row in range(1, 8):
        sums = sums + pltpu.roll(total[row : row + 1, :], span - row, 1)
    return sums


def attend_head(pair, second, q, keys, values, window, q_doc, k_doc, table, attended, log_total):
    tokens, span, count = q.shape[0], window.shape[1], keys.shape[0]
    lanes = slice(pair * PAIR, (pair + 1) * PAIR)
    head = 2 * pair + second
    table[...] = bias_table(window[head : head + 1, :], span)[:, : table.shape[1]]
    for k in range(tokens // TILE):
        rows = slice(k * TILE, k * TILE + TILE)
        shift = tokens - TILE - k * TILE
        scores = dot_nt(one_head(q[rows, lanes], second), keys[:, lanes]) + table[:, shift : shift + count]
        scores = jnp.where(q_doc[rows, :] == k_doc[...], scores, NEG_LARGE)
        top = jnp.max(scores, axis=1, keepdims=True)
        weights = jnp.exp(scores - top)
        total = jnp.sum(weights, axis=1, keepdims=True)
        part = dot_nn(weights.astype(jnp.bfloat16), values[:, lanes]) * (1.0 / total)
        logs = log_total[rows, :]
        lane = lax.broadcasted_iota(jnp.int32, logs.shape, 1)
        log_total[rows, :] = jnp.where(lane == head, top + jnp.log(total), logs)
        if second:
            attended[rows, lanes] = jnp.where(low_lanes(part.shape), attended[rows, lanes], part)
        else:
            attended[rows, lanes] = part


def pull_scores(pair, second, q, keys, values, window, q_doc, k_doc, attended, attended_grad, log_total, table, sums, pulled, probs, grads, diagonals):
    tokens, span, count = q.shape[0], window.shape[1], keys.shape[0]
    lanes = slice(pair * PAIR, (pair + 1) * PAIR)
    head = 2 * pair + second
    table[...] = bias_table(window[head : head + 1, :], span)[:, : table.shape[1]]
    pulled[...] = dot_nt(one_head(attended_grad[:, lanes], second), values[:, lanes])
    sums[...] = jnp.zeros_like(sums)
    for k in range(tokens // TILE):
        rows = slice(k * TILE, k * TILE + TILE)
        run = slice(tokens - TILE - k * TILE, tokens - TILE - k * TILE + count)
        product = one_head(attended_grad[rows, lanes], second).astype(jnp.float32) * attended[rows, lanes]
        delta = jnp.sum(product, axis=1, keepdims=True)
        logs = log_total[rows, :]
        lane = lax.broadcasted_iota(jnp.int32, logs.shape, 1)
        log = jnp.sum(jnp.where(lane == head, logs, 0.0), axis=1, keepdims=True)
        scores = dot_nt(one_head(q[rows, lanes], second), keys[:, lanes]) + table[:, run]
        weights = jnp.exp(jnp.where(q_doc[rows, :] == k_doc[...], scores - log, NEG_LARGE))
        score_grad = weights * (pulled[rows, :] - delta)
        sums[:, run] += score_grad
        here = slice(second * tokens + k * TILE, second * tokens + k * TILE + TILE)
        probs[here, :] = weights.astype(jnp.bfloat16)
        grads[here, :] = score_grad.astype(jnp.bfloat16)
    diagonals[head : head + 1, :] = diagonal_sums(sums[...], span)


def pull_pair(pair, q, keys, attended_grad, probs, grads, q_grad):
    tokens = q.shape[0]
    lanes = slice(pair * PAIR, (pair + 1) * PAIR)
    both = lambda rows: jnp.concatenate([one_head(rows, 0), one_head(rows, 1)], axis=0)
    key = keys[:, lanes]
    query_grad = dot_nn(grads[:tokens, :], one_head(key, 0)) + dot_nn(grads[tokens:, :], one_head(key, 1))
    q_grad[:, 3 * pair * PAIR : (3 * pair + 1) * PAIR] = (SCORE_SCALE * query_grad).astype(jnp.bfloat16)
    return (dot_tn(grads[...], both(q[:, lanes])), dot_tn(probs[...], both(attended_grad[:, lanes])))


def documents(lengths, core, tokens, q_doc, k_doc):
    count = k_doc.shape[1]
    queries = core * tokens + lax.broadcasted_iota(jnp.int32, (tokens, 1), 0)
    keys = lax.broadcasted_iota(jnp.int32, (1, count), 1)
    end = jnp.int32(0)
    q_index, k_index = jnp.zeros((tokens, 1), jnp.int32), jnp.zeros((1, count), jnp.int32)
    for n in range(lengths.shape[1]):
        end = end + lengths[0, n]
        q_index = q_index + (queries >= end).astype(jnp.int32)
        k_index = k_index + (keys >= end).astype(jnp.int32)
    q_doc[...] = q_index
    k_doc[...] = k_index


def window_hot(buckets, core, tokens, span, count):
    ids = buckets[:, pl.ds(pl.multiple_of((1 - core) * tokens, 128), span)]
    return (jnp.broadcast_to(ids, (count, span)) == lax.broadcasted_iota(jnp.int32, (count, span), 0)).astype(jnp.float32)


def upright(vector):
    count = vector.shape[0]
    row = jnp.broadcast_to(vector.astype(jnp.float32).reshape(1, count), (count, count))
    same = lax.broadcasted_iota(jnp.int32, (count, count), 0) == lax.broadcasted_iota(jnp.int32, (count, count), 1)
    return jnp.sum(jnp.where(same, row, 0.0), axis=1, keepdims=True)


def flat(column):
    count = column.shape[0]
    same = lax.broadcasted_iota(jnp.int32, (count, count), 0) == lax.broadcasted_iota(jnp.int32, (count, count), 1)
    return jnp.sum(jnp.where(same, jnp.broadcast_to(column, (count, count)), 0.0), axis=0)


BESIDE_IN = (False, False, False, True, True, True, True, True)
BESIDE_OUT = (True, True, True, True, False, False, False, False)


def layer_kernel(
    layer_input, cotangent, lengths, buckets, rel_bias, attn_gain, ffn_gain, qkv_own, out_own, up_own, down_own,
    output, grad_input, qkv_sum, out_sum, up_sum, down_sum, bias_sum,
    qkv, out, up, down, q, keys, values, attended, logs, residual, normed, first, hidden, slope,
    fold_qkv, fold_up, near_qkv, near_out, near_up, window, row_buckets, q_doc, k_doc, table, sums,
    down_part, up_part, out_part, attended_grad, qkv_grad, k_near, v_near, pulled, diagonals, bias_buf, *rest,
):
    bufs = [rest[7 * n : 7 * n + 7] for n in range(8)]
    ends, gets = rest[56:62], rest[62:68]
    swap_send, swap_recv, kv_send, kv_recv, end_send, end_recv, bias_send, bias_recv, output_sem = rest[68:77]
    gather_sems, scatter_sems = rest[77:87], rest[87:97]
    here = Slice()
    core = here.core
    tokens, width = layer_input.shape[1:]
    ff = up_own.shape[1]
    bf16, f32 = jnp.bfloat16, jnp.float32
    barrier = pltpu.get_barrier_semaphore()
    for target in here.everyone():
        pl.semaphore_signal(barrier, inc=1, device_id=target, device_id_type=MESH)
    mine = pl.ds(pl.multiple_of(core * tokens, tokens), tokens)
    theirs = pl.ds(pl.multiple_of((1 - core) * tokens, tokens), tokens)
    shard = 2 * qkv_own.shape[0]
    own_rows = down_own.shape[0]
    trio = 3 * PAIR

    split = ((fold_qkv, near_qkv), (out_own, near_out), (fold_up, near_up))
    swaps = []
    quarter = ff // 4
    gathers = [Gather(here, g, qkv, shard, shard, trio, (0, 2 * g * trio), (0, trio), BESIDE_IN[g], gather_sems) for g in range(3)]
    gathers += [
        Gather(here, 3, out, shard, shard, width // 2, (0, 0), (0, width // 2), BESIDE_IN[3], gather_sems),
        Gather(here, 4, up, shard, shard, quarter, (0, 0), (0, 2 * quarter), BESIDE_IN[4], gather_sems),
        Gather(here, 5, up, shard, shard, quarter, (0, quarter), (0, 2 * quarter), BESIDE_IN[5], gather_sems),
        Gather(here, 6, down, own_rows // 2, 2 * own_rows, width, (0, 0), (own_rows, 0), BESIDE_IN[6], gather_sems),
        Gather(here, 7, down, own_rows // 2, 2 * own_rows, width, (own_rows // 2, 0), (own_rows, 0), BESIDE_IN[7], gather_sems),
    ]

    def fold():
        gain = upright(attn_gain[...])
        for pair in range(PAIRS):
            for part in range(3):
                at = (pair % 2) * 3 * trio + (pair // 2) * trio + part * PAIR
                own = qkv_own[:, part * width + pair * PAIR : part * width + (pair + 1) * PAIR]
                fold_qkv[:, at : at + PAIR] = (own.astype(f32) * gain).astype(bf16)
        fold_up[...] = (up_own[...].astype(f32) * upright(ffn_gain[...])).astype(bf16)
        down[pl.ds(pl.multiple_of((2 * here.chip + core) * own_rows, own_rows), own_rows), :] = down_own[...]

    def enter():
        pl.semaphore_wait(barrier, len(here.everyone()))
        for n, (own, near) in enumerate(split):
            half = near.shape[1]
            other = own.at[:, pl.ds(pl.multiple_of((1 - core) * half, 128), half)]
            swaps.append(remote(other, near, swap_send.at[n], swap_recv.at[n], here.sibling))
            swaps[-1].start()

    def prepare():
        documents(lengths, core, tokens, q_doc, k_doc)
        count = buckets.shape[0]
        row_buckets[:, :count] = buckets[...].reshape(1, count)
        row_buckets[:, count:] = jnp.zeros((1, row_buckets.shape[1] - count), jnp.int32)
        hot = window_hot(row_buckets, core, tokens, window.shape[1], rel_bias.shape[1])
        window[...] = jnp.dot(rel_bias[...], hot, precision=lax.Precision.HIGHEST)
        first[...] = rms_scale(layer_input[0].astype(f32))[0].astype(bf16)

    def assemble(n):
        own, near = split[n]
        half = near.shape[1]
        swaps[n].wait_recv()
        own_half = own[:, pl.ds(pl.multiple_of(core * half, 128), half)].astype(f32)
        near_half = near[...].astype(f32)
        both = [jnp.where(core == 0, own_half, near_half), jnp.where(core == 0, near_half, own_half)]
        block = jnp.concatenate(both, axis=0).astype(bf16)
        rows = pl.ds(pl.multiple_of(here.chip * shard, shard), shard)
        if n == 0:
            for g in range(3):
                qkv[rows, pl.ds(pl.multiple_of((2 * g + core) * trio, 128), trio)] = block[:, g * trio : (g + 1) * trio]
        else:
            (out if n == 1 else up)[rows, pl.ds(pl.multiple_of(core * half, 128), half)] = block

    def line(n):
        gathers[n].line()

    def spread(n, step):
        gathers[n].spread(step)

    def relay_x(n, step):
        gathers[n].relay_x(step)

    def relay_y(n, step):
        gathers[n].relay_y(step)

    def close(n, m):
        gathers[n].close(m)

    def last(n, m):
        gathers[n].last(m)

    def arrive(*numbers):
        for n in numbers:
            gathers[n].arrive()

    def project(*numbers):
        for pair in numbers:
            value = dot_nn(first[...], qkv[:, pair * trio : (pair + 1) * trio]).astype(bf16)
            lanes = slice(pair * PAIR, (pair + 1) * PAIR)
            q[:, lanes] = (value[:, :PAIR].astype(f32) * SCORE_SCALE).astype(bf16)
            for n, ref in enumerate((keys, values)):
                ref[mine, lanes] = value[:, (n + 1) * PAIR : (n + 2) * PAIR]
                at = ref.at[mine, lanes]
                remote(at, at, kv_send.at[n, pair], kv_recv.at[n, pair], here.sibling).start()

    def attend(pair, second):
        lanes = slice(pair * PAIR, (pair + 1) * PAIR)
        if not second:
            await_bytes(keys.at[theirs, lanes], kv_recv.at[0, pair])
            await_bytes(values.at[theirs, lanes], kv_recv.at[1, pair])
        attend_head(pair, second, q, keys, values, window, q_doc, k_doc, table, attended, logs)

    def mix():
        rounded = attended[...].astype(bf16)
        for n in range(3):
            lanes = slice(256 * n, 256 * n + 256)
            residual[:, lanes] = layer_input[0, :, lanes].astype(f32) + dot_nn(rounded, out[:, lanes])
        normed[...] = rms_scale(residual[...])[0].astype(bf16)

    def hidden_at(lane, count):
        half = ff // 2
        return (pl.ds(lane // half * tokens, tokens), pl.ds(lane % half, count))

    def ascend(*numbers):
        for n in numbers:
            at = hidden_at(256 * n, 256)
            value = dot_nn(normed[...], up[:, 256 * n : 256 * n + 256])
            square = value * value
            bent = jnp.tanh(GELU_SLOPE * value * (1.0 + GELU_CUBE * square))
            hidden[at] = (0.5 * value * (1.0 + bent)).astype(bf16)
            slope[at] = (
                0.5 * (1.0 + bent) + (0.5 * GELU_SLOPE) * value * (1.0 - bent * bent) * (1.0 + (3.0 * GELU_CUBE) * square)
            ).astype(bf16)

    def give_output():
        return pltpu.make_async_copy(normed, output, output_sem.at[0])

    def descend():
        for n in range(3):
            lanes = slice(256 * n, 256 * n + 256)
            low, high = dot_nn(hidden[:tokens], down[: ff // 2, lanes]), dot_nn(hidden[tokens:], down[ff // 2 :, lanes])
            normed[:, lanes] = (residual[:, lanes] + low + high).astype(bf16)
        give_output().start()

    def columns(part, half, start, step):
        return lambda c: part.at[:, :, pl.ds(pl.multiple_of(c * step + start, 128), half)]

    half_rows = own_rows // 2
    halves = [lambda c: down_part.at[:, c, pl.ds(0, half_rows), :], lambda c: down_part.at[:, c, pl.ds(half_rows, half_rows), :]]
    halves += [columns(up_part, quarter, 0, 2 * quarter), columns(up_part, quarter, quarter, 2 * quarter)]
    halves += [columns(out_part, width // 2, 0, width // 2)]
    halves += [columns(up_part, trio, 2 * g * trio, trio) for g in range(3)]
    scatters = [Scatter(here, n, halves[n], BESIDE_OUT[n], bufs[n], scatter_sems) for n in range(8)]

    def swap(*numbers):
        for n in numbers:
            scatters[n].swap()

    def swapped(*numbers):
        for n in numbers:
            scatters[n].swapped()

    def merge(n):
        scatters[n].merge()

    def cross(n, m):
        scatters[n].cross(m)

    def turn(n, step):
        scatters[n].turn(step)

    def column(n):
        scatters[n].column()

    def finish(n):
        total = scatters[n].total()
        if n < 2:
            down_sum[n * half_rows : (n + 1) * half_rows, :] = total
            return
        rows = total.shape[0] // 2
        ends[n - 2][0] = total[:rows]
        ends[n - 2][1] = total[rows:]
        remote(ends[n - 2].at[1 - core], gets[n - 2], end_send.at[n - 2], end_recv.at[n - 2], here.sibling).start()

    def owned(n):
        await_bytes(gets[n - 2], end_recv.at[n - 2])
        own, near = ends[n - 2][core], gets[n - 2][...]
        return (jnp.where(core == 0, own, near), jnp.where(core == 0, near, own))

    def own(n):
        low, high = owned(n)
        if n in (2, 3):
            start = (n - 2) * quarter
            up_sum[:, start : start + quarter] = low
            up_sum[:, start + 2 * quarter : start + 3 * quarter] = high
        elif n == 4:
            out_sum[:, : width // 2] = low
            out_sum[:, width // 2 :] = high
        else:
            for pair, total in ((2 * (n - 5), low), (2 * (n - 5) + 1, high)):
                for part in range(3):
                    lanes = slice(part * width + pair * PAIR, part * width + (pair + 1) * PAIR)
                    qkv_sum[:, lanes] = total[:, part * PAIR : (part + 1) * PAIR]

    def chips(value):
        return value.reshape(CHIPS, value.shape[0] // CHIPS, value.shape[1])

    def pull_down(*numbers):
        for n in numbers:
            part = dot_tn(hidden[hidden_at(4 * own_rows * n, 4 * own_rows)], cotangent[0]).astype(bf16)
            down_part[2 * n : 2 * n + 2] = part.reshape(2, 2, own_rows, width)

    def pull_hidden(*numbers):
        for n in numbers:
            at = hidden_at(256 * n, 256)
            slope[at] = (slope[at].astype(f32) * dot_nt(cotangent[0], down[256 * n : 256 * n + 256, :])).astype(bf16)

    def pull_up(*numbers):
        for n in numbers:
            up_part[:, :, 256 * n : 256 * n + 256] = chips(dot_tn(normed[...], slope[hidden_at(256 * n, 256)]).astype(bf16))

    def pull_normed():
        for n in range(3):
            lanes = slice(256 * n, 256 * n + 256)
            grad_input[:, lanes] = dot_nt(slope[:tokens], up[lanes, : ff // 2]) + dot_nt(slope[tokens:], up[lanes, ff // 2 :])

    def pull_residual():
        grad_input[...] = cotangent[0].astype(f32) + rms_pull(residual[...], grad_input[...])
        normed[...] = grad_input[...].astype(bf16)

    def pull_out():
        out_part[...] = chips(dot_tn(attended[...].astype(bf16), normed[...]).astype(bf16))

    def pull_attended():
        attended_grad[...] = dot_nt(normed[...], out[...]).astype(bf16)

    probs, grads = slope.at[:, pl.ds(0, width)], slope.at[:, pl.ds(width, width)]
    nears = (k_near, v_near)
    chunks = tokens // own_rows

    def part_at(n, half):
        return pl.ds((2 * n + half) * (chunks // 2), chunks // 2)

    def pull_head(pair, second):
        pull_scores(pair, second, q, keys, values, window, q_doc, k_doc, attended, attended_grad, logs, table, sums, pulled, probs, grads, diagonals)

    def pull(pair):
        parts = pull_pair(pair, q, keys, attended_grad, probs, grads, qkv_grad)
        lanes = slice(pair * PAIR, (pair + 1) * PAIR)
        for n, (part, near) in enumerate(zip(parts, nears)):
            down_part[n * chunks : (n + 1) * chunks, :, :, lanes] = part.astype(bf16).reshape(chunks, 2, own_rows, PAIR)
            give = down_part.at[part_at(n, 1 - core), :, :, lanes]
            remote(give, near.at[:, :, :, lanes], kv_send.at[2 + n, pair], kv_recv.at[2 + n, pair], here.sibling).start()

    def pull_qkv(*numbers):
        for pair in numbers:
            lanes = slice(pair * PAIR, (pair + 1) * PAIR)
            for n, near in enumerate(nears):
                await_bytes(near.at[:, :, :, lanes], kv_recv.at[2 + n, pair])
                at = slice(pair * trio + (n + 1) * PAIR, pair * trio + (n + 2) * PAIR)
                total = down_part[part_at(n, core), :, :, lanes].astype(f32) + near[:, :, :, lanes].astype(f32)
                qkv_grad[:, at] = total.astype(bf16).reshape(tokens, PAIR)
            at = slice(pair * trio, (pair + 1) * trio)
            up_part[:, :, at] = chips(dot_tn(first[...], qkv_grad[:, at]).astype(bf16))

    def sum_bias():
        hot = window_hot(row_buckets, core, tokens, window.shape[1], rel_bias.shape[1])
        bias_buf[0] = jnp.zeros(bias_buf.shape[1:], f32)
        bias_buf[0, :HEADS, : rel_bias.shape[1]] = lax.dot_general(
            diagonals[...], hot, (((1,), (1,)), ((), ())), precision=lax.Precision.HIGHEST, preferred_element_type=f32
        )

    def pass_bias(n, slot, target):
        remote(bias_buf.at[slot], bias_buf.at[slot + 1], bias_send.at[n], bias_recv.at[n], target).start()

    def add_bias(n, slot):
        await_bytes(bias_buf.at[slot + 1], bias_recv.at[n])
        bias_buf[slot + 2] = bias_buf[slot] + bias_buf[slot + 1]

    def spread_bias():
        bias_buf[7 + here.z] = bias_buf[6]
        for step in (1, 2, 3):
            remote(bias_buf.at[6], bias_buf.at[7 + here.z], bias_send.at[2 + step], bias_recv.at[2 + step], here.to_z(step)).start()

    def total_bias():
        for step in (1, 2, 3):
            await_bytes(bias_buf.at[6], bias_recv.at[2 + step])
        bias_sum[...] = ((bias_buf[7] + bias_buf[8]) + (bias_buf[9] + bias_buf[10]))[:HEADS, : rel_bias.shape[1]]

    def pull_input():
        for n in range(3):
            lanes = slice(256 * n, 256 * n + 256)
            residual[:, lanes] = dot_nt(qkv_grad[...], qkv[lanes, :])
        grad_input[...] = grad_input[...] + rms_pull(layer_input[0].astype(f32), residual[...])

    def drain():
        give_output().wait()
        for piece in gathers + scatters:
            piece.drain()
        for n in range(6):
            await_bytes(gets[n], end_send.at[n])
            await_bytes(bias_buf.at[0], bias_send.at[n])
        for n in range(4):
            for pair in range(PAIRS):
                await_bytes(keys.at[pl.ds(0, tokens), pl.ds(0, PAIR)], kv_send.at[n, pair])
        for copy in swaps:
            copy.wait_send()

    run(
        (fold,), (enter,), (assemble, 0), (line, 0), (assemble, 1), (assemble, 2), (spread, 0, 0), (prepare,),
        (spread, 1, 0), (line, 1), (spread, 2, 0), (spread, 3, 0), (spread, 0, 1), (relay_x, 0, 0), (relay_y, 0, 0),
        (relay_x, 1, 0), (relay_y, 1, 0), (spread, 0, 2), (relay_x, 2, 0), (relay_y, 2, 0), (line, 2), (spread, 4, 0),
        (spread, 0, 3), (relay_x, 3, 0), (relay_y, 3, 0), (spread, 1, 1), (relay_x, 0, 1), (relay_y, 0, 1), (close, 0, 0),
        (relay_x, 0, 2), (spread, 1, 2), (close, 1, 0), (line, 3), (spread, 1, 3), (relay_y, 0, 2), (relay_x, 4, 0),
        (spread, 2, 1), (close, 2, 0), (relay_x, 0, 3), (relay_x, 1, 1), (spread, 2, 2), (relay_x, 1, 2), (relay_y, 4, 0),
        (line, 4), (spread, 2, 3), (relay_y, 0, 3), (relay_x, 1, 3), (spread, 3, 1), (close, 0, 2), (close, 3, 0),
        (relay_y, 1, 1), (relay_x, 2, 1), (spread, 3, 2), (close, 0, 1), (relay_x, 2, 2), (spread, 3, 3), (relay_y, 1, 2),
        (relay_x, 2, 3), (close, 0, 3), (relay_y, 1, 3), (spread, 4, 1), (relay_x, 3, 1), (arrive, 0), (project, 0),
        (close, 4, 0), (relay_x, 3, 2), (spread, 5, 0), (project, 1), (relay_y, 2, 1), (relay_x, 3, 3), (spread, 4, 2),
        (close, 1, 1), (close, 1, 2), (attend, 0, 0), (close, 1, 3), (relay_y, 2, 2), (relay_y, 2, 3), (line, 5),
        (attend, 0, 1), (last, 3, 0), (relay_y, 3, 1), (relay_x, 4, 1), (spread, 4, 3), (attend, 1, 0), (close, 2, 1),
        (last, 4, 0), (arrive, 1), (relay_y, 3, 2), (relay_x, 5, 0), (project, 2), (project, 3), (relay_y, 3, 3),
        (attend, 1, 1), (relay_x, 4, 2), (spread, 5, 1), (close, 2, 2), (relay_y, 4, 1), (attend, 2, 0), (close, 2, 3),
        (line, 6), (spread, 5, 2), (attend, 2, 1), (relay_y, 5, 0), (attend, 3, 0), (close, 3, 2), (relay_y, 4, 2),
        (relay_x, 4, 3), (arrive, 2), (project, 4), (spread, 5, 3), (project, 5), (attend, 3, 1), (relay_y, 4, 3),
        (relay_x, 5, 1), (spread, 6, 1), (attend, 4, 0), (close, 5, 0), (relay_x, 5, 2), (attend, 4, 1), (spread, 6, 2),
        (attend, 5, 0), (close, 4, 2), (relay_y, 5, 1), (attend, 5, 1), (relay_y, 5, 2), (relay_x, 5, 3), (line, 7),
        (spread, 6, 3), (last, 3, 1), (relay_y, 5, 3), (relay_x, 6, 1), (last, 5, 0), (arrive, 3), (mix,), (last, 4, 1),
        (relay_y, 6, 1), (relay_x, 6, 2), (spread, 6, 0), (spread, 7, 0), (spread, 7, 1), (close, 5, 2), (relay_y, 6, 2),
        (arrive, 4), (ascend, 0), (ascend, 1), (ascend, 2), (ascend, 6), (relay_x, 6, 3), (relay_y, 6, 3), (ascend, 7),
        (spread, 7, 2), (ascend, 8), (pull_down, 0), (pull_down, 1), (relay_x, 6, 0), (relay_y, 6, 0), (pull_down, 4),
        (pull_down, 5), (spread, 7, 3), (relay_x, 7, 0), (relay_y, 7, 0), (last, 5, 1), (relay_x, 7, 1), (relay_y, 7, 1),
        (arrive, 5), (ascend, 3), (ascend, 4), (ascend, 5), (close, 6, 2), (relay_y, 7, 2), (ascend, 9), (ascend, 10),
        (ascend, 11), (pull_down, 2), (close, 6, 0), (relay_x, 7, 2), (pull_down, 3), (pull_down, 6), (pull_down, 7),
        (swap, 0), (swap, 1), (last, 6, 1), (relay_x, 7, 3), (relay_y, 7, 3), (last, 6, 0), (close, 7, 0), (close, 7, 2),
        (merge, 0), (last, 7, 0), (swapped, 0), (last, 7, 1), (cross, 0, 0), (merge, 1), (swapped, 1), (arrive, 6),
        (cross, 0, 1), (arrive, 7), (pull_hidden, 0), (pull_hidden, 1), (pull_hidden, 2), (pull_hidden, 3),
        (pull_hidden, 4), (pull_hidden, 5), (pull_hidden, 6), (pull_hidden, 7), (pull_hidden, 8), (pull_hidden, 9),
        (cross, 1, 0), (pull_hidden, 10), (pull_hidden, 11), (pull_up, 0), (pull_up, 6), (cross, 1, 1), (pull_up, 1),
        (pull_up, 7), (pull_up, 2), (pull_up, 8), (turn, 0, 0), (swap, 2), (pull_up, 3), (pull_up, 9), (pull_up, 4),
        (pull_up, 10), (pull_up, 5), (pull_up, 11), (swap, 3), (pull_normed,), (pull_residual,), (turn, 0, 2), (merge, 2),
        (swapped, 2), (pull_attended,), (pull_head, 0, 0), (turn, 1, 0), (turn, 1, 2), (pull_head, 0, 1), (column, 0),
        (cross, 2, 0), (pull, 0), (cross, 2, 1), (pull_head, 1, 0), (pull_head, 1, 1), (pull, 1), (pull_head, 2, 0),
        (merge, 3), (swapped, 3), (pull_qkv, 0), (pull_qkv, 1), (column, 1), (swap, 5), (pull_head, 2, 1), (turn, 2, 2),
        (pull, 2), (turn, 2, 0), (pull_head, 3, 0), (finish, 0), (cross, 3, 0), (pull_head, 3, 1), (cross, 3, 1),
        (pull_qkv, 2), (pull, 3), (merge, 5), (pull_out,), (swap, 4), (pull_head, 4, 0), (column, 2), (pull_qkv, 3),
        (swap, 6), (pull_head, 4, 1), (turn, 3, 0), (turn, 3, 2), (turn, 5, 2), (turn, 5, 0), (pull, 4), (finish, 1),
        (turn, 5, 3), (descend,), (turn, 5, 1), (merge, 4), (pull_qkv, 4), (column, 3), (pull_head, 5, 0), (merge, 6),
        (pull_head, 5, 1), (finish, 2), (column, 5), (turn, 4, 0), (turn, 4, 2), (pull, 5), (turn, 4, 1), (turn, 4, 3),
        (sum_bias,), (pass_bias, 0, 0, here.sibling), (own, 2), (pull_qkv, 5),
        (add_bias, 0, 0), (pass_bias, 1, 2, here.to_x), (turn, 6, 0), (turn, 6, 2), (swap, 7), (pull_input,), (turn, 6, 1),
        (turn, 6, 3), (finish, 3), (merge, 7), (column, 4), (add_bias, 1, 2), (pass_bias, 2, 4, here.to_y), (own, 3),
        (column, 6), (turn, 7, 0), (finish, 5), (turn, 7, 2), (turn, 7, 1), (turn, 7, 3), (own, 5),
        (add_bias, 2, 4), (spread_bias,), (finish, 4), (column, 7), (own, 4), (finish, 6), (total_bias,), (own, 6),
        (finish, 7), (own, 7),
        (swapped, 4, 5, 6, 7), (drain,),
    )


def layer(layer_input, cotangent, lengths, buckets, rel_bias, attn_gain, ffn_gain, qkv_own, out_own, up_own, down_own):
    tokens, width = layer_input.shape[1:]
    pieces = lax.axis_size("blk")
    devices = lax.axis_size("row") * pieces
    count = tokens * pieces
    span = count + tokens
    shard, ff = up_own.shape
    own_rows = down_own.shape[0]
    bf16, f32, i32 = jnp.bfloat16, jnp.float32, jnp.int32
    vmem = pl.BlockSpec(memory_space=pltpu.VMEM)
    owns = (qkv_own, out_own, up_own, down_own)
    scratch = [((w.shape[0] * devices, w.shape[1]), bf16) for w in owns]
    scratch += [((tokens, width), bf16), ((count, width), bf16), ((count, width), bf16), ((tokens, width), f32), ((tokens, 128), f32)]
    scratch += [((tokens, width), f32), ((tokens, width), bf16), ((tokens, width), bf16)]
    scratch += [((2 * tokens, ff // 2), bf16)] * 2 + [(qkv_own.shape, bf16), (up_own.shape, bf16)]
    scratch += [((w.shape[0], w.shape[1] // 2), bf16) for w in owns[:3]]
    scratch += [((HEADS, span), f32), ((1, 2 * count), i32), ((tokens, 1), i32), ((1, count), i32)]
    scratch += [((TILE, span - TILE), f32)] * 2
    scratch += [((CHIPS, 2, own_rows, width), bf16), ((CHIPS, 2 * shard, ff), bf16), ((CHIPS, 2 * shard, width), bf16)]
    near = (tokens // own_rows // 2, 2, own_rows, width)
    scratch += [((tokens, width), bf16), ((tokens, 3 * width), bf16), (near, bf16), (near, bf16)]
    scratch += [((tokens, count), f32)]
    scratch += [((HEADS, span), f32), ((11, 16, 128), f32)]
    blocks = [(own_rows // 2, width)] * 2 + [(2 * shard, ff // 4)] * 2 + [(2 * shard, width // 2)] + [(2 * shard, 3 * PAIR)] * 3
    for block, beside in zip(blocks, BESIDE_OUT):
        counts = (CHIPS, 2, 1, 1, 4, 4, 3) if beside else (CHIPS, 1, 2, 2, 4, 4, 3)
        scratch += [((n, *block), bf16) for n in counts]
    scratch += [((2, rows // 2, columns), f32) for rows, columns in blocks[2:]]
    scratch += [((rows // 2, columns), f32) for rows, columns in blocks[2:]]
    dma = pltpu.SemaphoreType.DMA
    sems = [dma((3,))] * 2 + [dma((4, PAIRS))] * 2 + [dma((6,))] * 4 + [dma((1,))]
    sems += ([dma((8, 4))] * 2 + [dma((8, 6))] * 4 + [dma((8, 2))] * 2 + [dma((8,))] * 2) * 2
    outs = [((tokens, width), bf16), ((tokens, width), f32)] + [(w.shape, f32) for w in owns] + [(rel_bias.shape, f32)]
    return pl.pallas_call(
        layer_kernel,
        out_shape=[jax.ShapeDtypeStruct(*o) for o in outs],
        in_specs=[vmem, vmem, pl.BlockSpec(memory_space=pltpu.SMEM)] + [vmem] * 8,
        out_specs=[pl.BlockSpec(memory_space=pl.ANY)] + [vmem] * (len(outs) - 1),
        scratch_shapes=[pltpu.VMEM(*s) for s in scratch] + sems,
        compiler_params=pltpu.CompilerParams(collective_id=0, has_side_effects=True, vmem_limit_bytes=64 * 2**20 - 2**19),
    )(layer_input, cotangent, lengths, buckets, rel_bias, attn_gain, ffn_gain, *owns)


def settle_kernel(
    output, grad_input, qkv_sum, out_sum, up_sum, down_sum, bias_sum, attn_gain, ffn_gain, qkv_own, up_own,
    output_o, grad_input_o, attn_total, qkv_total, out_total, ffn_total, up_total, down_total, bias_total,
):
    f32 = jnp.float32
    output_o[0] = output[...]
    grad_input_o[0] = grad_input[...]
    qkv_total[...] = qkv_sum[...] * upright(attn_gain[...])
    attn_total[...] = flat(jnp.sum(qkv_sum[...] * qkv_own[...].astype(f32), axis=1, keepdims=True))
    up_total[...] = up_sum[...] * upright(ffn_gain[...])
    ffn_total[...] = flat(jnp.sum(up_sum[...] * up_own[...].astype(f32), axis=1, keepdims=True))
    out_total[...] = out_sum[...]
    down_total[...] = down_sum[...]
    bias_total[...] = bias_sum[...]


def slice_body(
    layer_input, doc_lengths, buckets, attn_gain, qkv_weight, out_weight, ffn_gain, up_weight, down_weight, rel_bias, cotangent
):
    f32 = jnp.float32
    sums = layer(
        layer_input, cotangent, doc_lengths, buckets, rel_bias, attn_gain, ffn_gain, qkv_weight, out_weight, up_weight, down_weight
    )
    shapes = [(layer_input.shape, jnp.bfloat16), (layer_input.shape, f32), (attn_gain.shape, f32), (qkv_weight.shape, f32)]
    shapes += [(out_weight.shape, f32), (ffn_gain.shape, f32), (up_weight.shape, f32), (down_weight.shape, f32), (rel_bias.shape, f32)]
    vmem = pl.BlockSpec(memory_space=pltpu.VMEM)
    return tuple(
        pl.pallas_call(
            settle_kernel,
            out_shape=[jax.ShapeDtypeStruct(*s) for s in shapes],
            in_specs=[vmem] * 11,
            out_specs=[vmem] * 9,
            compiler_params=pltpu.CompilerParams(vmem_limit_bytes=63 * 2**20),
        )(*sums, attn_gain, ffn_gain, qkv_weight, up_weight)
    )


def solution(mesh):
    fits = dict(mesh.shape) == {"row": CHIPS, "blk": 2}
    return jax.shard_map(
        slice_body if fits else body,
        mesh=mesh,
        in_specs=(
            P("row", "blk", None),
            P("row", None),
            P(),
            P(("row", "blk")),
            P(("row", "blk"), None),
            P(("row", "blk"), None),
            P(("row", "blk")),
            P(("row", "blk"), None),
            P(("row", "blk"), None),
            P(),
            P("row", "blk", None),
        ),
        out_specs=(
            P("row", "blk", None),
            P("row", "blk", None),
            P(("row", "blk")),
            P(("row", "blk"), None),
            P(("row", "blk"), None),
            P(("row", "blk")),
            P(("row", "blk"), None),
            P(("row", "blk"), None),
            P(),
        ),
        check_vma=False,
    )
```

```python
import jax
import jax.numpy as jnp
from jax import lax
from jax.experimental import pallas as pl
from jax.experimental.pallas import tpu as pltpu
from jax.sharding import PartitionSpec as P

D = 768
HEADS = 12
HEAD_DIM = 64


EPSILON = 1e-06
SCORE_SCALE = 0.125
NEG_LARGE = -1e30
PRECISE = lax.Precision.HIGHEST


def rms_forward(values, scale_gain):
    inverse = lax.rsqrt(jnp.mean(values * values, axis=-1, keepdims=True) + EPSILON)
    return (values * inverse * scale_gain, inverse)


def rms_backward(values, inverse, scale_gain, incoming):
    scaled = incoming * scale_gain
    gain_grad = jnp.sum(incoming * values * inverse, axis=0)
    value_grad = inverse * scaled - values * inverse**3 * jnp.mean(
        scaled * values, axis=-1, keepdims=True
    )
    return (value_grad, gain_grad)


def smooth_gate(values):
    return jax.nn.gelu(values, approximate=True)


def doc_index(positions, doc_ends):
    return jnp.sum((positions[:, None] >= doc_ends[None, :]).astype(jnp.int32), axis=1)


def block_width(row_count):
    return 512 if row_count % 512 == 0 else row_count


def bucket_hot(buckets, bucket_count, query_first, key_first, query_count, key_count):
    row_length = (buckets.shape[0] + 1) // 2
    span = query_count + key_count - 1
    start_at = key_first - query_first - (query_count - 1) + row_length - 1
    window_ids = lax.dynamic_slice_in_dim(buckets, start_at, span)
    return (window_ids[:, None] == jnp.arange(bucket_count, dtype=jnp.int32)[None, :]).astype(
        jnp.float32
    )


def spread_diagonals(window, query_count, key_count):
    head_count, span = window.shape
    tiled = jnp.broadcast_to(window[:, None, :], (head_count, query_count, span)).reshape(
        head_count, query_count * span
    )
    padded = jnp.pad(tiled, ((0, 0), (0, query_count)))
    grid = padded.reshape(head_count, query_count, span + 1)[:, :, :key_count]
    return grid[:, ::-1, :]


def sum_diagonals(grid):
    head_count, query_count, key_count = grid.shape
    span = query_count + key_count - 1
    flipped = grid[:, ::-1, :]
    padded = jnp.pad(flipped, ((0, 0), (0, 0), (0, span + 1 - key_count)))
    flat = padded.reshape(head_count, query_count * (span + 1))[:, : query_count * span]
    return jnp.sum(flat.reshape(head_count, query_count, span), axis=1)


def block_scores(query_heads, key_heads, query_pos, key_pos, query_doc, key_doc, buckets, rel_bias):
    query_count = query_heads.shape[0]
    key_count = key_heads.shape[0]
    raw_scores = (
        jnp.einsum("qhd,khd->hqk", query_heads, key_heads, preferred_element_type=jnp.float32)
        * SCORE_SCALE
    )
    hot_table = bucket_hot(
        buckets, rel_bias.shape[1], query_pos[0], key_pos[0], query_count, key_count
    )
    window = jnp.dot(rel_bias, hot_table.T, precision=PRECISE)
    scores = raw_scores + spread_diagonals(window, query_count, key_count)
    same_doc = (query_doc[:, None] == key_doc[None, :])[None]
    return (scores, same_doc, hot_table)


def grad_block(
    query_heads,
    dout_heads,
    log_total,
    delta,
    query_pos,
    query_doc,
    key_heads,
    value_heads,
    key_pos,
    key_doc,
    buckets,
    rel_bias,
):
    scores, same_doc, hot_table = block_scores(
        query_heads, key_heads, query_pos, key_pos, query_doc, key_doc, buckets, rel_bias
    )
    probabilities = jnp.where(same_doc, jnp.exp(scores - log_total[..., None]), 0.0)
    prob_grad = jnp.einsum(
        "qhd,khd->hqk", dout_heads, value_heads, preferred_element_type=jnp.float32
    )
    score_grad = (probabilities * (prob_grad - delta[..., None])).astype(jnp.bfloat16)
    query_part = (
        jnp.einsum("hqk,khd->qhd", score_grad, key_heads, preferred_element_type=jnp.float32)
        * SCORE_SCALE
    )
    key_part = (
        jnp.einsum("hqk,qhd->khd", score_grad, query_heads, preferred_element_type=jnp.float32)
        * SCORE_SCALE
    )
    value_part = jnp.einsum(
        "hqk,qhd->khd",
        probabilities.astype(jnp.bfloat16),
        dout_heads,
        preferred_element_type=jnp.float32,
    )
    diagonal_totals = sum_diagonals(score_grad.astype(jnp.float32))
    bias_part = jnp.dot(diagonal_totals, hot_table, precision=PRECISE)
    return (query_part, key_part, value_part, bias_part)


def body(
    layer_input,
    doc_lengths,
    buckets,
    attn_gain,
    qkv_weight,
    out_weight,
    ffn_gain,
    up_weight,
    down_weight,
    rel_bias,
    cotangent,
):
    tokens = layer_input.shape[1]
    my_piece = lax.axis_index("blk")
    positions = my_piece * tokens + jnp.arange(tokens, dtype=jnp.int32)
    doc_ends = jnp.cumsum(doc_lengths[0])
    my_docs = doc_index(positions, doc_ends)
    gathered = (
        lax.all_gather(attn_gain, ("row", "blk"), axis=0, tiled=True),
        lax.all_gather(qkv_weight, ("row", "blk"), axis=0, tiled=True),
        lax.all_gather(out_weight, ("row", "blk"), axis=0, tiled=True),
        lax.all_gather(ffn_gain, ("row", "blk"), axis=0, tiled=True),
        lax.all_gather(up_weight, ("row", "blk"), axis=0, tiled=True),
        lax.all_gather(down_weight, ("row", "blk"), axis=0, tiled=True),
    )
    gain_first, qkv_full, out_full, gain_second, up_full, down_full = gathered
    gain_first = gain_first.astype(jnp.float32)
    gain_second = gain_second.astype(jnp.float32)
    inputs = layer_input[0].astype(jnp.float32)
    normed, inv_attn = rms_forward(inputs, gain_first)
    normed_b = normed.astype(jnp.bfloat16)
    projected = jnp.dot(normed_b, qkv_full, preferred_element_type=jnp.float32).astype(jnp.bfloat16)
    query_proj = projected[:, :D]
    key_proj = projected[:, D : 2 * D]
    value_proj = projected[:, 2 * D :]
    query_heads = query_proj.reshape(tokens, HEADS, HEAD_DIM)
    start_state = (
        jnp.zeros((HEADS, tokens, HEAD_DIM), jnp.float32),
        jnp.full((HEADS, tokens), NEG_LARGE, jnp.float32),
        jnp.zeros((HEADS, tokens), jnp.float32),
    )
    key_piece = lax.all_gather(key_proj, "blk", axis=0, tiled=True)
    value_piece = lax.all_gather(value_proj, "blk", axis=0, tiled=True)
    row_count = key_piece.shape[0]
    attend_block_rows = block_width(row_count)
    block_count = row_count // attend_block_rows
    key_blocks = key_piece.reshape(block_count, attend_block_rows, HEADS, HEAD_DIM)
    value_blocks = value_piece.reshape(block_count, attend_block_rows, HEADS, HEAD_DIM)
    offsets = attend_block_rows * jnp.arange(block_count, dtype=jnp.int32)

    def advance(state_in, block_item):
        weighted, running_max, denominator = state_in
        key_block, value_block, offset = block_item
        key_pos = offset + jnp.arange(attend_block_rows, dtype=jnp.int32)
        scores, same_doc, unused_hot = block_scores(
            query_heads,
            key_block,
            positions,
            key_pos,
            my_docs,
            doc_index(key_pos, doc_ends),
            buckets,
            rel_bias,
        )
        scores = jnp.where(same_doc, scores, NEG_LARGE)
        new_max = jnp.maximum(running_max, jnp.max(scores, axis=2))
        rescale = jnp.exp(running_max - new_max)
        probabilities = jnp.where(same_doc, jnp.exp(scores - new_max[..., None]), 0.0)
        denominator = denominator * rescale + jnp.sum(probabilities, axis=2)
        weighted = weighted * rescale[..., None] + jnp.einsum(
            "hqk,khd->hqd",
            probabilities.astype(jnp.bfloat16),
            value_block,
            preferred_element_type=jnp.float32,
        )
        return ((weighted, new_max, denominator), None)

    state_out, unused_out = lax.scan(advance, start_state, (key_blocks, value_blocks, offsets))
    weighted, running_max, denominator = state_out
    attended = jnp.transpose(weighted / denominator[..., None], (1, 0, 2)).reshape(tokens, D)
    log_total = running_max + jnp.log(denominator)
    attended_b = attended.astype(jnp.bfloat16)
    residual = inputs + jnp.dot(attended_b, out_full, preferred_element_type=jnp.float32)
    normed_ffn, inv_ffn = rms_forward(residual, gain_second)
    normed_ffn_b = normed_ffn.astype(jnp.bfloat16)
    up_proj = jnp.dot(normed_ffn_b, up_full, preferred_element_type=jnp.float32)
    activated, activate_back = jax.vjp(smooth_gate, up_proj)
    hidden = activated.astype(jnp.bfloat16)
    result = residual + jnp.dot(hidden, down_full, preferred_element_type=jnp.float32)
    output = result.astype(jnp.bfloat16)[None]
    qkv_full, out_full, up_full, down_full = (
        lax.all_gather(qkv_weight, ("row", "blk"), axis=0, tiled=True),
        lax.all_gather(out_weight, ("row", "blk"), axis=0, tiled=True),
        lax.all_gather(up_weight, ("row", "blk"), axis=0, tiled=True),
        lax.all_gather(down_weight, ("row", "blk"), axis=0, tiled=True),
    )
    out_grad_b = cotangent[0]
    out_grad = out_grad_b.astype(jnp.float32)
    grad_down = jnp.einsum("tf,td->fd", hidden, out_grad_b, preferred_element_type=jnp.float32)
    hidden_grad = jnp.einsum("td,fd->tf", out_grad_b, down_full, preferred_element_type=jnp.float32)
    up_grad = activate_back(hidden_grad)[0].astype(jnp.bfloat16)
    grad_up = jnp.einsum("td,tf->df", normed_ffn_b, up_grad, preferred_element_type=jnp.float32)
    ffn_norm_grad = jnp.einsum("tf,df->td", up_grad, up_full, preferred_element_type=jnp.float32)
    residual_part, grad_ffn_gain = rms_backward(residual, inv_ffn, gain_second, ffn_norm_grad)
    residual_grad = out_grad + residual_part
    residual_grad_b = residual_grad.astype(jnp.bfloat16)
    grad_out = jnp.einsum(
        "td,te->de", attended_b, residual_grad_b, preferred_element_type=jnp.float32
    )
    attended_grad = jnp.einsum(
        "te,de->td", residual_grad_b, out_full, preferred_element_type=jnp.float32
    ).astype(jnp.bfloat16)
    dout_heads = attended_grad.reshape(tokens, HEADS, HEAD_DIM)
    delta = jnp.einsum(
        "thd,thd->ht", dout_heads.astype(jnp.float32), attended.reshape(tokens, HEADS, HEAD_DIM)
    )
    bias_start = jnp.zeros(rel_bias.shape, jnp.float32)
    all_keys, all_values = (
        lax.all_gather(key_proj, "blk", axis=0, tiled=True),
        lax.all_gather(value_proj, "blk", axis=0, tiled=True),
    )
    row_count = all_keys.shape[0]
    block_rows = block_width(row_count)
    block_count = row_count // block_rows
    offsets = block_rows * jnp.arange(block_count, dtype=jnp.int32)

    def key_step(state_in, block_item):
        query_total, bias_total = state_in
        key_block, value_block, offset = block_item
        key_pos = offset + jnp.arange(block_rows, dtype=jnp.int32)
        query_part, key_part, value_part, bias_part = grad_block(
            query_heads,
            dout_heads,
            log_total,
            delta,
            positions,
            my_docs,
            key_block,
            value_block,
            key_pos,
            doc_index(key_pos, doc_ends),
            buckets,
            rel_bias,
        )
        return ((query_total + query_part, bias_total + bias_part), (key_part, value_part))

    key_start = (jnp.zeros((tokens, HEADS, HEAD_DIM), jnp.float32), bias_start)
    (query_total, bias_total), (key_parts, value_parts) = lax.scan(
        key_step,
        key_start,
        (
            all_keys.reshape(block_count, block_rows, HEADS, HEAD_DIM),
            all_values.reshape(block_count, block_rows, HEADS, HEAD_DIM),
            offsets,
        ),
    )
    key_grad, value_grad = (
        lax.psum_scatter(
            key_parts.reshape(row_count, D).astype(jnp.bfloat16),
            "blk",
            scatter_dimension=0,
            tiled=True,
        ).astype(jnp.float32),
        lax.psum_scatter(
            value_parts.reshape(row_count, D).astype(jnp.bfloat16),
            "blk",
            scatter_dimension=0,
            tiled=True,
        ).astype(jnp.float32),
    )
    query_grad = query_total.reshape(tokens, D)
    qkv_grad = jnp.concatenate([query_grad, key_grad, value_grad], axis=1).astype(jnp.bfloat16)
    grad_qkv = jnp.einsum("td,te->de", normed_b, qkv_grad, preferred_element_type=jnp.float32)
    normed_grad = jnp.einsum("te,de->td", qkv_grad, qkv_full, preferred_element_type=jnp.float32)
    input_part, grad_attn_gain = rms_backward(inputs, inv_attn, gain_first, normed_grad)
    grad_input = (residual_grad + input_part)[None]
    shares = (
        lax.psum_scatter(grad_attn_gain, ("row", "blk"), scatter_dimension=0, tiled=True),
        lax.psum_scatter(grad_qkv, ("row", "blk"), scatter_dimension=0, tiled=True),
        lax.psum_scatter(grad_out, ("row", "blk"), scatter_dimension=0, tiled=True),
        lax.psum_scatter(grad_ffn_gain, ("row", "blk"), scatter_dimension=0, tiled=True),
        lax.psum_scatter(grad_up, ("row", "blk"), scatter_dimension=0, tiled=True),
        lax.psum_scatter(grad_down, ("row", "blk"), scatter_dimension=0, tiled=True),
    )
    attn_share, qkv_share, out_share, ffn_share, up_share, down_share = shares
    bias_grad = lax.psum(bias_total, ("row", "blk"))
    return (
        output,
        grad_input,
        attn_share,
        qkv_share,
        out_share,
        ffn_share,
        up_share,
        down_share,
        bias_grad,
    )


MESH = pl.DeviceIdType.MESH
CHIPS = 16
LINE = 4
HALF = 64
PAIR = 128
TILE = 128
PAIRS = HEADS // 2
GELU_SLOPE = 0.7978845608028654
GELU_CUBE = 0.044715


def rms_scale(values):
    inverse = lax.rsqrt(jnp.mean(values * values, axis=-1, keepdims=True) + EPSILON)
    return (values * inverse, inverse)


def rms_pull(values, scaled):
    inverse = lax.rsqrt(jnp.mean(values * values, axis=-1, keepdims=True) + EPSILON)
    return inverse * scaled - values * inverse**3 * jnp.mean(scaled * values, axis=-1, keepdims=True)


def place():
    row = lax.axis_index("row")
    return (lax.rem(row, 2), lax.rem(lax.div(row, 2), 2), lax.div(row, 4), lax.axis_index("blk"))


def chip_of(x, y, z):
    return (z * 2 + y) * 2 + x


class Slice:
    def __init__(self):
        self.x, self.y, self.z, self.core = place()
        x, y, z, core = self.x, self.y, self.z, self.core
        self.chip = chip_of(x, y, z)
        self.sibling = (self.chip, 1 - core)
        self.to_x = (chip_of(1 - x, y, z), core)
        self.to_y = (chip_of(x, 1 - y, z), core)
        self.beside = z + 1 - 2 * lax.rem(z, 2)
        self.to_beside = (chip_of(x, y, self.beside), core)

    def line(self, step):
        return lax.rem(self.z + step, LINE)

    def to_z(self, step):
        return (chip_of(self.x, self.y, self.line(step)), self.core)

    def everyone(self):
        return [self.sibling, self.to_x, self.to_y] + [self.to_z(step) for step in (1, 2, 3)]


def run(*steps):
    for step, *given in steps:
        step(*given)


def remote(src, dst, send, recv, target):
    return pltpu.make_async_remote_copy(
        src_ref=src, dst_ref=dst, send_sem=send, recv_sem=recv, device_id=target, device_id_type=MESH
    )


def await_bytes(like, sem):
    pltpu.make_async_copy(like, like, sem).wait()


class Gather:
    def __init__(self, here, number, full, rows, pitch, width, start, core_step, beside, sems):
        self.here, self.number, self.full, self.beside = here, number, full, beside
        self.rows, self.pitch, self.width, self.start, self.core_step = rows, pitch, width, start, core_step
        self.sent, self.shared, self.z_recv, self.x_recv, self.y_recv, self.b_recv, self.c_recv = sems

    def block(self, chip):
        row = pl.multiple_of(chip * self.pitch + self.here.core * self.core_step[0] + self.start[0], 16)
        column = pl.multiple_of(self.here.core * self.core_step[1] + self.start[1], 128)
        return self.full.at[pl.ds(row, self.rows), pl.ds(column, self.width)]

    def line(self):
        mine, n = self.block(self.here.chip), self.number
        for step in (1, 2, 3):
            remote(mine, mine, self.sent.at[n], self.z_recv.at[n, step - 1], self.here.to_z(step)).start()

    def column(self, step, x, y):
        return self.block(chip_of(x, y, self.here.line(LINE - step)))

    def share(self, block):
        remote(block, block, self.shared.at[self.number], self.c_recv.at[self.number], self.here.sibling).start()

    def spread(self, step):
        here, n = self.here, self.number
        block = self.column(step, here.x, here.y)
        if step:
            await_bytes(block, self.z_recv.at[n, step - 1])
        remote(block, block, self.sent.at[n], self.x_recv.at[n, step], here.to_x).start()
        remote(block, block, self.sent.at[n], self.y_recv.at[n, step], here.to_y).start()
        self.share(block)

    def steps(self):
        return (0, 2) if self.beside else (0, 1, 2, 3)

    def relay_x(self, step):
        here, n = self.here, self.number
        block = self.column(step, 1 - here.x, here.y)
        await_bytes(block, self.x_recv.at[n, step])
        if step < 2 and step in self.steps():
            remote(block, block, self.sent.at[n], self.y_recv.at[n, 4 + step], here.to_y).start()
        self.share(block)

    def relay_y(self, step):
        here, n = self.here, self.number
        block = self.column(step, here.x, 1 - here.y)
        await_bytes(block, self.y_recv.at[n, step])
        if step >= 2 and step in self.steps():
            remote(block, block, self.sent.at[n], self.x_recv.at[n, 2 + step], here.to_x).start()
        self.share(block)

    def close(self, step):
        here, n = self.here, self.number
        block = self.column(step, 1 - here.x, 1 - here.y)
        await_bytes(block, self.y_recv.at[n, 4 + step] if step < 2 else self.x_recv.at[n, 2 + step])
        if self.beside:
            remote(block, block, self.sent.at[n], self.b_recv.at[n, step // 2], here.to_beside).start()
        self.share(block)

    def last(self, m):
        here, n = self.here, self.number
        block = self.block(chip_of(1 - here.x, 1 - here.y, lax.rem(here.beside + 2 * m, LINE)))
        await_bytes(block, self.b_recv.at[n, m])
        self.share(block)

    def whole(self):
        return self.full.at[pl.ds(0, CHIPS * self.rows), pl.ds(0, self.width)]

    def arrive(self):
        await_bytes(self.whole(), self.c_recv.at[self.number])

    def drain(self):
        n = self.number
        await_bytes(self.full.at[pl.ds(0, (CHIPS - 1) * self.rows), pl.ds(0, self.width)], self.sent.at[n])
        await_bytes(self.whole(), self.shared.at[n])


class Scatter:
    def __init__(self, here, number, half, beside, bufs, sems):
        self.here, self.number, self.half, self.beside = here, number, half, beside
        self.held, self.b_in, self.x_turn, self.y_turn, self.x_in, self.y_in, self.z_in = bufs
        self.sent, self.c_send, self.z_recv, self.x_recv, self.y_recv, self.xt_recv, self.yt_recv, self.b_recv, self.c_recv = sems

    def swap(self):
        n = self.number
        remote(self.half(1 - self.here.core), self.held, self.c_send.at[n], self.c_recv.at[n], self.here.sibling).start()

    def swapped(self):
        await_bytes(self.held, self.c_send.at[self.number])

    def block(self, x, y, z):
        return self.held.at[chip_of(x, y, z)]

    def merge(self):
        here, n = self.here, self.number
        await_bytes(self.held, self.c_recv.at[n])
        mine = self.half(here.core)

        def one(chip, _):
            self.held[chip] = (mine[chip].astype(jnp.float32) + self.held[chip].astype(jnp.float32)).astype(jnp.bfloat16)
            return 0

        lax.fori_loop(0, CHIPS, one, 0, unroll=True)
        if self.beside:
            for m in (0, 1):
                block = self.block(1 - here.x, 1 - here.y, lax.rem(here.beside + 2 * m, LINE))
                remote(block, self.b_in.at[m], self.sent.at[n], self.b_recv.at[n, m], here.to_beside).start()
        else:
            for step in (0, 2, 1, 3):
                self.across(step)
        for step in range(LINE):
            if step >= 2 or step not in self.steps():
                self.to_x(here.line(step))
            if step < 2 or step not in self.steps():
                self.to_y(here.line(step))

    def steps(self):
        return (0, 2) if self.beside else (0, 1, 2, 3)

    def across(self, step):
        here, n = self.here, self.number
        block = self.block(1 - here.x, 1 - here.y, here.line(step))
        if step < 2:
            remote(block, self.y_turn.at[step], self.sent.at[n], self.yt_recv.at[n, step], here.to_y).start()
        else:
            remote(block, self.x_turn.at[step - 2], self.sent.at[n], self.xt_recv.at[n, step - 2], here.to_x).start()

    def to_x(self, z):
        here, n = self.here, self.number
        remote(self.block(1 - here.x, here.y, z), self.x_in.at[z], self.sent.at[n], self.x_recv.at[n], here.to_x).start()

    def to_y(self, z):
        here, n = self.here, self.number
        remote(self.block(here.x, 1 - here.y, z), self.y_in.at[z], self.sent.at[n], self.y_recv.at[n], here.to_y).start()

    def add(self, x, y, z, *terms):
        chip = chip_of(x, y, z)
        total = self.held[chip].astype(jnp.float32)
        for term in terms:
            total = total + term[...].astype(jnp.float32)
        self.held[chip] = total.astype(jnp.bfloat16)

    def cross(self, m):
        here, n = self.here, self.number
        await_bytes(self.b_in.at[m], self.b_recv.at[n, m])
        self.add(1 - here.x, 1 - here.y, here.line(2 * m), self.b_in.at[m])
        self.across(2 * m)

    def turn(self, step):
        here, n = self.here, self.number
        z = here.line(step)
        if step < 2:
            await_bytes(self.y_turn.at[step], self.yt_recv.at[n, step])
            self.add(1 - here.x, here.y, z, self.y_turn.at[step])
            self.to_x(z)
        else:
            await_bytes(self.x_turn.at[step - 2], self.xt_recv.at[n, step - 2])
            self.add(here.x, 1 - here.y, z, self.x_turn.at[step - 2])
            self.to_y(z)

    def column(self):
        here, n = self.here, self.number
        await_bytes(self.x_in, self.x_recv.at[n])
        await_bytes(self.y_in, self.y_recv.at[n])
        for step in (1, 3, 2, 0):
            z = here.line(step)
            self.add(here.x, here.y, z, self.x_in.at[z], self.y_in.at[z])
            if step:
                remote(self.block(here.x, here.y, z), self.z_in.at[step - 1], self.sent.at[n], self.z_recv.at[n], here.to_z(step)).start()

    def total(self):
        here, n = self.here, self.number
        total = self.held[here.chip].astype(jnp.float32)
        await_bytes(self.z_in, self.z_recv.at[n])
        for step in (1, 2, 3):
            total = total + self.z_in[step - 1].astype(jnp.float32)
        return total

    def drain(self):
        await_bytes(self.held.at[pl.ds(0, CHIPS - 1)], self.sent.at[self.number])


def low_lanes(shape):
    return lax.broadcasted_iota(jnp.int32, shape, 1) < HALF


def one_head(block, second):
    low = low_lanes(block.shape)
    return jnp.where(low != bool(second), block, jnp.zeros_like(block))


def dot_nt(a, b):
    return lax.dot_general(a, b, (((1,), (1,)), ((), ())), preferred_element_type=jnp.float32)


def dot_tn(a, b):
    return lax.dot_general(a, b, (((0,), (0,)), ((), ())), preferred_element_type=jnp.float32)


def dot_nn(a, b):
    return jnp.dot(a, b, preferred_element_type=jnp.float32)


def bias_table(window_row, span):
    rows = jnp.broadcast_to(window_row, (TILE, span))
    return pltpu.roll(rows, span - (TILE - 1), 1, stride=1, stride_axis=0)


def diagonal_sums(table, span):
    wide = jnp.concatenate([table, jnp.zeros((TILE, span - table.shape[1]), jnp.float32)], axis=1)
    total = jnp.zeros((8, span), jnp.float32)
    for group in range(TILE // 8):
        total = total + pltpu.roll(wide[8 * group : 8 * group + 8, :], TILE - 1 - 8 * group, 1)
    sums = total[0:1, :]
    for row in range(1, 8):
        sums = sums + pltpu.roll(total[row : row + 1, :], span - row, 1)
    return sums


def attend_head(pair, second, q, keys, values, q_doc, k_doc, table, attended, log_total):
    tokens, count = q.shape[0], keys.shape[0]
    lanes = slice(pair * PAIR, (pair + 1) * PAIR)
    head = 2 * pair + second
    for k in range(tokens // TILE):
        rows = slice(k * TILE, k * TILE + TILE)
        shift = tokens - TILE - k * TILE
        scores = dot_nt(one_head(q[rows, lanes], second), keys[:, lanes]) + table[:, shift : shift + count]
        scores = jnp.where(q_doc[rows, :] == k_doc[...], scores, NEG_LARGE)
        top = jnp.max(scores, axis=1, keepdims=True)
        weights = jnp.exp(scores - top)
        total = jnp.sum(weights, axis=1, keepdims=True)
        part = dot_nn(weights.astype(jnp.bfloat16), values[:, lanes]) * (1.0 / total)
        logs = log_total[rows, :]
        lane = lax.broadcasted_iota(jnp.int32, logs.shape, 1)
        log_total[rows, :] = jnp.where(lane == head, top + jnp.log(total), logs)
        if second:
            attended[rows, lanes] = jnp.where(low_lanes(part.shape), attended[rows, lanes], part)
        else:
            attended[rows, lanes] = part


def pull_scores(pair, second, q, keys, values, q_doc, k_doc, attended, attended_grad, log_total, table, sums, probs, grads, diagonals):
    tokens, count = q.shape[0], keys.shape[0]
    lanes = slice(pair * PAIR, (pair + 1) * PAIR)
    head = 2 * pair + second
    sums[...] = jnp.zeros_like(sums)
    for k in range(tokens // TILE):
        rows = slice(k * TILE, k * TILE + TILE)
        run = slice(tokens - TILE - k * TILE, tokens - TILE - k * TILE + count)
        product = one_head(attended_grad[rows, lanes], second).astype(jnp.float32) * attended[rows, lanes]
        delta = jnp.sum(product, axis=1, keepdims=True)
        logs = log_total[rows, :]
        lane = lax.broadcasted_iota(jnp.int32, logs.shape, 1)
        log = jnp.sum(jnp.where(lane == head, logs, 0.0), axis=1, keepdims=True)
        scores = dot_nt(one_head(q[rows, lanes], second), keys[:, lanes]) + table[:, run]
        weights = jnp.exp(jnp.where(q_doc[rows, :] == k_doc[...], scores - log, NEG_LARGE))
        pulled = dot_nt(one_head(attended_grad[rows, lanes], second), values[:, lanes])
        score_grad = weights * (pulled - delta)
        sums[:, run] += score_grad
        here = slice(second * tokens + k * TILE, second * tokens + k * TILE + TILE)
        probs[here, :] = weights.astype(jnp.bfloat16)
        grads[here, :] = score_grad.astype(jnp.bfloat16)
    diagonals[head : head + 1, :] = diagonal_sums(sums[...], count + tokens)


def pull_pair(pair, q, keys, attended_grad, probs, grads, q_grad):
    tokens = q.shape[0]
    lanes = slice(pair * PAIR, (pair + 1) * PAIR)
    both = lambda rows: jnp.concatenate([one_head(rows, 0), one_head(rows, 1)], axis=0)
    key = keys[:, lanes]
    query_grad = dot_nn(grads[:tokens, :], one_head(key, 0)) + dot_nn(grads[tokens:, :], one_head(key, 1))
    q_grad[:, 3 * pair * PAIR : (3 * pair + 1) * PAIR] = (SCORE_SCALE * query_grad).astype(jnp.bfloat16)
    return (dot_tn(grads[...], both(q[:, lanes])), dot_tn(probs[...], both(attended_grad[:, lanes])))


def documents(lengths, core, tokens, q_doc, k_doc):
    count = k_doc.shape[1]
    queries = core * tokens + lax.broadcasted_iota(jnp.int32, (tokens, 1), 0)
    keys = lax.broadcasted_iota(jnp.int32, (1, count), 1)
    end = jnp.int32(0)
    q_index, k_index = jnp.zeros((tokens, 1), jnp.int32), jnp.zeros((1, count), jnp.int32)
    for n in range(lengths.shape[1]):
        end = end + lengths[0, n]
        q_index = q_index + (queries >= end).astype(jnp.int32)
        k_index = k_index + (keys >= end).astype(jnp.int32)
    q_doc[...] = q_index
    k_doc[...] = k_index


def window_hot(buckets, core, tokens, span, count):
    ids = buckets[:, pl.ds(pl.multiple_of((1 - core) * tokens, 128), span)]
    return (jnp.broadcast_to(ids, (count, span)) == lax.broadcasted_iota(jnp.int32, (count, span), 0)).astype(jnp.float32)


def upright(vector):
    count = vector.shape[0]
    row = jnp.broadcast_to(vector.astype(jnp.float32).reshape(1, count), (count, count))
    same = lax.broadcasted_iota(jnp.int32, (count, count), 0) == lax.broadcasted_iota(jnp.int32, (count, count), 1)
    return jnp.sum(jnp.where(same, row, 0.0), axis=1, keepdims=True)


def flat(column):
    count = column.shape[0]
    same = lax.broadcasted_iota(jnp.int32, (count, count), 0) == lax.broadcasted_iota(jnp.int32, (count, count), 1)
    return jnp.sum(jnp.where(same, jnp.broadcast_to(column, (count, count)), 0.0), axis=0)


BESIDE_IN = (False, False, True, True, True, False, True, False)
BESIDE_OUT = (True, True, True, True, False, False, False, False)


def layer_kernel(
    layer_input, cotangent, lengths, buckets, rel_bias, attn_gain, ffn_gain, qkv_own, out_own, up_own, down_own,
    output_h, tables, grad_input_h, qkv_h, out_h, up_h, down_h, small_h,
    grad_input, qkv_sum, out_sum, up_sum, down_sum, small, qkv, out, up, down, q, keys, values, attended, logs, residual, normed, first, hidden, slope,
    fold_qkv, fold_up, near_qkv, near_out, near_up, window, row_buckets, q_doc, k_doc, table, sums,
    down_part, up_part, attended_grad, qkv_grad, k_near, v_near, diagonals, bias_buf, *rest,
):
    bufs = [rest[7 * n : 7 * n + 7] for n in range(8)]
    ends, gets = rest[56:62], rest[62:68]
    swap_send, swap_recv, kv_send, kv_recv, end_send, end_recv, bias_send, bias_recv, output_sem, table_sem = rest[68:78]
    gather_sems, scatter_sems = rest[78:85], rest[85:94]
    here = Slice()
    core = here.core
    tokens, width = layer_input.shape[1:]
    ff = up_own.shape[1]
    bf16, f32 = jnp.bfloat16, jnp.float32
    barrier = pltpu.get_barrier_semaphore()
    for target in here.everyone():
        pl.semaphore_signal(barrier, inc=1, device_id=target, device_id_type=MESH)
    mine = pl.ds(pl.multiple_of(core * tokens, tokens), tokens)
    theirs = pl.ds(pl.multiple_of((1 - core) * tokens, tokens), tokens)
    shard = 2 * qkv_own.shape[0]
    own_rows = down_own.shape[0]
    trio = 3 * PAIR

    split = ((fold_qkv, near_qkv), (out_own, near_out), (fold_up, near_up))
    swaps = []
    quarter = ff // 4
    gathers = [Gather(here, g, qkv, shard, shard, trio, (0, 2 * g * trio), (0, trio), BESIDE_IN[g], gather_sems) for g in range(3)]
    gathers += [
        Gather(here, 3, out, shard, shard, width // 2, (0, 0), (0, width // 2), BESIDE_IN[3], gather_sems),
        Gather(here, 4, up, shard, shard, quarter, (0, 0), (0, 2 * quarter), BESIDE_IN[4], gather_sems),
        Gather(here, 5, up, shard, shard, quarter, (0, quarter), (0, 2 * quarter), BESIDE_IN[5], gather_sems),
        Gather(here, 6, down, own_rows // 2, 2 * own_rows, width, (0, 0), (own_rows, 0), BESIDE_IN[6], gather_sems),
        Gather(here, 7, down, own_rows // 2, 2 * own_rows, width, (own_rows // 2, 0), (own_rows, 0), BESIDE_IN[7], gather_sems),
    ]

    def fold():
        gain = upright(attn_gain[...])
        for pair in range(PAIRS):
            for part in range(3):
                at = (pair % 2) * 3 * trio + (pair // 2) * trio + part * PAIR
                own = qkv_own[:, part * width + pair * PAIR : part * width + (pair + 1) * PAIR]
                fold_qkv[:, at : at + PAIR] = (own.astype(f32) * gain).astype(bf16)
        fold_up[...] = (up_own[...].astype(f32) * upright(ffn_gain[...])).astype(bf16)
        down[pl.ds(pl.multiple_of((2 * here.chip + core) * own_rows, own_rows), own_rows), :] = down_own[...]

    def enter():
        pl.semaphore_wait(barrier, len(here.everyone()))
        for n, (own, near) in enumerate(split):
            half = near.shape[1]
            other = own.at[:, pl.ds(pl.multiple_of((1 - core) * half, 128), half)]
            swaps.append(remote(other, near, swap_send.at[n], swap_recv.at[n], here.sibling))
            swaps[-1].start()

    def prepare():
        documents(lengths, core, tokens, q_doc, k_doc)
        count = buckets.shape[0]
        row_buckets[:, :count] = buckets[...].reshape(1, count)
        row_buckets[:, count:] = jnp.zeros((1, row_buckets.shape[1] - count), jnp.int32)
        hot = window_hot(row_buckets, core, tokens, window.shape[1], rel_bias.shape[1])
        window[...] = jnp.dot(rel_bias[...], hot, precision=lax.Precision.HIGHEST)
        first[...] = rms_scale(layer_input[0].astype(f32))[0].astype(bf16)

    def assemble(n):
        own, near = split[n]
        half = near.shape[1]
        swaps[n].wait_recv()
        own_half = own[:, pl.ds(pl.multiple_of(core * half, 128), half)].astype(f32)
        near_half = near[...].astype(f32)
        both = [jnp.where(core == 0, own_half, near_half), jnp.where(core == 0, near_half, own_half)]
        block = jnp.concatenate(both, axis=0).astype(bf16)
        rows = pl.ds(pl.multiple_of(here.chip * shard, shard), shard)
        if n == 0:
            for g in range(3):
                qkv[rows, pl.ds(pl.multiple_of((2 * g + core) * trio, 128), trio)] = block[:, g * trio : (g + 1) * trio]
        else:
            (out if n == 1 else up)[rows, pl.ds(pl.multiple_of(core * half, 128), half)] = block

    def line(n):
        gathers[n].line()

    def spread(n, step):
        gathers[n].spread(step)

    def relay_x(n, step):
        gathers[n].relay_x(step)

    def relay_y(n, step):
        gathers[n].relay_y(step)

    def close(n, m):
        gathers[n].close(m)

    def last(n, m):
        gathers[n].last(m)

    def arrive(*numbers):
        for n in numbers:
            gathers[n].arrive()

    def project(*numbers):
        for pair in numbers:
            value = dot_nn(first[...], qkv[:, pair * trio : (pair + 1) * trio]).astype(bf16)
            lanes = slice(pair * PAIR, (pair + 1) * PAIR)
            q[:, lanes] = (value[:, :PAIR].astype(f32) * SCORE_SCALE).astype(bf16)
            for n, ref in enumerate((keys, values)):
                ref[mine, lanes] = value[:, (n + 1) * PAIR : (n + 2) * PAIR]
                at = ref.at[mine, lanes]
                remote(at, at, kv_send.at[0], kv_recv.at[0, pair], here.sibling).start()

    def keep_table(head):
        return pltpu.make_async_copy(table.at[head % 4], tables.at[head], table_sem.at[head % 4])

    def make_table(head):
        if head >= 4:
            keep_table(head - 4).wait()
        table[head % 4] = bias_table(window[head : head + 1, :], window.shape[1])[:, : table.shape[2]]
        keep_table(head).start()

    def take_table(turn):
        return pltpu.make_async_copy(tables.at[turn % HEADS], table.at[turn % 4], table_sem.at[4 + turn % 4])

    def ready_tables(turn):
        if turn == 0:
            for head in range(HEADS - 4, HEADS):
                keep_table(head).wait()
            take_table(0).start()
            take_table(1).start()
        for ahead in (turn + 2, turn + 3):
            if ahead < 2 * HEADS:
                take_table(ahead).start()
        take_table(turn).wait()
        take_table(turn + 1).wait()

    def attend(pair, second):
        lanes = slice(pair * PAIR, (pair + 1) * PAIR)
        if not second:
            ready_tables(2 * pair)
            await_bytes(keys.at[:, lanes], kv_recv.at[0, pair])
        attend_head(pair, second, q, keys, values, q_doc, k_doc, table.at[(2 * pair + second) % 4], attended, logs)

    def mix():
        rounded = attended[...].astype(bf16)
        for n in range(3):
            lanes = slice(256 * n, 256 * n + 256)
            residual[:, lanes] = layer_input[0, :, lanes].astype(f32) + dot_nn(rounded, out[:, lanes])
        normed[...] = rms_scale(residual[...])[0].astype(bf16)

    def hidden_at(lane, count):
        half = ff // 2
        return (pl.ds(lane // half * tokens, tokens), pl.ds(lane % half, count))

    def ascend(*numbers):
        for n in numbers:
            at = hidden_at(256 * n, 256)
            value = dot_nn(normed[...], up[:, 256 * n : 256 * n + 256])
            square = value * value
            bent = jnp.tanh(GELU_SLOPE * value * (1.0 + GELU_CUBE * square))
            hidden[at] = (0.5 * value * (1.0 + bent)).astype(bf16)
            slope[at] = (
                0.5 * (1.0 + bent) + (0.5 * GELU_SLOPE) * value * (1.0 - bent * bent) * (1.0 + (3.0 * GELU_CUBE) * square)
            ).astype(bf16)

    def give(n, src, dst):
        return pltpu.make_async_copy(src, dst, output_sem.at[n])

    def give_output():
        return give(0, normed, output_h)

    def descend():
        for n in range(3):
            lanes = slice(256 * n, 256 * n + 256)
            low, high = dot_nn(hidden[:tokens], down[: ff // 2, lanes]), dot_nn(hidden[tokens:], down[ff // 2 :, lanes])
            normed[:, lanes] = (residual[:, lanes] + low + high).astype(bf16)
        give_output().start()

    def columns(part, half, start, step):
        return lambda c: part.at[:, :, pl.ds(pl.multiple_of(c * step + start, 128), half)]

    half_rows = own_rows // 2
    halves = [lambda c: down_part.at[:, c, pl.ds(0, half_rows), :], lambda c: down_part.at[:, c, pl.ds(half_rows, half_rows), :]]
    halves += [columns(up_part, quarter, 0, 2 * quarter), columns(up_part, quarter, quarter, 2 * quarter)]
    halves += [columns(up_part, width // 2, 3 * width, width // 2)]
    halves += [columns(up_part, trio, 2 * g * trio, trio) for g in range(3)]
    scatters = [Scatter(here, n, halves[n], BESIDE_OUT[n], bufs[n], scatter_sems) for n in range(8)]

    def swap(*numbers):
        for n in numbers:
            scatters[n].swap()

    def swapped(*numbers):
        for n in numbers:
            scatters[n].swapped()

    def merge(n):
        scatters[n].merge()

    def cross(n, m):
        scatters[n].cross(m)

    def turn(n, step):
        scatters[n].turn(step)

    def column(n):
        scatters[n].column()

    def finish(n):
        total = scatters[n].total()
        if n < 2:
            down_sum[n * half_rows : (n + 1) * half_rows, :] = total
            if n == 0:
                give(5, down_sum, down_h).start()
            return
        rows = total.shape[0] // 2
        ends[n - 2][0] = total[:rows]
        ends[n - 2][1] = total[rows:]
        remote(ends[n - 2].at[1 - core], gets[n - 2], end_send.at[0], end_recv.at[n - 2], here.sibling).start()

    def owned(n):
        await_bytes(gets[n - 2], end_recv.at[n - 2])
        own, near = ends[n - 2][core], gets[n - 2][...]
        return (jnp.where(core == 0, own, near), jnp.where(core == 0, near, own))

    def own(n):
        low, high = owned(n)
        if n in (2, 3):
            for start, total in (((n - 2) * quarter, low), (n * quarter, high)):
                up_sum[:, start : start + quarter] = total
        elif n == 4:
            out_sum[:, : width // 2] = low
            out_sum[:, width // 2 :] = high
            give(3, out_sum, out_h).start()
        else:
            for pair, total in ((2 * (n - 5), low), (2 * (n - 5) + 1, high)):
                for part in range(3):
                    lanes = slice(part * width + pair * PAIR, part * width + (pair + 1) * PAIR)
                    qkv_sum[:, lanes] = total[:, part * PAIR : (part + 1) * PAIR]

    def level(n):
        total, weight, gain, dst = ((up_sum, up_own, ffn_gain, up_h), (qkv_sum, qkv_own, attn_gain, qkv_h))[n]
        count = total.shape[0]
        small[1 - n, :, :count] = flat(jnp.sum(total[...] * weight[...].astype(f32), axis=1, keepdims=True)).reshape(1, count)
        total[...] = total[...] * upright(gain[...])
        give((4, 2)[n], total, dst).start()

    def chips(value):
        return value.reshape(CHIPS, value.shape[0] // CHIPS, value.shape[1])

    def pull_down(*numbers):
        for n in numbers:
            part = dot_tn(hidden[hidden_at(4 * own_rows * n, 4 * own_rows)], cotangent[0]).astype(bf16)
            down_part[2 * n : 2 * n + 2] = part.reshape(2, 2, own_rows, width)

    def pull_hidden(*numbers):
        for n in numbers:
            at = hidden_at(256 * n, 256)
            slope[at] = (slope[at].astype(f32) * dot_nt(cotangent[0], down[256 * n : 256 * n + 256, :])).astype(bf16)

    def pull_up(*numbers):
        for n in numbers:
            up_part[:, :, 256 * n : 256 * n + 256] = chips(dot_tn(normed[...], slope[hidden_at(256 * n, 256)]).astype(bf16))

    def pull_normed():
        for n in range(3):
            lanes = slice(256 * n, 256 * n + 256)
            grad_input[:, lanes] = dot_nt(slope[:tokens], up[lanes, : ff // 2]) + dot_nt(slope[tokens:], up[lanes, ff // 2 :])

    def pull_residual():
        grad_input[...] = cotangent[0].astype(f32) + rms_pull(residual[...], grad_input[...])
        normed[...] = grad_input[...].astype(bf16)

    def pull_out():
        up_part[:, :, 3 * width :] = chips(dot_tn(attended[...].astype(bf16), normed[...]).astype(bf16))

    def pull_attended():
        attended_grad[...] = dot_nt(normed[...], out[...]).astype(bf16)

    probs, grads = slope.at[:, pl.ds(0, width)], slope.at[:, pl.ds(width, width)]
    nears = (k_near, v_near)
    chunks = tokens // own_rows

    def part_at(n, half):
        return pl.ds((2 * n + half) * (chunks // 2), chunks // 2)

    def pull(pair):
        ready_tables(HEADS + 2 * pair)
        for second in (0, 1):
            bias = table.at[(HEADS + 2 * pair + second) % 4]
            pull_scores(pair, second, q, keys, values, q_doc, k_doc, attended, attended_grad, logs, bias, sums, probs, grads, diagonals)
        parts = pull_pair(pair, q, keys, attended_grad, probs, grads, qkv_grad)
        lanes = slice(pair * PAIR, (pair + 1) * PAIR)
        for n, (part, near) in enumerate(zip(parts, nears)):
            down_part[n * chunks : (n + 1) * chunks, :, :, lanes] = part.astype(bf16).reshape(chunks, 2, own_rows, PAIR)
            give = down_part.at[part_at(n, 1 - core), :, :, lanes]
            remote(give, near.at[:, :, :, lanes], kv_send.at[0], kv_recv.at[1, pair], here.sibling).start()

    def pull_qkv(*numbers):
        for pair in numbers:
            lanes = slice(pair * PAIR, (pair + 1) * PAIR)
            await_bytes(keys.at[:, lanes], kv_recv.at[1, pair])
            for n, near in enumerate(nears):
                at = slice(pair * trio + (n + 1) * PAIR, pair * trio + (n + 2) * PAIR)
                total = down_part[part_at(n, core), :, :, lanes].astype(f32) + near[:, :, :, lanes].astype(f32)
                qkv_grad[:, at] = total.astype(bf16).reshape(tokens, PAIR)
            at = slice(pair * trio, (pair + 1) * trio)
            up_part[:, :, at] = chips(dot_tn(first[...], qkv_grad[:, at]).astype(bf16))

    def sum_bias():
        hot = window_hot(row_buckets, core, tokens, window.shape[1], rel_bias.shape[1])
        bias_buf[0] = jnp.zeros(bias_buf.shape[1:], f32)
        bias_buf[0, :HEADS, : rel_bias.shape[1]] = lax.dot_general(
            diagonals[...], hot, (((1,), (1,)), ((), ())), precision=lax.Precision.HIGHEST, preferred_element_type=f32
        )

    def pass_bias(n, slot, target):
        remote(bias_buf.at[slot], bias_buf.at[slot + 1], bias_send.at[0], bias_recv.at[n], target).start()

    def add_bias(n, slot):
        await_bytes(bias_buf.at[slot + 1], bias_recv.at[n])
        bias_buf[slot + 2] = bias_buf[slot] + bias_buf[slot + 1]

    def spread_bias():
        bias_buf[7 + here.z] = bias_buf[6]
        for step in (1, 2, 3):
            remote(bias_buf.at[6], bias_buf.at[7 + here.z], bias_send.at[0], bias_recv.at[3], here.to_z(step)).start()

    def total_bias():
        await_bytes(bias_buf.at[pl.ds(0, LINE - 1)], bias_recv.at[3])
        small[2:] = ((bias_buf[7] + bias_buf[8]) + (bias_buf[9] + bias_buf[10]))[:HEADS, :].reshape(HEADS, 1, 128)
        give(6, small, small_h).start()

    def pull_input():
        for n in range(3):
            lanes = slice(256 * n, 256 * n + 256)
            residual[:, lanes] = dot_nt(qkv_grad[...], qkv[lanes, :])
        grad_input[...] = grad_input[...] + rms_pull(layer_input[0].astype(f32), residual[...])
        give(1, grad_input, grad_input_h).start()

    results = ((normed, output_h), (grad_input, grad_input_h), (qkv_sum, qkv_h), (out_sum, out_h), (up_sum, up_h), (down_sum, down_h), (small, small_h))

    def drain():
        for n, (src, dst) in enumerate(results):
            give(n, src, dst).wait()
        for piece in gathers + scatters:
            piece.drain()
        await_bytes(up_sum, end_send.at[0])
        await_bytes(bias_buf.at[pl.ds(0, 6)], bias_send.at[0])
        await_bytes(hidden, kv_send.at[0])
        for copy in swaps:
            copy.wait_send()

    run(
        (fold,), (enter,), (assemble, 0), (line, 0), (spread, 0, 0), (spread, 1, 0), (assemble, 1), (prepare,),
        (make_table, 0), (make_table, 1), (make_table, 2), (spread, 2, 0), (make_table, 3), (spread, 3, 0), (line, 1),
        (line, 2), (make_table, 4), (relay_x, 0, 0), (relay_y, 0, 0), (spread, 0, 1), (line, 3), (make_table, 5),
        (relay_y, 1, 0), (make_table, 6), (spread, 0, 2), (relay_x, 1, 0), (assemble, 2), (spread, 4, 0), (make_table, 7),
        (relay_x, 2, 0), (relay_y, 2, 0), (spread, 0, 3), (make_table, 8), (make_table, 9), (relay_x, 3, 0),
        (make_table, 10), (close, 0, 0), (spread, 1, 2), (relay_x, 0, 1), (spread, 1, 1), (make_table, 11), (relay_x, 0, 2),
        (relay_y, 0, 1), (relay_y, 3, 0), (relay_y, 0, 2), (spread, 1, 3), (close, 1, 0), (spread, 2, 1), (line, 4),
        (relay_x, 4, 0), (relay_x, 0, 3), (spread, 2, 2), (relay_y, 4, 0), (relay_x, 1, 2), (close, 2, 0), (spread, 2, 3),
        (relay_x, 1, 1), (relay_y, 0, 3), (spread, 3, 1), (close, 0, 2), (close, 3, 0), (relay_x, 1, 3), (spread, 3, 2),
        (relay_y, 1, 2), (relay_x, 2, 1), (close, 0, 1), (spread, 3, 3), (relay_x, 2, 2), (relay_y, 1, 1), (relay_x, 2, 3),
        (relay_y, 1, 3), (spread, 4, 1), (close, 0, 3), (relay_y, 2, 1), (relay_x, 3, 1), (line, 5), (relay_x, 3, 2),
        (spread, 4, 2), (close, 4, 0), (arrive, 0), (project, 0), (close, 1, 2), (project, 1), (relay_y, 2, 2),
        (spread, 5, 0), (relay_x, 3, 3), (relay_y, 2, 3), (close, 1, 3), (close, 1, 1), (spread, 4, 3), (last, 2, 0),
        (attend, 0, 0), (relay_x, 4, 1), (relay_y, 3, 2), (last, 3, 0), (relay_y, 3, 1), (attend, 0, 1), (spread, 5, 1),
        (relay_x, 4, 2), (arrive, 1), (project, 2), (project, 3), (close, 2, 2), (relay_y, 3, 3), (relay_y, 4, 1),
        (attend, 1, 0), (line, 6), (spread, 5, 2), (attend, 1, 1), (relay_y, 4, 2), (relay_x, 5, 0), (attend, 2, 0),
        (spread, 5, 3), (close, 3, 2), (attend, 2, 1), (relay_y, 4, 3), (last, 2, 1), (relay_y, 5, 0), (relay_x, 4, 3),
        (last, 4, 0), (relay_x, 5, 1), (attend, 3, 0), (attend, 3, 1), (spread, 6, 1), (arrive, 2), (project, 4),
        (project, 5), (relay_y, 5, 1), (relay_x, 5, 2), (relay_y, 5, 2), (close, 4, 2), (spread, 6, 2), (line, 7),
        (close, 5, 0), (relay_x, 5, 3), (attend, 4, 0), (relay_x, 6, 1), (relay_y, 5, 3), (spread, 6, 3), (attend, 4, 1),
        (last, 3, 1), (last, 4, 1), (attend, 5, 0), (close, 5, 1), (close, 5, 2), (attend, 5, 1), (arrive, 3), (arrive, 4),
        (spread, 6, 0), (spread, 7, 0), (spread, 7, 1), (relay_x, 6, 2), (relay_y, 6, 1), (mix,), (relay_y, 6, 2),
        (close, 5, 3), (ascend, 0, 1, 2), (spread, 7, 2), (ascend, 6, 7, 8), (relay_y, 6, 3), (arrive, 5), (relay_x, 6, 3),
        (ascend, 3, 4, 5), (spread, 7, 3), (relay_y, 6, 0), (relay_x, 6, 0), (ascend, 9, 10, 11), (relay_x, 7, 0),
        (relay_y, 7, 0), (pull_down, 0, 1, 2, 3), (relay_y, 7, 1), (relay_x, 7, 1), (pull_down, 4, 5, 6, 7), (swap, 1),
        (close, 6, 2), (swap, 0), (relay_y, 7, 2), (relay_y, 7, 3), (relay_x, 7, 2), (close, 6, 0), (relay_x, 7, 3),
        (last, 6, 1), (close, 7, 0), (close, 7, 2), (merge, 1), (swapped, 1), (close, 7, 1), (close, 7, 3), (last, 6, 0),
        (merge, 0), (swapped, 0), (cross, 1, 0), (cross, 1, 1), (arrive, 7), (arrive, 6), (pull_hidden, 3, 4, 5, 9, 10, 11),
        (pull_hidden, 0, 1, 2, 6, 7, 8), (cross, 0, 0), (pull_up, 3, 4, 5, 9, 10, 11), (cross, 0, 1), (swap, 3),
        (pull_normed,), (pull_up, 0, 1, 2, 6, 7, 8), (swap, 2), (turn, 1, 0), (turn, 1, 2), (pull_residual,),
        (pull_attended,), (merge, 3), (turn, 0, 0), (turn, 0, 2), (swapped, 3), (pull_out,), (swap, 4), (pull, 0),
        (cross, 3, 0), (column, 1), (cross, 3, 1), (pull, 1), (merge, 2), (swapped, 2), (pull_qkv, 0), (pull, 2),
        (column, 0), (turn, 3, 0), (turn, 3, 2), (pull, 3), (finish, 1), (pull_qkv, 2), (cross, 2, 0), (cross, 2, 1),
        (pull_qkv, 1), (swap, 5), (merge, 4), (column, 3), (pull, 4), (turn, 2, 0), (turn, 2, 2), (pull_qkv, 3),
        (turn, 4, 0), (turn, 4, 2), (swap, 6), (merge, 5), (pull, 5), (turn, 4, 3), (finish, 0), (turn, 4, 1),
        (pull_qkv, 4), (column, 2), (merge, 6), (sum_bias,), (pass_bias, 0, 0, here.sibling), (descend,), (turn, 5, 0),
        (turn, 5, 1), (finish, 3), (turn, 5, 3), (turn, 5, 2), (pull_qkv, 5), (swap, 7), (column, 4),
        (add_bias, 0, 0), (pass_bias, 1, 2, here.to_x), (pull_input,), (turn, 6, 1), (turn, 6, 3), (turn, 6, 0),
        (turn, 6, 2), (merge, 7), (column, 5), (add_bias, 1, 2), (pass_bias, 2, 4, here.to_y), (finish, 2), (column, 6),
        (turn, 7, 2), (turn, 7, 0), (finish, 4), (turn, 7, 3), (turn, 7, 1), (add_bias, 2, 4), (spread_bias,), (finish, 5),
        (column, 7), (finish, 6), (finish, 7), (own, 4), (own, 3), (own, 5), (own, 2), (level, 0), (own, 6), (own, 7), (level, 1),
        (total_bias,), (swapped, 4, 5, 6, 7), (drain,),
    )


def layer(layer_input, cotangent, lengths, buckets, rel_bias, attn_gain, ffn_gain, qkv_own, out_own, up_own, down_own):
    tokens, width = layer_input.shape[1:]
    pieces = lax.axis_size("blk")
    devices = lax.axis_size("row") * pieces
    count = tokens * pieces
    span = count + tokens
    shard, ff = up_own.shape
    own_rows = down_own.shape[0]
    bf16, f32, i32 = jnp.bfloat16, jnp.float32, jnp.int32
    vmem = pl.BlockSpec(memory_space=pltpu.VMEM)
    owns = (qkv_own, out_own, up_own, down_own)
    scratch = [((w.shape[0] * devices, w.shape[1]), bf16) for w in owns]
    scratch += [((tokens, width), bf16), ((count, width), bf16), ((count, width), bf16), ((tokens, width), f32), ((tokens, 128), f32)]
    scratch += [((tokens, width), f32), ((tokens, width), bf16), ((tokens, width), bf16)]
    scratch += [((2 * tokens, ff // 2), bf16)] * 2 + [(qkv_own.shape, bf16), (up_own.shape, bf16)]
    scratch += [((w.shape[0], w.shape[1] // 2), bf16) for w in owns[:3]]
    scratch += [((HEADS, span), f32), ((1, 2 * count), i32), ((tokens, 1), i32), ((1, count), i32)]
    scratch += [((4, TILE, span - TILE), f32), ((TILE, span - TILE), f32)]
    scratch += [((CHIPS, 2, own_rows, width), bf16), ((CHIPS, 2 * shard, ff), bf16)]
    near = (tokens // own_rows // 2, 2, own_rows, width)
    scratch += [((tokens, width), bf16), ((tokens, 3 * width), bf16), (near, bf16), (near, bf16)]
    scratch += [((HEADS, span), f32), ((11, 16, 128), f32)]
    blocks = [(own_rows // 2, width)] * 2 + [(2 * shard, ff // 4)] * 2 + [(2 * shard, width // 2)] + [(2 * shard, 3 * PAIR)] * 3
    for block, beside in zip(blocks, BESIDE_OUT):
        counts = (CHIPS, 2, 1, 1, 4, 4, 3) if beside else (CHIPS, 1, 2, 2, 4, 4, 3)
        scratch += [((n, *block), bf16) for n in counts]
    scratch += [((2, rows // 2, columns), f32) for rows, columns in blocks[2:]]
    scratch += [((rows // 2, columns), f32) for rows, columns in blocks[2:]]
    dma = pltpu.SemaphoreType.DMA
    sems = [dma((3,)), dma((3,)), dma((1,)), dma((2, PAIRS)), dma((1,)), dma((6,)), dma((1,)), dma((4,)), dma((7,)), dma((8,))]
    sems += [dma((8,)), dma((8,)), dma((8, 3)), dma((8, 6)), dma((8, 6)), dma((8, 2)), dma((8,))]
    sems += [dma((8,))] * 5 + [dma((8, 2))] * 3 + [dma((8,))]
    sums = [((tokens, width), f32)] + [(w.shape, f32) for w in owns] + [((2 + HEADS, 1, 128), f32)]
    outs = [((tokens, width), bf16), ((HEADS, TILE, span - TILE), f32)] + sums
    return pl.pallas_call(
        layer_kernel,
        out_shape=[jax.ShapeDtypeStruct(*o) for o in outs],
        in_specs=[vmem, vmem, pl.BlockSpec(memory_space=pltpu.SMEM)] + [vmem] * 8,
        out_specs=[pl.BlockSpec(memory_space=pl.ANY)] * len(outs),
        scratch_shapes=[pltpu.VMEM(*s) for s in sums + scratch] + sems,
        compiler_params=pltpu.CompilerParams(collective_id=0, has_side_effects=True, vmem_limit_bytes=64 * 2**20 - 2**19),
    )(layer_input, cotangent, lengths, buckets, rel_bias, attn_gain, ffn_gain, *owns)


def settle_kernel(small, output, grad_input, qkv, out, up, down, attn_total, ffn_total, bias_total, *results):
    count = attn_total.shape[0]
    attn_total[...] = small[0, :, :count].reshape(count)
    ffn_total[...] = small[1, :, :count].reshape(count)
    bias_total[...] = small[2:].reshape(bias_total.shape[0], 128)[:, : bias_total.shape[1]]
    for result, src in zip(results, (output, grad_input, qkv, out, up, down)):
        result[...] = src[...]


def slice_body(
    layer_input, doc_lengths, buckets, attn_gain, qkv_weight, out_weight, ffn_gain, up_weight, down_weight, rel_bias, cotangent
):
    f32 = jnp.float32
    output, _, grad_input, *sums, small = layer(
        layer_input, cotangent, doc_lengths, buckets, rel_bias, attn_gain, ffn_gain, qkv_weight, out_weight, up_weight, down_weight
    )
    shapes = [(attn_gain.shape, f32), (ffn_gain.shape, f32), (rel_bias.shape, f32)]
    shapes += [(output.shape, jnp.bfloat16)] + [(total.shape, f32) for total in (grad_input, *sums)]
    vmem = pl.BlockSpec(memory_space=pltpu.VMEM)
    attn_total, ffn_total, bias_total, output, grad_input, qkv, out, up, down = pl.pallas_call(
        settle_kernel,
        out_shape=[jax.ShapeDtypeStruct(*s) for s in shapes],
        in_specs=[vmem] * 7,
        out_specs=[vmem] * 9,
        compiler_params=pltpu.CompilerParams(vmem_limit_bytes=63 * 2**20),
    )(small, output, grad_input, *sums)
    return (output[None], grad_input[None], attn_total, qkv, out, ffn_total, up, down, bias_total)


def solution(mesh):
    fits = dict(mesh.shape) == {"row": CHIPS, "blk": 2}
    return jax.shard_map(
        slice_body if fits else body,
        mesh=mesh,
        in_specs=(
            P("row", "blk", None),
            P("row", None),
            P(),
            P(("row", "blk")),
            P(("row", "blk"), None),
            P(("row", "blk"), None),
            P(("row", "blk")),
            P(("row", "blk"), None),
            P(("row", "blk"), None),
            P(),
            P("row", "blk", None),
        ),
        out_specs=(
            P("row", "blk", None),
            P("row", "blk", None),
            P(("row", "blk")),
            P(("row", "blk"), None),
            P(("row", "blk"), None),
            P(("row", "blk")),
            P(("row", "blk"), None),
            P(("row", "blk"), None),
            P(),
        ),
        check_vma=False,
    )
```

```python
import jax
import jax.numpy as jnp
from jax import lax
from jax.experimental import pallas as pl
from jax.experimental.pallas import tpu as pltpu
from jax.sharding import PartitionSpec as P

D = 768
HEADS = 12
HEAD_DIM = 64


EPSILON = 1e-06
SCORE_SCALE = 0.125
NEG_LARGE = -1e30
PRECISE = lax.Precision.HIGHEST


def rms_forward(values, scale_gain):
    inverse = lax.rsqrt(jnp.mean(values * values, axis=-1, keepdims=True) + EPSILON)
    return (values * inverse * scale_gain, inverse)


def rms_backward(values, inverse, scale_gain, incoming):
    scaled = incoming * scale_gain
    gain_grad = jnp.sum(incoming * values * inverse, axis=0)
    value_grad = inverse * scaled - values * inverse**3 * jnp.mean(
        scaled * values, axis=-1, keepdims=True
    )
    return (value_grad, gain_grad)


def smooth_gate(values):
    return jax.nn.gelu(values, approximate=True)


def doc_index(positions, doc_ends):
    return jnp.sum((positions[:, None] >= doc_ends[None, :]).astype(jnp.int32), axis=1)


def block_width(row_count):
    return 512 if row_count % 512 == 0 else row_count


def bucket_hot(buckets, bucket_count, query_first, key_first, query_count, key_count):
    row_length = (buckets.shape[0] + 1) // 2
    span = query_count + key_count - 1
    start_at = key_first - query_first - (query_count - 1) + row_length - 1
    window_ids = lax.dynamic_slice_in_dim(buckets, start_at, span)
    return (window_ids[:, None] == jnp.arange(bucket_count, dtype=jnp.int32)[None, :]).astype(
        jnp.float32
    )


def spread_diagonals(window, query_count, key_count):
    head_count, span = window.shape
    tiled = jnp.broadcast_to(window[:, None, :], (head_count, query_count, span)).reshape(
        head_count, query_count * span
    )
    padded = jnp.pad(tiled, ((0, 0), (0, query_count)))
    grid = padded.reshape(head_count, query_count, span + 1)[:, :, :key_count]
    return grid[:, ::-1, :]


def sum_diagonals(grid):
    head_count, query_count, key_count = grid.shape
    span = query_count + key_count - 1
    flipped = grid[:, ::-1, :]
    padded = jnp.pad(flipped, ((0, 0), (0, 0), (0, span + 1 - key_count)))
    flat = padded.reshape(head_count, query_count * (span + 1))[:, : query_count * span]
    return jnp.sum(flat.reshape(head_count, query_count, span), axis=1)


def block_scores(query_heads, key_heads, query_pos, key_pos, query_doc, key_doc, buckets, rel_bias):
    query_count = query_heads.shape[0]
    key_count = key_heads.shape[0]
    raw_scores = (
        jnp.einsum("qhd,khd->hqk", query_heads, key_heads, preferred_element_type=jnp.float32)
        * SCORE_SCALE
    )
    hot_table = bucket_hot(
        buckets, rel_bias.shape[1], query_pos[0], key_pos[0], query_count, key_count
    )
    window = jnp.dot(rel_bias, hot_table.T, precision=PRECISE)
    scores = raw_scores + spread_diagonals(window, query_count, key_count)
    same_doc = (query_doc[:, None] == key_doc[None, :])[None]
    return (scores, same_doc, hot_table)


def grad_block(
    query_heads,
    dout_heads,
    log_total,
    delta,
    query_pos,
    query_doc,
    key_heads,
    value_heads,
    key_pos,
    key_doc,
    buckets,
    rel_bias,
):
    scores, same_doc, hot_table = block_scores(
        query_heads, key_heads, query_pos, key_pos, query_doc, key_doc, buckets, rel_bias
    )
    probabilities = jnp.where(same_doc, jnp.exp(scores - log_total[..., None]), 0.0)
    prob_grad = jnp.einsum(
        "qhd,khd->hqk", dout_heads, value_heads, preferred_element_type=jnp.float32
    )
    score_grad = (probabilities * (prob_grad - delta[..., None])).astype(jnp.bfloat16)
    query_part = (
        jnp.einsum("hqk,khd->qhd", score_grad, key_heads, preferred_element_type=jnp.float32)
        * SCORE_SCALE
    )
    key_part = (
        jnp.einsum("hqk,qhd->khd", score_grad, query_heads, preferred_element_type=jnp.float32)
        * SCORE_SCALE
    )
    value_part = jnp.einsum(
        "hqk,qhd->khd",
        probabilities.astype(jnp.bfloat16),
        dout_heads,
        preferred_element_type=jnp.float32,
    )
    diagonal_totals = sum_diagonals(score_grad.astype(jnp.float32))
    bias_part = jnp.dot(diagonal_totals, hot_table, precision=PRECISE)
    return (query_part, key_part, value_part, bias_part)


def body(
    layer_input,
    doc_lengths,
    buckets,
    attn_gain,
    qkv_weight,
    out_weight,
    ffn_gain,
    up_weight,
    down_weight,
    rel_bias,
    cotangent,
):
    tokens = layer_input.shape[1]
    my_piece = lax.axis_index("blk")
    positions = my_piece * tokens + jnp.arange(tokens, dtype=jnp.int32)
    doc_ends = jnp.cumsum(doc_lengths[0])
    my_docs = doc_index(positions, doc_ends)
    gathered = (
        lax.all_gather(attn_gain, ("row", "blk"), axis=0, tiled=True),
        lax.all_gather(qkv_weight, ("row", "blk"), axis=0, tiled=True),
        lax.all_gather(out_weight, ("row", "blk"), axis=0, tiled=True),
        lax.all_gather(ffn_gain, ("row", "blk"), axis=0, tiled=True),
        lax.all_gather(up_weight, ("row", "blk"), axis=0, tiled=True),
        lax.all_gather(down_weight, ("row", "blk"), axis=0, tiled=True),
    )
    gain_first, qkv_full, out_full, gain_second, up_full, down_full = gathered
    gain_first = gain_first.astype(jnp.float32)
    gain_second = gain_second.astype(jnp.float32)
    inputs = layer_input[0].astype(jnp.float32)
    normed, inv_attn = rms_forward(inputs, gain_first)
    normed_b = normed.astype(jnp.bfloat16)
    projected = jnp.dot(normed_b, qkv_full, preferred_element_type=jnp.float32).astype(jnp.bfloat16)
    query_proj = projected[:, :D]
    key_proj = projected[:, D : 2 * D]
    value_proj = projected[:, 2 * D :]
    query_heads = query_proj.reshape(tokens, HEADS, HEAD_DIM)
    start_state = (
        jnp.zeros((HEADS, tokens, HEAD_DIM), jnp.float32),
        jnp.full((HEADS, tokens), NEG_LARGE, jnp.float32),
        jnp.zeros((HEADS, tokens), jnp.float32),
    )
    key_piece = lax.all_gather(key_proj, "blk", axis=0, tiled=True)
    value_piece = lax.all_gather(value_proj, "blk", axis=0, tiled=True)
    row_count = key_piece.shape[0]
    attend_block_rows = block_width(row_count)
    block_count = row_count // attend_block_rows
    key_blocks = key_piece.reshape(block_count, attend_block_rows, HEADS, HEAD_DIM)
    value_blocks = value_piece.reshape(block_count, attend_block_rows, HEADS, HEAD_DIM)
    offsets = attend_block_rows * jnp.arange(block_count, dtype=jnp.int32)

    def advance(state_in, block_item):
        weighted, running_max, denominator = state_in
        key_block, value_block, offset = block_item
        key_pos = offset + jnp.arange(attend_block_rows, dtype=jnp.int32)
        scores, same_doc, unused_hot = block_scores(
            query_heads,
            key_block,
            positions,
            key_pos,
            my_docs,
            doc_index(key_pos, doc_ends),
            buckets,
            rel_bias,
        )
        scores = jnp.where(same_doc, scores, NEG_LARGE)
        new_max = jnp.maximum(running_max, jnp.max(scores, axis=2))
        rescale = jnp.exp(running_max - new_max)
        probabilities = jnp.where(same_doc, jnp.exp(scores - new_max[..., None]), 0.0)
        denominator = denominator * rescale + jnp.sum(probabilities, axis=2)
        weighted = weighted * rescale[..., None] + jnp.einsum(
            "hqk,khd->hqd",
            probabilities.astype(jnp.bfloat16),
            value_block,
            preferred_element_type=jnp.float32,
        )
        return ((weighted, new_max, denominator), None)

    state_out, unused_out = lax.scan(advance, start_state, (key_blocks, value_blocks, offsets))
    weighted, running_max, denominator = state_out
    attended = jnp.transpose(weighted / denominator[..., None], (1, 0, 2)).reshape(tokens, D)
    log_total = running_max + jnp.log(denominator)
    attended_b = attended.astype(jnp.bfloat16)
    residual = inputs + jnp.dot(attended_b, out_full, preferred_element_type=jnp.float32)
    normed_ffn, inv_ffn = rms_forward(residual, gain_second)
    normed_ffn_b = normed_ffn.astype(jnp.bfloat16)
    up_proj = jnp.dot(normed_ffn_b, up_full, preferred_element_type=jnp.float32)
    activated, activate_back = jax.vjp(smooth_gate, up_proj)
    hidden = activated.astype(jnp.bfloat16)
    result = residual + jnp.dot(hidden, down_full, preferred_element_type=jnp.float32)
    output = result.astype(jnp.bfloat16)[None]
    qkv_full, out_full, up_full, down_full = (
        lax.all_gather(qkv_weight, ("row", "blk"), axis=0, tiled=True),
        lax.all_gather(out_weight, ("row", "blk"), axis=0, tiled=True),
        lax.all_gather(up_weight, ("row", "blk"), axis=0, tiled=True),
        lax.all_gather(down_weight, ("row", "blk"), axis=0, tiled=True),
    )
    out_grad_b = cotangent[0]
    out_grad = out_grad_b.astype(jnp.float32)
    grad_down = jnp.einsum("tf,td->fd", hidden, out_grad_b, preferred_element_type=jnp.float32)
    hidden_grad = jnp.einsum("td,fd->tf", out_grad_b, down_full, preferred_element_type=jnp.float32)
    up_grad = activate_back(hidden_grad)[0].astype(jnp.bfloat16)
    grad_up = jnp.einsum("td,tf->df", normed_ffn_b, up_grad, preferred_element_type=jnp.float32)
    ffn_norm_grad = jnp.einsum("tf,df->td", up_grad, up_full, preferred_element_type=jnp.float32)
    residual_part, grad_ffn_gain = rms_backward(residual, inv_ffn, gain_second, ffn_norm_grad)
    residual_grad = out_grad + residual_part
    residual_grad_b = residual_grad.astype(jnp.bfloat16)
    grad_out = jnp.einsum(
        "td,te->de", attended_b, residual_grad_b, preferred_element_type=jnp.float32
    )
    attended_grad = jnp.einsum(
        "te,de->td", residual_grad_b, out_full, preferred_element_type=jnp.float32
    ).astype(jnp.bfloat16)
    dout_heads = attended_grad.reshape(tokens, HEADS, HEAD_DIM)
    delta = jnp.einsum(
        "thd,thd->ht", dout_heads.astype(jnp.float32), attended.reshape(tokens, HEADS, HEAD_DIM)
    )
    bias_start = jnp.zeros(rel_bias.shape, jnp.float32)
    all_keys, all_values = (
        lax.all_gather(key_proj, "blk", axis=0, tiled=True),
        lax.all_gather(value_proj, "blk", axis=0, tiled=True),
    )
    row_count = all_keys.shape[0]
    block_rows = block_width(row_count)
    block_count = row_count // block_rows
    offsets = block_rows * jnp.arange(block_count, dtype=jnp.int32)

    def key_step(state_in, block_item):
        query_total, bias_total = state_in
        key_block, value_block, offset = block_item
        key_pos = offset + jnp.arange(block_rows, dtype=jnp.int32)
        query_part, key_part, value_part, bias_part = grad_block(
            query_heads,
            dout_heads,
            log_total,
            delta,
            positions,
            my_docs,
            key_block,
            value_block,
            key_pos,
            doc_index(key_pos, doc_ends),
            buckets,
            rel_bias,
        )
        return ((query_total + query_part, bias_total + bias_part), (key_part, value_part))

    key_start = (jnp.zeros((tokens, HEADS, HEAD_DIM), jnp.float32), bias_start)
    (query_total, bias_total), (key_parts, value_parts) = lax.scan(
        key_step,
        key_start,
        (
            all_keys.reshape(block_count, block_rows, HEADS, HEAD_DIM),
            all_values.reshape(block_count, block_rows, HEADS, HEAD_DIM),
            offsets,
        ),
    )
    key_grad, value_grad = (
        lax.psum_scatter(
            key_parts.reshape(row_count, D).astype(jnp.bfloat16),
            "blk",
            scatter_dimension=0,
            tiled=True,
        ).astype(jnp.float32),
        lax.psum_scatter(
            value_parts.reshape(row_count, D).astype(jnp.bfloat16),
            "blk",
            scatter_dimension=0,
            tiled=True,
        ).astype(jnp.float32),
    )
    query_grad = query_total.reshape(tokens, D)
    qkv_grad = jnp.concatenate([query_grad, key_grad, value_grad], axis=1).astype(jnp.bfloat16)
    grad_qkv = jnp.einsum("td,te->de", normed_b, qkv_grad, preferred_element_type=jnp.float32)
    normed_grad = jnp.einsum("te,de->td", qkv_grad, qkv_full, preferred_element_type=jnp.float32)
    input_part, grad_attn_gain = rms_backward(inputs, inv_attn, gain_first, normed_grad)
    grad_input = (residual_grad + input_part)[None]
    shares = (
        lax.psum_scatter(grad_attn_gain, ("row", "blk"), scatter_dimension=0, tiled=True),
        lax.psum_scatter(grad_qkv, ("row", "blk"), scatter_dimension=0, tiled=True),
        lax.psum_scatter(grad_out, ("row", "blk"), scatter_dimension=0, tiled=True),
        lax.psum_scatter(grad_ffn_gain, ("row", "blk"), scatter_dimension=0, tiled=True),
        lax.psum_scatter(grad_up, ("row", "blk"), scatter_dimension=0, tiled=True),
        lax.psum_scatter(grad_down, ("row", "blk"), scatter_dimension=0, tiled=True),
    )
    attn_share, qkv_share, out_share, ffn_share, up_share, down_share = shares
    bias_grad = lax.psum(bias_total, ("row", "blk"))
    return (
        output,
        grad_input,
        attn_share,
        qkv_share,
        out_share,
        ffn_share,
        up_share,
        down_share,
        bias_grad,
    )


MESH = pl.DeviceIdType.MESH
CHIPS = 16
LINE = 4
HALF = 64
PAIR = 128
TILE = 128
PAIRS = HEADS // 2
GELU_SLOPE = 0.7978845608028654
GELU_CUBE = 0.044715


def rms_scale(values):
    inverse = lax.rsqrt(jnp.mean(values * values, axis=-1, keepdims=True) + EPSILON)
    return (values * inverse, inverse)


def rms_pull(values, scaled):
    inverse = lax.rsqrt(jnp.mean(values * values, axis=-1, keepdims=True) + EPSILON)
    return inverse * scaled - values * inverse**3 * jnp.mean(scaled * values, axis=-1, keepdims=True)


def place():
    row = lax.axis_index("row")
    return (lax.rem(row, 2), lax.rem(lax.div(row, 2), 2), lax.div(row, 4), lax.axis_index("blk"))


def chip_of(x, y, z):
    return (z * 2 + y) * 2 + x


class Slice:
    def __init__(self):
        self.x, self.y, self.z, self.core = place()
        x, y, z, core = self.x, self.y, self.z, self.core
        self.chip = chip_of(x, y, z)
        self.sibling = (self.chip, 1 - core)
        self.to_x = (chip_of(1 - x, y, z), core)
        self.to_y = (chip_of(x, 1 - y, z), core)
        self.beside = z + 1 - 2 * lax.rem(z, 2)
        self.to_beside = (chip_of(x, y, self.beside), core)

    def line(self, step):
        return lax.rem(self.z + step, LINE)

    def to_z(self, step):
        return (chip_of(self.x, self.y, self.line(step)), self.core)

    def everyone(self):
        return [self.sibling, self.to_x, self.to_y] + [self.to_z(step) for step in (1, 2, 3)]


def run(*steps):
    for step, *given in steps:
        step(*given)


def remote(src, dst, send, recv, target):
    return pltpu.make_async_remote_copy(
        src_ref=src, dst_ref=dst, send_sem=send, recv_sem=recv, device_id=target, device_id_type=MESH
    )


def await_bytes(like, sem):
    pltpu.make_async_copy(like, like, sem).wait()


class Gather:
    def __init__(self, here, number, full, rows, pitch, width, start, core_step, beside, sems):
        self.here, self.number, self.full, self.beside = here, number, full, beside
        self.rows, self.pitch, self.width, self.start, self.core_step = rows, pitch, width, start, core_step
        self.sent, self.shared, self.z_recv, self.x_recv, self.y_recv, self.b_recv, self.c_recv = sems

    def block(self, chip):
        row = pl.multiple_of(chip * self.pitch + self.here.core * self.core_step[0] + self.start[0], 16)
        column = pl.multiple_of(self.here.core * self.core_step[1] + self.start[1], 128)
        return self.full.at[pl.ds(row, self.rows), pl.ds(column, self.width)]

    def line(self):
        mine, n = self.block(self.here.chip), self.number
        for step in (1, 2, 3):
            remote(mine, mine, self.sent.at[n], self.z_recv.at[n, step - 1], self.here.to_z(step)).start()

    def column(self, step, x, y):
        return self.block(chip_of(x, y, self.here.line(LINE - step)))

    def share(self, block):
        remote(block, block, self.shared.at[self.number], self.c_recv.at[self.number], self.here.sibling).start()

    def spread(self, step):
        here, n = self.here, self.number
        block = self.column(step, here.x, here.y)
        if step:
            await_bytes(block, self.z_recv.at[n, step - 1])
        remote(block, block, self.sent.at[n], self.x_recv.at[n, step], here.to_x).start()
        remote(block, block, self.sent.at[n], self.y_recv.at[n, step], here.to_y).start()
        self.share(block)

    def steps(self):
        return (0, 2) if self.beside else (0, 1, 2, 3)

    def relay_x(self, step):
        here, n = self.here, self.number
        block = self.column(step, 1 - here.x, here.y)
        await_bytes(block, self.x_recv.at[n, step])
        if step < 2 and step in self.steps():
            remote(block, block, self.sent.at[n], self.y_recv.at[n, 4 + step], here.to_y).start()
        self.share(block)

    def relay_y(self, step):
        here, n = self.here, self.number
        block = self.column(step, here.x, 1 - here.y)
        await_bytes(block, self.y_recv.at[n, step])
        if step >= 2 and step in self.steps():
            remote(block, block, self.sent.at[n], self.x_recv.at[n, 2 + step], here.to_x).start()
        self.share(block)

    def close(self, step):
        here, n = self.here, self.number
        block = self.column(step, 1 - here.x, 1 - here.y)
        await_bytes(block, self.y_recv.at[n, 4 + step] if step < 2 else self.x_recv.at[n, 2 + step])
        if self.beside:
            remote(block, block, self.sent.at[n], self.b_recv.at[n, step // 2], here.to_beside).start()
        self.share(block)

    def last(self, m):
        here, n = self.here, self.number
        block = self.block(chip_of(1 - here.x, 1 - here.y, lax.rem(here.beside + 2 * m, LINE)))
        await_bytes(block, self.b_recv.at[n, m])
        self.share(block)

    def whole(self):
        return self.full.at[pl.ds(0, CHIPS * self.rows), pl.ds(0, self.width)]

    def arrive(self):
        await_bytes(self.whole(), self.c_recv.at[self.number])

    def drain(self):
        n = self.number
        await_bytes(self.full.at[pl.ds(0, (CHIPS - 1) * self.rows), pl.ds(0, self.width)], self.sent.at[n])
        await_bytes(self.whole(), self.shared.at[n])


class Scatter:
    def __init__(self, here, number, half, beside, bufs, sems):
        self.here, self.number, self.half, self.beside = here, number, half, beside
        self.held, self.b_in, self.x_turn, self.y_turn, self.x_in, self.y_in, self.z_in = bufs
        self.sent, self.c_send, self.z_recv, self.x_recv, self.y_recv, self.xt_recv, self.yt_recv, self.b_recv, self.c_recv = sems

    def swap(self):
        n = self.number
        remote(self.half(1 - self.here.core), self.held, self.c_send.at[n], self.c_recv.at[n], self.here.sibling).start()

    def swapped(self):
        await_bytes(self.held, self.c_send.at[self.number])

    def block(self, x, y, z):
        return self.held.at[chip_of(x, y, z)]

    def merge(self):
        here, n = self.here, self.number
        await_bytes(self.held, self.c_recv.at[n])
        mine = self.half(here.core)

        def one(chip, _):
            self.held[chip] = (mine[chip].astype(jnp.float32) + self.held[chip].astype(jnp.float32)).astype(jnp.bfloat16)
            return 0

        lax.fori_loop(0, CHIPS, one, 0, unroll=True)
        if self.beside:
            for m in (0, 1):
                block = self.block(1 - here.x, 1 - here.y, lax.rem(here.beside + 2 * m, LINE))
                remote(block, self.b_in.at[m], self.sent.at[n], self.b_recv.at[n, m], here.to_beside).start()
        else:
            for step in (0, 2, 1, 3):
                self.across(step)
        for step in range(LINE):
            if step >= 2 or step not in self.steps():
                self.to_x(here.line(step))
            if step < 2 or step not in self.steps():
                self.to_y(here.line(step))

    def steps(self):
        return (0, 2) if self.beside else (0, 1, 2, 3)

    def across(self, step):
        here, n = self.here, self.number
        block = self.block(1 - here.x, 1 - here.y, here.line(step))
        if step < 2:
            remote(block, self.y_turn.at[step], self.sent.at[n], self.yt_recv.at[n, step], here.to_y).start()
        else:
            remote(block, self.x_turn.at[step - 2], self.sent.at[n], self.xt_recv.at[n, step - 2], here.to_x).start()

    def to_x(self, z):
        here, n = self.here, self.number
        remote(self.block(1 - here.x, here.y, z), self.x_in.at[z], self.sent.at[n], self.x_recv.at[n], here.to_x).start()

    def to_y(self, z):
        here, n = self.here, self.number
        remote(self.block(here.x, 1 - here.y, z), self.y_in.at[z], self.sent.at[n], self.y_recv.at[n], here.to_y).start()

    def add(self, x, y, z, *terms):
        chip = chip_of(x, y, z)
        total = self.held[chip].astype(jnp.float32)
        for term in terms:
            total = total + term[...].astype(jnp.float32)
        self.held[chip] = total.astype(jnp.bfloat16)

    def cross(self, m):
        here, n = self.here, self.number
        await_bytes(self.b_in.at[m], self.b_recv.at[n, m])
        self.add(1 - here.x, 1 - here.y, here.line(2 * m), self.b_in.at[m])
        self.across(2 * m)

    def turn(self, step):
        here, n = self.here, self.number
        z = here.line(step)
        if step < 2:
            await_bytes(self.y_turn.at[step], self.yt_recv.at[n, step])
            self.add(1 - here.x, here.y, z, self.y_turn.at[step])
            self.to_x(z)
        else:
            await_bytes(self.x_turn.at[step - 2], self.xt_recv.at[n, step - 2])
            self.add(here.x, 1 - here.y, z, self.x_turn.at[step - 2])
            self.to_y(z)

    def column(self):
        here, n = self.here, self.number
        await_bytes(self.x_in, self.x_recv.at[n])
        await_bytes(self.y_in, self.y_recv.at[n])
        for step in (1, 3, 2, 0):
            z = here.line(step)
            self.add(here.x, here.y, z, self.x_in.at[z], self.y_in.at[z])
            if step:
                remote(self.block(here.x, here.y, z), self.z_in.at[step - 1], self.sent.at[n], self.z_recv.at[n], here.to_z(step)).start()

    def total(self):
        here, n = self.here, self.number
        total = self.held[here.chip].astype(jnp.float32)
        await_bytes(self.z_in, self.z_recv.at[n])
        for step in (1, 2, 3):
            total = total + self.z_in[step - 1].astype(jnp.float32)
        return total

    def drain(self):
        await_bytes(self.held.at[pl.ds(0, CHIPS - 1)], self.sent.at[self.number])


def low_lanes(shape):
    return lax.broadcasted_iota(jnp.int32, shape, 1) < HALF


def one_head(block, second):
    low = low_lanes(block.shape)
    return jnp.where(low != bool(second), block, jnp.zeros_like(block))


def dot_nt(a, b):
    return lax.dot_general(a, b, (((1,), (1,)), ((), ())), preferred_element_type=jnp.float32)


def dot_tn(a, b):
    return lax.dot_general(a, b, (((0,), (0,)), ((), ())), preferred_element_type=jnp.float32)


def dot_nn(a, b):
    return jnp.dot(a, b, preferred_element_type=jnp.float32)


def bias_table(window_row, span):
    rows = jnp.broadcast_to(window_row, (TILE, span))
    return pltpu.roll(rows, span - (TILE - 1), 1, stride=1, stride_axis=0)


def diagonal_sums(table, span):
    wide = jnp.concatenate([table, jnp.zeros((TILE, span - table.shape[1]), jnp.float32)], axis=1)
    total = jnp.zeros((8, span), jnp.float32)
    for group in range(TILE // 8):
        total = total + pltpu.roll(wide[8 * group : 8 * group + 8, :], TILE - 1 - 8 * group, 1)
    sums = total[0:1, :]
    for row in range(1, 8):
        sums = sums + pltpu.roll(total[row : row + 1, :], span - row, 1)
    return sums


def attend_head(pair, second, q, keys, values, q_doc, k_doc, table, attended, log_total):
    tokens, count = q.shape[0], keys.shape[0]
    lanes = slice(pair * PAIR, (pair + 1) * PAIR)
    head = 2 * pair + second
    for k in range(tokens // TILE):
        rows = slice(k * TILE, k * TILE + TILE)
        shift = tokens - TILE - k * TILE
        scores = dot_nt(one_head(q[rows, lanes], second), keys[:, lanes]) + table[:, shift : shift + count]
        scores = jnp.where(q_doc[rows, :] == k_doc[...], scores, NEG_LARGE)
        top = jnp.max(scores, axis=1, keepdims=True)
        weights = jnp.exp(scores - top)
        total = jnp.sum(weights, axis=1, keepdims=True)
        part = dot_nn(weights.astype(jnp.bfloat16), values[:, lanes]) * (1.0 / total)
        logs = log_total[rows, :]
        lane = lax.broadcasted_iota(jnp.int32, logs.shape, 1)
        log_total[rows, :] = jnp.where(lane == head, top + jnp.log(total), logs)
        if second:
            attended[rows, lanes] = jnp.where(low_lanes(part.shape), attended[rows, lanes], part)
        else:
            attended[rows, lanes] = part


def pull_scores(pair, second, q, keys, values, q_doc, k_doc, attended, attended_grad, log_total, table, sums, probs, grads, diagonals):
    tokens, count = q.shape[0], keys.shape[0]
    lanes = slice(pair * PAIR, (pair + 1) * PAIR)
    head = 2 * pair + second
    sums[...] = jnp.zeros_like(sums)
    for k in range(tokens // TILE):
        rows = slice(k * TILE, k * TILE + TILE)
        run = slice(tokens - TILE - k * TILE, tokens - TILE - k * TILE + count)
        product = one_head(attended_grad[rows, lanes], second).astype(jnp.float32) * attended[rows, lanes]
        delta = jnp.sum(product, axis=1, keepdims=True)
        logs = log_total[rows, :]
        lane = lax.broadcasted_iota(jnp.int32, logs.shape, 1)
        log = jnp.sum(jnp.where(lane == head, logs, 0.0), axis=1, keepdims=True)
        scores = dot_nt(one_head(q[rows, lanes], second), keys[:, lanes]) + table[:, run]
        weights = jnp.exp(jnp.where(q_doc[rows, :] == k_doc[...], scores - log, NEG_LARGE))
        pulled = dot_nt(one_head(attended_grad[rows, lanes], second), values[:, lanes])
        score_grad = weights * (pulled - delta)
        sums[:, run] += score_grad
        here = slice(second * tokens + k * TILE, second * tokens + k * TILE + TILE)
        probs[here, :] = weights.astype(jnp.bfloat16)
        grads[here, :] = score_grad.astype(jnp.bfloat16)
    diagonals[head : head + 1, :] = diagonal_sums(sums[...], count + tokens)


def pull_pair(pair, q, keys, attended_grad, probs, grads, q_grad):
    tokens = q.shape[0]
    lanes = slice(pair * PAIR, (pair + 1) * PAIR)
    both = lambda rows: jnp.concatenate([one_head(rows, 0), one_head(rows, 1)], axis=0)
    key = keys[:, lanes]
    query_grad = dot_nn(grads[:tokens, :], one_head(key, 0)) + dot_nn(grads[tokens:, :], one_head(key, 1))
    q_grad[:, 3 * pair * PAIR : (3 * pair + 1) * PAIR] = (SCORE_SCALE * query_grad).astype(jnp.bfloat16)
    return (dot_tn(grads[...], both(q[:, lanes])), dot_tn(probs[...], both(attended_grad[:, lanes])))


def documents(lengths, core, tokens, q_doc, k_doc):
    count = k_doc.shape[1]
    queries = core * tokens + lax.broadcasted_iota(jnp.int32, (tokens, 1), 0)
    keys = lax.broadcasted_iota(jnp.int32, (1, count), 1)
    end = jnp.int32(0)
    q_index, k_index = jnp.zeros((tokens, 1), jnp.int32), jnp.zeros((1, count), jnp.int32)
    for n in range(lengths.shape[1]):
        end = end + lengths[0, n]
        q_index = q_index + (queries >= end).astype(jnp.int32)
        k_index = k_index + (keys >= end).astype(jnp.int32)
    q_doc[...] = q_index
    k_doc[...] = k_index


def window_hot(buckets, core, tokens, span, count):
    ids = buckets[:, pl.ds(pl.multiple_of((1 - core) * tokens, 128), span)]
    return (jnp.broadcast_to(ids, (count, span)) == lax.broadcasted_iota(jnp.int32, (count, span), 0)).astype(jnp.float32)


def upright(vector):
    count = vector.shape[0]
    row = jnp.broadcast_to(vector.astype(jnp.float32).reshape(1, count), (count, count))
    same = lax.broadcasted_iota(jnp.int32, (count, count), 0) == lax.broadcasted_iota(jnp.int32, (count, count), 1)
    return jnp.sum(jnp.where(same, row, 0.0), axis=1, keepdims=True)


def flat(column):
    count = column.shape[0]
    same = lax.broadcasted_iota(jnp.int32, (count, count), 0) == lax.broadcasted_iota(jnp.int32, (count, count), 1)
    return jnp.sum(jnp.where(same, jnp.broadcast_to(column, (count, count)), 0.0), axis=0)


BESIDE_IN = (False, False, True, True, True, False, True, False)
BESIDE_OUT = (True, True, True, True, False, False, False, False)


def layer_kernel(
    layer_input, cotangent, lengths, buckets, rel_bias, attn_gain, ffn_gain, qkv_own, out_own, up_own, down_own,
    output_h, tables, grad_input_h, qkv_h, out_h, up_h, down_h, small_h,
    grad_input, qkv_sum, out_sum, up_sum, down_sum, small, qkv, out, up, down, q, keys, values, attended, logs, residual, normed, first, hidden, slope,
    fold_qkv, fold_up, near_qkv, near_out, near_up, window, row_buckets, q_doc, k_doc, table, sums,
    down_part, up_part, attended_grad, qkv_grad, k_near, v_near, diagonals, bias_buf, *rest,
):
    bufs = [rest[7 * n : 7 * n + 7] for n in range(8)]
    ends, gets = rest[56:62], rest[62:68]
    swap_send, swap_recv, kv_send, kv_recv, end_send, end_recv, bias_send, bias_recv, output_sem, table_sem = rest[68:78]
    gather_sems, scatter_sems = rest[78:85], rest[85:94]
    here = Slice()
    core = here.core
    tokens, width = layer_input.shape[1:]
    ff = up_own.shape[1]
    bf16, f32 = jnp.bfloat16, jnp.float32
    barrier = pltpu.get_barrier_semaphore()
    for target in here.everyone():
        pl.semaphore_signal(barrier, inc=1, device_id=target, device_id_type=MESH)
    mine = pl.ds(pl.multiple_of(core * tokens, tokens), tokens)
    theirs = pl.ds(pl.multiple_of((1 - core) * tokens, tokens), tokens)
    shard = 2 * qkv_own.shape[0]
    own_rows = down_own.shape[0]
    trio = 3 * PAIR

    split = ((fold_qkv, near_qkv), (out_own, near_out), (fold_up, near_up))
    swaps = []
    quarter = ff // 4
    gathers = [Gather(here, g, qkv, shard, shard, trio, (0, 2 * g * trio), (0, trio), BESIDE_IN[g], gather_sems) for g in range(3)]
    gathers += [
        Gather(here, 3, out, shard, shard, width // 2, (0, 0), (0, width // 2), BESIDE_IN[3], gather_sems),
        Gather(here, 4, up, shard, shard, quarter, (0, 0), (0, 2 * quarter), BESIDE_IN[4], gather_sems),
        Gather(here, 5, up, shard, shard, quarter, (0, quarter), (0, 2 * quarter), BESIDE_IN[5], gather_sems),
        Gather(here, 6, down, own_rows // 2, 2 * own_rows, width, (0, 0), (own_rows, 0), BESIDE_IN[6], gather_sems),
        Gather(here, 7, down, own_rows // 2, 2 * own_rows, width, (own_rows // 2, 0), (own_rows, 0), BESIDE_IN[7], gather_sems),
    ]

    def fold():
        gain = upright(attn_gain[...])
        for pair in range(PAIRS):
            for part in range(3):
                at = (pair % 2) * 3 * trio + (pair // 2) * trio + part * PAIR
                own = qkv_own[:, part * width + pair * PAIR : part * width + (pair + 1) * PAIR]
                fold_qkv[:, at : at + PAIR] = (own.astype(f32) * gain).astype(bf16)
        fold_up[...] = (up_own[...].astype(f32) * upright(ffn_gain[...])).astype(bf16)
        down[pl.ds(pl.multiple_of((2 * here.chip + core) * own_rows, own_rows), own_rows), :] = down_own[...]

    def enter():
        pl.semaphore_wait(barrier, len(here.everyone()))
        for n, (own, near) in enumerate(split):
            half = near.shape[1]
            other = own.at[:, pl.ds(pl.multiple_of((1 - core) * half, 128), half)]
            swaps.append(remote(other, near, swap_send.at[n], swap_recv.at[n], here.sibling))
            swaps[-1].start()

    def prepare():
        documents(lengths, core, tokens, q_doc, k_doc)
        count = buckets.shape[0]
        row_buckets[:, :count] = buckets[...].reshape(1, count)
        row_buckets[:, count:] = jnp.zeros((1, row_buckets.shape[1] - count), jnp.int32)
        hot = window_hot(row_buckets, core, tokens, window.shape[1], rel_bias.shape[1])
        window[...] = jnp.dot(rel_bias[...], hot, precision=lax.Precision.HIGHEST)
        first[...] = rms_scale(layer_input[0].astype(f32))[0].astype(bf16)

    def assemble(n):
        own, near = split[n]
        half = near.shape[1]
        swaps[n].wait_recv()
        own_half = own[:, pl.ds(pl.multiple_of(core * half, 128), half)].astype(f32)
        near_half = near[...].astype(f32)
        both = [jnp.where(core == 0, own_half, near_half), jnp.where(core == 0, near_half, own_half)]
        block = jnp.concatenate(both, axis=0).astype(bf16)
        rows = pl.ds(pl.multiple_of(here.chip * shard, shard), shard)
        if n == 0:
            for g in range(3):
                qkv[rows, pl.ds(pl.multiple_of((2 * g + core) * trio, 128), trio)] = block[:, g * trio : (g + 1) * trio]
        else:
            (out if n == 1 else up)[rows, pl.ds(pl.multiple_of(core * half, 128), half)] = block

    def line(n):
        gathers[n].line()

    def spread(n, step):
        gathers[n].spread(step)

    def relay_x(n, step):
        gathers[n].relay_x(step)

    def relay_y(n, step):
        gathers[n].relay_y(step)

    def close(n, m):
        gathers[n].close(m)

    def last(n, m):
        gathers[n].last(m)

    def arrive(*numbers):
        for n in numbers:
            gathers[n].arrive()

    def project(*numbers):
        for pair in numbers:
            value = dot_nn(first[...], qkv[:, pair * trio : (pair + 1) * trio]).astype(bf16)
            lanes = slice(pair * PAIR, (pair + 1) * PAIR)
            q[:, lanes] = (value[:, :PAIR].astype(f32) * SCORE_SCALE).astype(bf16)
            for n, ref in enumerate((keys, values)):
                ref[mine, lanes] = value[:, (n + 1) * PAIR : (n + 2) * PAIR]
                at = ref.at[mine, lanes]
                remote(at, at, kv_send.at[0], kv_recv.at[0, pair], here.sibling).start()

    def keep_table(head):
        return pltpu.make_async_copy(table.at[head % 4], tables.at[head], table_sem.at[head % 4])

    def make_table(head):
        if head >= 4:
            keep_table(head - 4).wait()
        table[head % 4] = bias_table(window[head : head + 1, :], window.shape[1])[:, : table.shape[2]]
        keep_table(head).start()

    def take_table(turn):
        return pltpu.make_async_copy(tables.at[turn % HEADS], table.at[turn % 4], table_sem.at[4 + turn % 4])

    def first_tables():
        for head in range(HEADS - 4, HEADS):
            keep_table(head).wait()
        take_table(0).start()
        take_table(1).start()

    def ready_tables(turn):
        for ahead in (turn + 2, turn + 3):
            if ahead < 2 * HEADS:
                take_table(ahead).start()
        take_table(turn).wait()
        take_table(turn + 1).wait()

    def attend(pair, second):
        lanes = slice(pair * PAIR, (pair + 1) * PAIR)
        if not second:
            ready_tables(2 * pair)
            await_bytes(keys.at[:, lanes], kv_recv.at[0, pair])
        attend_head(pair, second, q, keys, values, q_doc, k_doc, table.at[(2 * pair + second) % 4], attended, logs)

    def mix():
        rounded = attended[...].astype(bf16)
        for n in range(3):
            lanes = slice(256 * n, 256 * n + 256)
            residual[:, lanes] = layer_input[0, :, lanes].astype(f32) + dot_nn(rounded, out[:, lanes])
        normed[...] = rms_scale(residual[...])[0].astype(bf16)

    def hidden_at(lane, count):
        half = ff // 2
        return (pl.ds(lane // half * tokens, tokens), pl.ds(lane % half, count))

    def ascend(*numbers):
        for n in numbers:
            at = hidden_at(256 * n, 256)
            value = dot_nn(normed[...], up[:, 256 * n : 256 * n + 256])
            square = value * value
            bent = jnp.tanh(GELU_SLOPE * value * (1.0 + GELU_CUBE * square))
            hidden[at] = (0.5 * value * (1.0 + bent)).astype(bf16)
            slope[at] = (
                0.5 * (1.0 + bent) + (0.5 * GELU_SLOPE) * value * (1.0 - bent * bent) * (1.0 + (3.0 * GELU_CUBE) * square)
            ).astype(bf16)

    def give(n, src, dst):
        return pltpu.make_async_copy(src, dst, output_sem.at[n])

    def give_output():
        return give(0, normed, output_h)

    def descend():
        for n in range(3):
            lanes = slice(256 * n, 256 * n + 256)
            low, high = dot_nn(hidden[:tokens], down[: ff // 2, lanes]), dot_nn(hidden[tokens:], down[ff // 2 :, lanes])
            normed[:, lanes] = (residual[:, lanes] + low + high).astype(bf16)
        give_output().start()

    def columns(part, half, start, step):
        return lambda c: part.at[:, :, pl.ds(pl.multiple_of(c * step + start, 128), half)]

    half_rows = own_rows // 2
    halves = [lambda c: down_part.at[:, c, pl.ds(0, half_rows), :], lambda c: down_part.at[:, c, pl.ds(half_rows, half_rows), :]]
    halves += [columns(up_part, quarter, 0, 2 * quarter), columns(up_part, quarter, quarter, 2 * quarter)]
    halves += [columns(up_part, width // 2, 3 * width, width // 2)]
    halves += [columns(up_part, trio, 2 * g * trio, trio) for g in range(3)]
    scatters = [Scatter(here, n, halves[n], BESIDE_OUT[n], bufs[n], scatter_sems) for n in range(8)]

    def swap(*numbers):
        for n in numbers:
            scatters[n].swap()

    def swapped(*numbers):
        for n in numbers:
            scatters[n].swapped()

    def merge(n):
        scatters[n].merge()

    def cross(n, m):
        scatters[n].cross(m)

    def turn(n, step):
        scatters[n].turn(step)

    def column(n):
        scatters[n].column()

    def finish(n):
        total = scatters[n].total()
        if n < 2:
            down_sum[n * half_rows : (n + 1) * half_rows, :] = total
            if n == 0:
                give(5, down_sum, down_h).start()
            return
        rows = total.shape[0] // 2
        ends[n - 2][0] = total[:rows]
        ends[n - 2][1] = total[rows:]
        remote(ends[n - 2].at[1 - core], gets[n - 2], end_send.at[0], end_recv.at[n - 2], here.sibling).start()

    def owned(n):
        await_bytes(gets[n - 2], end_recv.at[n - 2])
        own, near = ends[n - 2][core], gets[n - 2][...]
        return (jnp.where(core == 0, own, near), jnp.where(core == 0, near, own))

    def own(n):
        low, high = owned(n)
        if n in (2, 3):
            for start, total in (((n - 2) * quarter, low), (n * quarter, high)):
                up_sum[:, start : start + quarter] = total
        elif n == 4:
            out_sum[:, : width // 2] = low
            out_sum[:, width // 2 :] = high
            give(3, out_sum, out_h).start()
        else:
            for pair, total in ((2 * (n - 5), low), (2 * (n - 5) + 1, high)):
                for part in range(3):
                    lanes = slice(part * width + pair * PAIR, part * width + (pair + 1) * PAIR)
                    qkv_sum[:, lanes] = total[:, part * PAIR : (part + 1) * PAIR]

    def level(n):
        total, weight, gain, dst = ((up_sum, up_own, ffn_gain, up_h), (qkv_sum, qkv_own, attn_gain, qkv_h))[n]
        count = total.shape[0]
        small[1 - n, :, :count] = flat(jnp.sum(total[...] * weight[...].astype(f32), axis=1, keepdims=True)).reshape(1, count)
        total[...] = total[...] * upright(gain[...])
        give((4, 2)[n], total, dst).start()

    def chips(value):
        return value.reshape(CHIPS, value.shape[0] // CHIPS, value.shape[1])

    def pull_down(*numbers):
        for n in numbers:
            part = dot_tn(hidden[hidden_at(4 * own_rows * n, 4 * own_rows)], cotangent[0]).astype(bf16)
            down_part[2 * n : 2 * n + 2] = part.reshape(2, 2, own_rows, width)

    def pull_hidden(*numbers):
        for n in numbers:
            at = hidden_at(256 * n, 256)
            slope[at] = (slope[at].astype(f32) * dot_nt(cotangent[0], down[256 * n : 256 * n + 256, :])).astype(bf16)

    def pull_up(*numbers):
        for n in numbers:
            up_part[:, :, 256 * n : 256 * n + 256] = chips(dot_tn(normed[...], slope[hidden_at(256 * n, 256)]).astype(bf16))

    def pull_normed():
        for n in range(3):
            lanes = slice(256 * n, 256 * n + 256)
            grad_input[:, lanes] = dot_nt(slope[:tokens], up[lanes, : ff // 2]) + dot_nt(slope[tokens:], up[lanes, ff // 2 :])

    def pull_residual():
        grad_input[...] = cotangent[0].astype(f32) + rms_pull(residual[...], grad_input[...])
        normed[...] = grad_input[...].astype(bf16)

    def pull_out():
        up_part[:, :, 3 * width :] = chips(dot_tn(attended[...].astype(bf16), normed[...]).astype(bf16))

    def pull_attended():
        attended_grad[...] = dot_nt(normed[...], out[...]).astype(bf16)

    probs, grads = slope.at[:, pl.ds(0, width)], slope.at[:, pl.ds(width, width)]
    nears = (k_near, v_near)
    chunks = tokens // own_rows

    def part_at(n, half):
        return pl.ds((2 * n + half) * (chunks // 2), chunks // 2)

    def pull(pair):
        ready_tables(HEADS + 2 * pair)
        for second in (0, 1):
            bias = table.at[(HEADS + 2 * pair + second) % 4]
            pull_scores(pair, second, q, keys, values, q_doc, k_doc, attended, attended_grad, logs, bias, sums, probs, grads, diagonals)
        parts = pull_pair(pair, q, keys, attended_grad, probs, grads, qkv_grad)
        lanes = slice(pair * PAIR, (pair + 1) * PAIR)
        for n, (part, near) in enumerate(zip(parts, nears)):
            down_part[n * chunks : (n + 1) * chunks, :, :, lanes] = part.astype(bf16).reshape(chunks, 2, own_rows, PAIR)
            give = down_part.at[part_at(n, 1 - core), :, :, lanes]
            remote(give, near.at[:, :, :, lanes], kv_send.at[0], kv_recv.at[1, pair], here.sibling).start()

    def pull_qkv(*numbers):
        for pair in numbers:
            lanes = slice(pair * PAIR, (pair + 1) * PAIR)
            await_bytes(keys.at[:, lanes], kv_recv.at[1, pair])
            for n, near in enumerate(nears):
                at = slice(pair * trio + (n + 1) * PAIR, pair * trio + (n + 2) * PAIR)
                total = down_part[part_at(n, core), :, :, lanes].astype(f32) + near[:, :, :, lanes].astype(f32)
                qkv_grad[:, at] = total.astype(bf16).reshape(tokens, PAIR)
            at = slice(pair * trio, (pair + 1) * trio)
            up_part[:, :, at] = chips(dot_tn(first[...], qkv_grad[:, at]).astype(bf16))

    def sum_bias():
        hot = window_hot(row_buckets, core, tokens, window.shape[1], rel_bias.shape[1])
        bias_buf[0] = jnp.zeros(bias_buf.shape[1:], f32)
        bias_buf[0, :HEADS, : rel_bias.shape[1]] = lax.dot_general(
            diagonals[...], hot, (((1,), (1,)), ((), ())), precision=lax.Precision.HIGHEST, preferred_element_type=f32
        )

    def pass_bias(n, slot, target):
        remote(bias_buf.at[slot], bias_buf.at[slot + 1], bias_send.at[0], bias_recv.at[n], target).start()

    def add_bias(n, slot):
        await_bytes(bias_buf.at[slot + 1], bias_recv.at[n])
        bias_buf[slot + 2] = bias_buf[slot] + bias_buf[slot + 1]

    def spread_bias():
        bias_buf[7 + here.z] = bias_buf[6]
        for step in (1, 2, 3):
            remote(bias_buf.at[6], bias_buf.at[7 + here.z], bias_send.at[0], bias_recv.at[3], here.to_z(step)).start()

    def total_bias():
        await_bytes(bias_buf.at[pl.ds(0, LINE - 1)], bias_recv.at[3])
        small[2:] = ((bias_buf[7] + bias_buf[8]) + (bias_buf[9] + bias_buf[10]))[:HEADS, :].reshape(HEADS, 1, 128)
        give(6, small, small_h).start()

    def pull_input():
        for n in range(3):
            lanes = slice(256 * n, 256 * n + 256)
            residual[:, lanes] = dot_nt(qkv_grad[...], qkv[lanes, :])
        grad_input[...] = grad_input[...] + rms_pull(layer_input[0].astype(f32), residual[...])
        give(1, grad_input, grad_input_h).start()

    results = ((normed, output_h), (grad_input, grad_input_h), (qkv_sum, qkv_h), (out_sum, out_h), (up_sum, up_h), (down_sum, down_h), (small, small_h))

    def drain():
        for n, (src, dst) in enumerate(results):
            give(n, src, dst).wait()
        for piece in gathers + scatters:
            piece.drain()
        await_bytes(up_sum, end_send.at[0])
        await_bytes(bias_buf.at[pl.ds(0, 6)], bias_send.at[0])
        await_bytes(hidden, kv_send.at[0])
        for copy in swaps:
            copy.wait_send()

    run(
        (fold,), (enter,), (spread, 6, 0), (assemble, 0), (spread, 0, 0), (line, 0), (line, 1), (spread, 1, 0),
        (assemble, 2), (prepare,), (assemble, 1), (spread, 2, 0), (spread, 3, 0), (spread, 4, 0), (line, 2), (line, 3),
        (spread, 0, 1), (relay_x, 0, 0), (spread, 0, 3), (spread, 0, 2), (make_table, 0), (make_table, 1), (spread, 1, 1),
        (make_table, 2), (make_table, 3), (make_table, 4), (relay_x, 1, 0), (relay_x, 0, 1), (spread, 1, 2),
        (make_table, 5), (make_table, 6), (make_table, 7), (relay_y, 0, 3), (relay_y, 0, 2), (spread, 1, 3), (spread, 2, 2),
        (line, 4), (relay_y, 0, 1), (spread, 2, 1), (close, 0, 0), (relay_y, 0, 0), (relay_x, 1, 1), (close, 0, 1),
        (relay_x, 1, 2), (close, 0, 3), (relay_x, 3, 0), (make_table, 8), (relay_x, 0, 2), (make_table, 9), (relay_y, 1, 0),
        (relay_x, 0, 3), (close, 0, 2), (relay_y, 1, 2), (relay_y, 1, 3), (make_table, 10), (relay_x, 2, 2),
        (relay_y, 4, 0), (relay_y, 2, 2), (relay_x, 2, 0), (spread, 3, 2), (arrive, 0), (project, 0), (spread, 3, 3),
        (relay_y, 3, 0), (project, 1), (relay_y, 1, 1), (spread, 2, 3), (make_table, 11), (first_tables,), (spread, 3, 1),
        (relay_x, 1, 3), (close, 2, 2), (close, 1, 1), (close, 1, 3), (close, 1, 2), (relay_y, 3, 2), (close, 1, 0),
        (close, 2, 0), (line, 5), (spread, 4, 1), (relay_y, 2, 0), (attend, 0, 0), (spread, 4, 2), (relay_x, 4, 0),
        (spread, 5, 0), (attend, 0, 1), (relay_y, 2, 3), (arrive, 1), (relay_x, 2, 3), (close, 3, 2), (close, 3, 0),
        (last, 2, 0), (project, 3), (project, 2), (attend, 1, 0), (relay_y, 4, 2), (relay_y, 2, 1), (last, 2, 1),
        (spread, 4, 3), (attend, 1, 1), (relay_x, 3, 2), (relay_x, 2, 1), (relay_y, 3, 1), (spread, 5, 1), (attend, 2, 0),
        (close, 4, 0), (relay_y, 3, 3), (attend, 2, 1), (close, 4, 2), (spread, 5, 2), (relay_x, 4, 1), (relay_y, 5, 0),
        (relay_x, 3, 1), (arrive, 2), (project, 5), (line, 6), (project, 4), (relay_y, 4, 3), (spread, 5, 3),
        (attend, 3, 0), (last, 4, 0), (last, 3, 0), (relay_x, 5, 0), (attend, 3, 1), (relay_x, 4, 2), (last, 3, 1),
        (relay_x, 5, 1), (relay_x, 3, 3), (relay_x, 4, 3), (relay_y, 5, 1), (relay_y, 5, 2), (line, 7), (relay_y, 4, 1),
        (attend, 4, 0), (relay_y, 5, 3), (spread, 7, 0), (attend, 4, 1), (last, 4, 1), (spread, 6, 1), (attend, 5, 0),
        (relay_x, 5, 2), (attend, 5, 1), (relay_x, 5, 3), (spread, 6, 2), (close, 5, 2), (close, 5, 1), (close, 5, 0),
        (arrive, 3), (mix,), (spread, 6, 3), (arrive, 4), (close, 5, 3), (ascend, 0, 1, 2), (relay_x, 6, 0),
        (ascend, 6, 7, 8), (relay_y, 7, 0), (relay_y, 6, 0), (relay_y, 6, 1), (spread, 7, 1), (arrive, 5),
        (ascend, 9, 10, 11), (relay_y, 6, 2), (pull_down, 4, 5, 6, 7), (spread, 7, 2), (ascend, 3, 4, 5), (relay_x, 6, 3),
        (spread, 7, 3), (close, 6, 0), (relay_x, 6, 1), (relay_x, 7, 0), (relay_x, 7, 1), (relay_x, 6, 2),
        (pull_down, 0, 1, 2, 3), (swap, 0), (close, 6, 2), (relay_y, 7, 2), (last, 6, 0), (relay_y, 7, 3), (relay_y, 7, 1),
        (relay_x, 7, 2), (last, 6, 1), (relay_x, 7, 3), (close, 7, 2), (close, 7, 0), (relay_y, 6, 3), (merge, 0),
        (swapped, 0), (close, 7, 1), (close, 7, 3), (swap, 1), (arrive, 7), (arrive, 6), (pull_hidden, 3, 4, 5, 9, 10, 11),
        (cross, 0, 1), (cross, 0, 0), (pull_up, 3, 4, 5, 9, 10, 11), (swap, 3), (merge, 1), (pull_hidden, 0, 1, 2, 6, 7, 8),
        (pull_normed,), (turn, 0, 0), (turn, 0, 2), (pull_up, 0, 1, 2, 6, 7, 8), (swap, 2), (pull_residual,), (cross, 1, 1),
        (cross, 1, 0), (merge, 3), (swapped, 1), (swapped, 3), (pull_out,), (pull_attended,), (column, 0), (pull, 0),
        (turn, 1, 0), (turn, 1, 2), (cross, 3, 1), (cross, 3, 0), (swap, 4), (merge, 2), (swapped, 2), (pull, 1), (pull, 2),
        (column, 1), (turn, 3, 2), (turn, 3, 0), (pull, 3), (cross, 2, 1), (cross, 2, 0), (pull_qkv, 2), (pull_qkv, 0),
        (merge, 4), (pull_qkv, 1), (pull_qkv, 3), (column, 3), (swap, 6), (pull, 4), (turn, 2, 0), (turn, 2, 2),
        (turn, 4, 0), (turn, 4, 2), (swap, 5), (turn, 4, 3), (turn, 4, 1), (pull, 5), (merge, 6), (column, 2),
        (pull_qkv, 4), (finish, 3), (merge, 5), (turn, 6, 2), (pull_qkv, 5), (finish, 1), (swap, 7), (turn, 6, 0),
        (column, 4), (turn, 6, 1), (finish, 0), (turn, 6, 3), (descend,), (turn, 5, 0), (turn, 5, 1), (turn, 5, 2),
        (sum_bias,), (pass_bias, 0, 0, here.sibling), (turn, 5, 3), (merge, 7), (column, 6), (turn, 7, 0), (turn, 7, 2),
        (column, 5), (turn, 7, 1), (turn, 7, 3), (add_bias, 0, 0), (pass_bias, 1, 2, here.to_x), (finish, 2), (column, 7),
        (finish, 6), (finish, 5), (add_bias, 1, 2), (pass_bias, 2, 4, here.to_y), (pull_input,),
        (add_bias, 2, 4), (spread_bias,), (finish, 4), (finish, 7), (own, 4), (own, 3), (own, 6), (own, 5), (own, 2), (level, 0),
        (own, 7), (level, 1),
        (total_bias,), (swapped, 4, 5, 6, 7), (drain,),
    )


def layer(layer_input, cotangent, lengths, buckets, rel_bias, attn_gain, ffn_gain, qkv_own, out_own, up_own, down_own):
    tokens, width = layer_input.shape[1:]
    pieces = lax.axis_size("blk")
    devices = lax.axis_size("row") * pieces
    count = tokens * pieces
    span = count + tokens
    shard, ff = up_own.shape
    own_rows = down_own.shape[0]
    bf16, f32, i32 = jnp.bfloat16, jnp.float32, jnp.int32
    vmem = pl.BlockSpec(memory_space=pltpu.VMEM)
    owns = (qkv_own, out_own, up_own, down_own)
    scratch = [((w.shape[0] * devices, w.shape[1]), bf16) for w in owns]
    scratch += [((tokens, width), bf16), ((count, width), bf16), ((count, width), bf16), ((tokens, width), f32), ((tokens, 128), f32)]
    scratch += [((tokens, width), f32), ((tokens, width), bf16), ((tokens, width), bf16)]
    scratch += [((2 * tokens, ff // 2), bf16)] * 2 + [(qkv_own.shape, bf16), (up_own.shape, bf16)]
    scratch += [((w.shape[0], w.shape[1] // 2), bf16) for w in owns[:3]]
    scratch += [((HEADS, span), f32), ((1, 2 * count), i32), ((tokens, 1), i32), ((1, count), i32)]
    scratch += [((4, TILE, span - TILE), f32), ((TILE, span - TILE), f32)]
    scratch += [((CHIPS, 2, own_rows, width), bf16), ((CHIPS, 2 * shard, ff), bf16)]
    near = (tokens // own_rows // 2, 2, own_rows, width)
    scratch += [((tokens, width), bf16), ((tokens, 3 * width), bf16), (near, bf16), (near, bf16)]
    scratch += [((HEADS, span), f32), ((11, 16, 128), f32)]
    blocks = [(own_rows // 2, width)] * 2 + [(2 * shard, ff // 4)] * 2 + [(2 * shard, width // 2)] + [(2 * shard, 3 * PAIR)] * 3
    for block, beside in zip(blocks, BESIDE_OUT):
        counts = (CHIPS, 2, 1, 1, 4, 4, 3) if beside else (CHIPS, 1, 2, 2, 4, 4, 3)
        scratch += [((n, *block), bf16) for n in counts]
    scratch += [((2, rows // 2, columns), f32) for rows, columns in blocks[2:]]
    scratch += [((rows // 2, columns), f32) for rows, columns in blocks[2:]]
    dma = pltpu.SemaphoreType.DMA
    sems = [dma((3,)), dma((3,)), dma((1,)), dma((2, PAIRS)), dma((1,)), dma((6,)), dma((1,)), dma((4,)), dma((7,)), dma((8,))]
    sems += [dma((8,)), dma((8,)), dma((8, 3)), dma((8, 6)), dma((8, 6)), dma((8, 2)), dma((8,))]
    sems += [dma((8,))] * 5 + [dma((8, 2))] * 3 + [dma((8,))]
    sums = [((tokens, width), f32)] + [(w.shape, f32) for w in owns] + [((2 + HEADS, 1, 128), f32)]
    outs = [((tokens, width), bf16), ((HEADS, TILE, span - TILE), f32)] + sums
    return pl.pallas_call(
        layer_kernel,
        out_shape=[jax.ShapeDtypeStruct(*o) for o in outs],
        in_specs=[vmem, vmem, pl.BlockSpec(memory_space=pltpu.SMEM)] + [vmem] * 8,
        out_specs=[pl.BlockSpec(memory_space=pl.ANY)] * len(outs),
        scratch_shapes=[pltpu.VMEM(*s) for s in sums + scratch] + sems,
        compiler_params=pltpu.CompilerParams(collective_id=0, has_side_effects=True, vmem_limit_bytes=64 * 2**20 - 2**19),
    )(layer_input, cotangent, lengths, buckets, rel_bias, attn_gain, ffn_gain, *owns)


def settle_kernel(small, output, grad_input, qkv, out, up, down, attn_total, ffn_total, bias_total, *results):
    count = attn_total.shape[0]
    attn_total[...] = small[0, :, :count].reshape(count)
    ffn_total[...] = small[1, :, :count].reshape(count)
    bias_total[...] = small[2:].reshape(bias_total.shape[0], 128)[:, : bias_total.shape[1]]
    for result, src in zip(results, (output, grad_input, qkv, out, up, down)):
        result[...] = src[...]


def slice_body(
    layer_input, doc_lengths, buckets, attn_gain, qkv_weight, out_weight, ffn_gain, up_weight, down_weight, rel_bias, cotangent
):
    f32 = jnp.float32
    output, _, grad_input, *sums, small = layer(
        layer_input, cotangent, doc_lengths, buckets, rel_bias, attn_gain, ffn_gain, qkv_weight, out_weight, up_weight, down_weight
    )
    shapes = [(attn_gain.shape, f32), (ffn_gain.shape, f32), (rel_bias.shape, f32)]
    shapes += [(output.shape, jnp.bfloat16)] + [(total.shape, f32) for total in (grad_input, *sums)]
    vmem = pl.BlockSpec(memory_space=pltpu.VMEM)
    attn_total, ffn_total, bias_total, output, grad_input, qkv, out, up, down = pl.pallas_call(
        settle_kernel,
        out_shape=[jax.ShapeDtypeStruct(*s) for s in shapes],
        in_specs=[vmem] * 7,
        out_specs=[vmem] * 9,
        compiler_params=pltpu.CompilerParams(vmem_limit_bytes=63 * 2**20),
    )(small, output, grad_input, *sums)
    return (output[None], grad_input[None], attn_total, qkv, out, ffn_total, up, down, bias_total)


def solution(mesh):
    fits = dict(mesh.shape) == {"row": CHIPS, "blk": 2}
    return jax.shard_map(
        slice_body if fits else body,
        mesh=mesh,
        in_specs=(
            P("row", "blk", None),
            P("row", None),
            P(),
            P(("row", "blk")),
            P(("row", "blk"), None),
            P(("row", "blk"), None),
            P(("row", "blk")),
            P(("row", "blk"), None),
            P(("row", "blk"), None),
            P(),
            P("row", "blk", None),
        ),
        out_specs=(
            P("row", "blk", None),
            P("row", "blk", None),
            P(("row", "blk")),
            P(("row", "blk"), None),
            P(("row", "blk"), None),
            P(("row", "blk")),
            P(("row", "blk"), None),
            P(("row", "blk"), None),
            P(),
        ),
        check_vma=False,
    )
```
